32 devices in a mesh: dp: 16 (over z, y, x), tensor: 2 (over core).
Axes of the slice: x: 2, y: 2, z: 4, core: 2. Of those that a mesh axis runs over, the one named last changes fastest.
Arguments:
- tokens: bfloat16 [9216, 768], P('dp'), may hold values from -6 to 6
- region_ids: int32 [576], replicated, may hold values from 0 to 2
- rel_index: int32 [144, 144], replicated, may hold values from 0 to 528
- valid: int32 [16], P('dp'), may hold values 0 or 1
- ln1_gain: bfloat16 [2, 768], replicated, may hold values from 0.5 to 1.5
- ln1_bias: bfloat16 [2, 768], replicated, may hold values from -4 to 4
- qkv_weight: bfloat16 [2, 3, 768, 768], P(None, None, None, 'tensor'), may hold values from -0.21875 to 0.21875
- qv_bias: bfloat16 [2, 2, 768], P(None, None, 'tensor'), may hold values from -4 to 4
- rel_table: bfloat16 [2, 529, 24], P(None, None, 'tensor'), may hold values from -4 to 4
- proj_weight: bfloat16 [2, 768, 768], P(None, 'tensor'), may hold values from -0.875 to 0.875
- proj_bias: bfloat16 [2, 768], replicated, may hold values from -4 to 4
- ln2_gain: bfloat16 [2, 768], replicated, may hold values from 0.5 to 1.5
- ln2_bias: bfloat16 [2, 768], replicated, may hold values from -4 to 4
- fc1_weight: bfloat16 [2, 768, 3072], P(None, None, 'tensor'), may hold values from -0.21875 to 0.21875
- fc1_bias: bfloat16 [2, 3072], P(None, 'tensor'), may hold values from -4 to 4
- fc2_weight: bfloat16 [2, 3072, 768], P(None, 'tensor'), may hold values from -0.109375 to 0.109375
- fc2_bias: bfloat16 [2, 768], replicated, may hold values from -4 to 4
- cotangent: bfloat16 [9216, 768], P('dp'), may hold values from -6 to 6
Outputs:
- output: float32 [9216, 768], P('dp')
- input_grad: float32 [9216, 768], P('dp')
- ln1_gain_grad: float32 [2, 768], replicated
- ln1_bias_grad: float32 [2, 768], replicated
- qkv_weight_grad: float32 [2, 3, 768, 768], P(None, None, 'dp', 'tensor')
- qv_bias_grad: float32 [2, 2, 768], P(None, None, 'tensor')
- rel_table_grad: float32 [2, 529, 24], P(None, None, 'tensor')
- proj_weight_grad: float32 [2, 768, 768], P(None, 'tensor', 'dp')
- proj_bias_grad: float32 [2, 768], replicated
- ln2_gain_grad: float32 [2, 768], replicated
- ln2_bias_grad: float32 [2, 768], replicated
- fc1_weight_grad: float32 [2, 768, 3072], P(None, 'dp', 'tensor')
- fc1_bias_grad: float32 [2, 3072], P(None, 'tensor')
- fc2_weight_grad: float32 [2, 3072, 768], P(None, 'tensor', 'dp')
- fc2_bias_grad: float32 [2, 768], replicated
The draws below stay inside these ranges and needn't reach their ends.
Inputs may be any that keep to these rules, and one draw needn't show every extreme that they name: `rel_index`: a row of rel_table for each pair of positions in a window.
All inputs are finite; a program needn't handle non-finite values. No bound on the sum of `valid` on one device may be relied on, other than what follows from the above.
Results may differ from the reference program's by a relative error of at most 0.025.
Values may be sent and summed in bfloat16 or wider, within the bound.
A program may use at most 192 MiB of HBM per device.

```python
import jax
import jax.numpy as jnp
from jax import lax

D = 768
HEADS = 24
HD = 32
FF = 3072
WIN = 12
SIDE = 24
LAYERS = 2
SHIFT = 6
TABLE = 529
IMAGES = 16
TOKENS = 9216
N_TENSOR = 2


def touch_ends(values, own_key, low, top_value):
    longest = values.shape.index(max(values.shape))
    spots = []
    for shift in (0, 1):
        where = [jax.random.randint(jax.random.fold_in(own_key, axis), (), 0, length) for axis, length in enumerate(values.shape)]
        where[longest] = (where[longest] + shift) % values.shape[longest]
        spots.append(tuple(where))
    return values.at[spots[0]].set(low).at[spots[1]].set(top_value)


def with_spikes(array, stream_key, source, target, shards_of, factor):
    def block_of(position):
        return (jnp.arange(array.shape[position]) // (array.shape[position] // shards_of)).reshape((-1,) + (1,) * (array.ndim - 1 - position))

    near = jax.random.permutation(stream_key, shards_of)[block_of(target)]
    second = (block_of(target) + shards_of // 2) % shards_of
    return jnp.where((block_of(source) == near) | (block_of(source) == second), factor * array, array)


def levels(stream_key, shape, shards, least, top_value):
    level, own = 1.0, jax.random.fold_in(stream_key, 6)
    for axis_at, blocks in shards:
        draws = jnp.exp(jax.random.uniform(jax.random.fold_in(own, axis_at), (blocks,), jnp.float32, least / len(shards), top_value / len(shards)))
        level = level * jnp.repeat(draws, shape[axis_at] // blocks).reshape([-1 if axis == axis_at else 1 for axis in range(len(shape))])
    return level


def normal_values(rng, shape, deviation, reach, pieces=(), dtype=jnp.bfloat16):
    values = deviation * jax.random.normal(rng, shape, jnp.float32)
    if pieces:
        values = values * levels(rng, shape, pieces, -0.22, 0.18)
    return jnp.clip(values, -reach, reach).astype(dtype)


def gaussian_with(own_key, extent, scale, reach, cuts, heavy, dtype=jnp.bfloat16):
    entries = scale * jax.random.normal(own_key, extent, jnp.float32)
    if cuts:
        entries = entries * levels(own_key, extent, cuts, -0.22, 0.18)
    return jnp.clip(with_spikes(entries, jax.random.fold_in(own_key, 3), *heavy), -reach, reach).astype(dtype)


def setup_inputs(seed: int = 0) -> dict:
    splits = jax.random.split(jax.random.key(seed), 19)
    return {
        "tokens": normal_values(splits[0], (TOKENS, D), 1.0, 6.0, ((0, 16),)),
        "region_ids": touch_ends(jax.random.randint(splits[1], (SIDE * SIDE,), 0, 3), jax.random.fold_in(splits[1], 1), 0, 2).astype(jnp.int32),
        "rel_index": touch_ends(jax.random.randint(splits[2], (WIN * WIN, WIN * WIN), 0, TABLE), jax.random.fold_in(splits[2], 1), 0, TABLE - 1).astype(jnp.int32),
        "valid": touch_ends((jax.random.randint(splits[3], (IMAGES,), 0, 4) < 3).astype(jnp.int32), jax.random.fold_in(splits[3], 1), 0, 1),
        "ln1_gain": jnp.clip(1.0 + 0.1 * jax.random.normal(splits[4], (LAYERS, D), jnp.float32), 0.5, 1.5).astype(jnp.bfloat16),
        "ln1_bias": normal_values(splits[5], (LAYERS, D), 0.3, 4.0),
        "qkv_weight": normal_values(splits[6], (LAYERS, 3, D, D), D ** -0.5, 0.21875, ((3, 2),)),
        "qv_bias": normal_values(splits[7], (LAYERS, 2, D), 0.3, 4.0, ((2, 2),)),
        "rel_table": normal_values(splits[8], (LAYERS, TABLE, HEADS), 1.0, 4.0, ((2, 2),)),
        "proj_weight": normal_values(splits[9], (LAYERS, D, D), (D // 16) ** -0.5, 0.875, ((1, 2),)),
        "proj_bias": normal_values(splits[10], (LAYERS, D), 0.3, 4.0),
        "ln2_gain": jnp.clip(1.0 + 0.1 * jax.random.normal(splits[11], (LAYERS, D), jnp.float32), 0.5, 1.5).astype(jnp.bfloat16),
        "ln2_bias": normal_values(splits[12], (LAYERS, D), 0.3, 4.0),
        "fc1_weight": normal_values(splits[13], (LAYERS, D, FF), D ** -0.5, 0.21875, ((2, 2),)),
        "fc1_bias": normal_values(splits[14], (LAYERS, FF), 0.3, 4.0, ((1, 2),)),
        "fc2_weight": normal_values(splits[15], (LAYERS, FF, D), FF ** -0.5, 0.109375, ((1, 2),)),
        "fc2_bias": normal_values(splits[16], (LAYERS, D), 0.3, 4.0),
        "cotangent": gaussian_with(splits[17], (TOKENS, D), 1.0, 6.0, ((0, 16),), (0, 1, 16, 2.0)),
    }


EPSILON = 1e-05
HIGHEST = lax.Precision.HIGHEST

@jax.custom_vjp
def low(v):
    return lax.optimization_barrier(v.astype(jnp.bfloat16)).astype(jnp.float32)

@jax.custom_vjp
def low_back(v):
    return v

def low_keep(v):
    return (low(v), None)

def low_pass(kept, grad):
    return (grad,)

def back_keep(v):
    return (v, None)

def back_low(kept, grad):
    return (low(grad),)
low.defvjp(low_keep, low_pass)
low_back.defvjp(back_keep, back_low)

def layer_norm(carried, gain, offset):
    center = carried - lax.optimization_barrier(jnp.mean(carried, axis=-1, keepdims=True))
    spread = lax.optimization_barrier(jnp.mean(center * center, axis=-1, keepdims=True))
    return center * lax.rsqrt(spread + EPSILON) * gain + offset

def to_windows(grid):
    count = SIDE // WIN
    blocks = grid.reshape(count, WIN, count, WIN, grid.shape[-1]).transpose(0, 2, 1, 3, 4)
    return blocks.reshape(count * count, WIN * WIN, grid.shape[-1])

def from_windows(blocks):
    count = SIDE // WIN
    grid = blocks.reshape(count, count, WIN, WIN, blocks.shape[-1]).transpose(0, 2, 1, 3, 4)
    return grid.reshape(SIDE, SIDE, blocks.shape[-1])

def window_attention(queries, key_rows, value_rows, head_bias, region_ids, shifted):
    width = queries.shape[-1]
    heads_here = width // HD

    def arrange(rows):
        grid = rows.reshape(SIDE, SIDE, width)
        if shifted:
            grid = jnp.roll(grid, (-SHIFT, -SHIFT), axis=(0, 1))
        return to_windows(grid).reshape(-1, WIN * WIN, heads_here, HD)
    query_win = arrange(queries)
    key_win = arrange(key_rows)
    value_win = arrange(value_rows)
    scores = jnp.einsum('bihd,bjhd->bhij', query_win, key_win, precision=HIGHEST) * HD ** (-0.5)
    scores = low_back(scores) + head_bias[None]
    if shifted:
        region_win = to_windows(region_ids.reshape(SIDE, SIDE, 1))[:, :, 0]
        same_region = region_win[:, :, None] == region_win[:, None, :]
        scores = jnp.where(same_region[:, None], scores, -1000000000.0)
    attn_prob = jax.nn.softmax(scores, axis=-1)
    mixed = jnp.einsum('bhij,bjhd->bihd', low(attn_prob), value_win, precision=HIGHEST)
    grid = from_windows(mixed.reshape(-1, WIN * WIN, width))
    if shifted:
        grid = jnp.roll(grid, (SHIFT, SHIFT), axis=(0, 1))
    return grid.reshape(SIDE * SIDE, width)

def layer(carried, params, region_ids, rel_index, shifted):
    gain_one, offset_one, qkv_w, qv_b, table, proj_w, proj_b, gain_two, offset_two, up_w, up_b, down_w, down_b = params
    head_width = D // N_TENSOR
    hidden_width = FF // N_TENSOR
    head_count = HEADS // N_TENSOR
    all_bias = jnp.transpose(table[rel_index], (2, 0, 1))
    normed = low(layer_norm(carried, gain_one, offset_one))
    attn_out = jnp.zeros_like(carried)
    for group in range(N_TENSOR):
        start_col = group * head_width
        stop_col = start_col + head_width
        inputs = low_back(normed)
        projected = low_back(jnp.einsum('rd,kde->kre', inputs, qkv_w[:, :, start_col:stop_col], precision=HIGHEST))
        queries = low(projected[0] + qv_b[0, start_col:stop_col])
        key_rows = low(projected[1])
        value_rows = low(projected[2] + qv_b[1, start_col:stop_col])
        head_bias = all_bias[group * head_count:(group + 1) * head_count]
        mixed = window_attention(queries, key_rows, value_rows, head_bias, region_ids, shifted)
        mixed = low(low_back(mixed))
        attn_out = attn_out + low(jnp.dot(mixed, proj_w[start_col:stop_col], precision=HIGHEST))
    middle = carried + low_back(attn_out) + proj_b
    normed_two = low(layer_norm(middle, gain_two, offset_two))
    mlp_out = jnp.zeros_like(carried)
    for group in range(N_TENSOR):
        start_col = group * hidden_width
        stop_col = start_col + hidden_width
        inputs = low_back(normed_two)
        hidden_pre = low_back(jnp.dot(inputs, up_w[:, start_col:stop_col], precision=HIGHEST)) + up_b[start_col:stop_col]
        hidden = low(jax.nn.gelu(hidden_pre, approximate=False))
        mlp_out = mlp_out + low(jnp.dot(hidden, down_w[start_col:stop_col], precision=HIGHEST))
    return middle + low_back(mlp_out) + down_b

def reference(tokens, region_ids, rel_index, valid, ln1_gain, ln1_bias, qkv_weight, qv_bias, rel_table, proj_weight, proj_bias, ln2_gain, ln2_bias, fc1_weight, fc1_bias, fc2_weight, fc2_bias, cotangent):
    weights = tuple((entry.astype(jnp.float32) for entry in (ln1_gain, ln1_bias, qkv_weight, qv_bias, rel_table, proj_weight, proj_bias, ln2_gain, ln2_bias, fc1_weight, fc1_bias, fc2_weight, fc2_bias)))

    def image_forward(image_rows, every):
        carried = image_rows
        for layer_id in range(LAYERS):
            params = tuple((entry[layer_id] for entry in every))
            carried = layer(carried, params, region_ids, rel_index, layer_id % 2 == 1)
        return carried

    def advance(totals, item):
        image_rows, image_cot, keep_flag = item
        result, pull = jax.vjp(image_forward, image_rows, weights)
        grad_rows, grad_weights = pull(image_cot * keep_flag)
        totals = tuple((total + piece for total, piece in zip(totals, grad_weights)))
        return (totals, (result, grad_rows))
    rows_in = tokens.astype(jnp.float32).reshape(IMAGES, SIDE * SIDE, D)
    cot_in = cotangent.astype(jnp.float32).reshape(IMAGES, SIDE * SIDE, D)
    keep_in = valid.astype(jnp.float32)[:, None, None]
    zeros = tuple((jnp.zeros_like(entry) for entry in weights))
    grads, (results, grad_in) = lax.scan(advance, zeros, (rows_in, cot_in, keep_in))
    return (results.reshape(TOKENS, D), grad_in.reshape(TOKENS, D), grads[0], grads[1], grads[2], grads[3], grads[4], grads[5], grads[6], grads[7], grads[8], grads[9], grads[10], grads[11], grads[12])
```

```python
import functools

import jax
import jax.numpy as jnp
from jax import lax
from jax.experimental import pallas as pl
from jax.experimental.pallas import tpu as pltpu
from jax.sharding import PartitionSpec as P

HD = 32
WIN = 12
SIDE = 24
LAYERS = 2
SHIFT = 6
ROWS = SIDE * SIDE
CELL = WIN * WIN
WINDOWS = ROWS // CELL
PER_TILE = 4
LANES = PER_TILE * HD
EPSILON = 1e-05
LOG2E = 1.4426950408889634
SCALE = HD**-0.5
VMEM_LIMIT = 62 * 1024 * 1024
MESH_ID = pl.DeviceIdType.MESH

f32 = jnp.float32
bf16 = jnp.bfloat16


def nn(a, b):
    return jnp.dot(a, b, preferred_element_type=f32)


def nt(a, b):
    return lax.dot_general(a, b, (((1,), (1,)), ((), ())), preferred_element_type=f32)


def tn(a, b):
    return lax.dot_general(a, b, (((0,), (0,)), ((), ())), preferred_element_type=f32)


def window_row(i, j, shifted):
    if shifted:
        i, j = (i - SHIFT) % SIDE, (j - SHIFT) % SIDE
    return ((i // WIN) * (SIDE // WIN) + j // WIN) * CELL + (i % WIN) * WIN + j % WIN


def pieces(source, target):
    found = []
    for i in range(SIDE):
        for j in range(0, SIDE, SHIFT):
            row = [i * SIDE + j if o is None else window_row(i, j, o) for o in (source, target)]
            found.append(tuple(row))
    return found


def move_rows(source_ref, target_ref, source, target):
    for here, there in pieces(source, target):
        target_ref[there : there + SHIFT, :] = source_ref[here : here + SHIFT, :]


def lane_head(values, head):
    lane = lax.broadcasted_iota(jnp.int32, values.shape, 1)
    return jnp.where((lane >= HD * head) & (lane < HD * (head + 1)), values, jnp.zeros_like(values))


def row_norm(values):
    center = values - jnp.mean(values, axis=-1, keepdims=True)
    scale = lax.rsqrt(jnp.mean(center * center, axis=-1, keepdims=True) + EPSILON)
    return center * scale, scale


def wide(ref, layer):
    return ref[layer : layer + 1, :].astype(f32)


def bias_kernel(table_ref, index_ref, region_ref, bias_ref, mask_ref, index_t_ref, rows_ref):
    heads = table_ref.shape[2]
    rows = table_ref.shape[1]
    rows_ref[...] = jnp.zeros_like(rows_ref)
    for layer in range(LAYERS):
        rows_ref[layer, :heads, :rows] = table_ref[layer].astype(f32).T * LOG2E
    index_t = index_ref[...].astype(f32).T.astype(jnp.int32)
    index_t_ref[...] = index_t
    for first in (0, CELL - 128):
        part = index_t[:, first : first + 128]
        low = part & 127
        high = part >> 7
        for layer in range(LAYERS):
            for head in range(heads):
                found = jnp.zeros((CELL, 128), f32)
                for chunk in range(rows_ref.shape[2] // 128):
                    row = rows_ref[layer, head : head + 1, chunk * 128 : (chunk + 1) * 128]
                    took = jnp.take_along_axis(
                        jnp.broadcast_to(row, (CELL, 128)), low, axis=1, mode="promise_in_bounds"
                    )
                    found = jnp.where(high == chunk, took, found)
                bias_ref[layer * heads + head, :, first : first + 128] = found
    for window in range(WINDOWS):
        row = jnp.broadcast_to(region_ref[window : window + 1, :].astype(f32), (CELL, CELL))
        mask_ref[window] = (row == row.T).astype(f32)


def make_bias(table, index, region):
    heads = table.shape[2]
    rows = -(-table.shape[1] // 128) * 128
    return pl.pallas_call(
        bias_kernel,
        out_shape=(
            jax.ShapeDtypeStruct((LAYERS * heads, CELL, CELL), f32),
            jax.ShapeDtypeStruct((WINDOWS, CELL, CELL), f32),
            jax.ShapeDtypeStruct((CELL, CELL), jnp.int32),
        ),
        in_specs=[pl.BlockSpec(memory_space=pltpu.VMEM)] * 3,
        out_specs=(pl.BlockSpec(memory_space=pltpu.VMEM),) * 3,
        scratch_shapes=[pltpu.VMEM((LAYERS, 16, rows), f32)],
        compiler_params=pltpu.CompilerParams(vmem_limit_bytes=VMEM_LIMIT),
        name="bias",
    )(table, index, region)


def forward_attention(q, k, v, bias, mask, store):
    stacked = jnp.concatenate([lane_head(k, head) for head in range(PER_TILE)], axis=0)
    scores = nt(stacked, q)
    v_t = v.T
    mixed = []
    for head in range(PER_TILE):
        s = scores[head * CELL : (head + 1) * CELL] * (SCALE * LOG2E) + bias(head)
        if mask is not None:
            s = jnp.where(mask > 0.5, s, -1000000000.0 * LOG2E)
        e = jnp.exp2(s - jnp.max(s, axis=0, keepdims=True))
        prob = (e * (1.0 / jnp.sum(e, axis=0, keepdims=True))).astype(bf16)
        store(head, prob)
        mixed.append(nn(v_t[head * HD : (head + 1) * HD], prob))
    return jnp.concatenate(mixed, axis=0).T


SAVED = ("h1", "n1", "r1", "qkv", "prob", "mix", "h2", "n2", "r2", "hid", "slope")


def saved_shapes(width, heads_width, hidden):
    heads = heads_width // HD
    return {
        "h1": ((ROWS, width), bf16),
        "n1": ((ROWS, width), bf16),
        "r1": ((ROWS, 1), f32),
        "qkv": ((3, ROWS, heads_width), bf16),
        "prob": ((WINDOWS, heads, CELL, CELL), bf16),
        "mix": ((ROWS, heads_width), bf16),
        "h2": ((ROWS, width), bf16),
        "n2": ((ROWS, width), bf16),
        "r2": ((ROWS, 1), f32),
        "hid": ((ROWS, hidden), bf16),
        "slope": ((ROWS, hidden), bf16),
    }


def forward_kernel(*refs):
    it = iter(refs)
    tokens, gain1, off1, qv_b, proj_b, gain2, off2, up_b, down_b, bias, mask = (next(it) for _ in range(11))
    weights_hbm = [next(it) for _ in range(4)]
    out = next(it)
    kept_hbm = {name: next(it) for name in SAVED}
    weights = [next(it) for _ in range(4)]
    kept = {name: next(it) for name in SAVED}
    x, y, send, recv = (next(it) for _ in range(4))
    weight_sem, kept_sem, send_sem, recv_sem = (next(it) for _ in range(4))
    qkv_w, proj_w, up_w, down_w = weights
    heads_width = proj_w.shape[1]
    heads = heads_width // HD
    other = 1 - lax.axis_index("tensor")

    def load(slot, layer):
        return pltpu.make_async_copy(
            weights_hbm[slot].at[layer], weights[slot].at[layer], weight_sem.at[slot, layer]
        )

    def keep(name, layer):
        return pltpu.make_async_copy(
            kept[name].at[layer], kept_hbm[name].at[layer], kept_sem.at[SAVED.index(name), layer]
        )

    def swap(turn, window):
        return pltpu.make_async_remote_copy(
            src_ref=send.at[turn, window],
            dst_ref=recv.at[turn, window],
            send_sem=send_sem.at[turn, window],
            recv_sem=recv_sem.at[turn, window],
            device_id={"tensor": other},
            device_id_type=MESH_ID,
        )

    for layer in range(LAYERS):
        for slot in range(4):
            load(slot, layer).start()
    barrier = pltpu.get_barrier_semaphore()
    pl.semaphore_signal(barrier, inc=1, device_id={"tensor": other}, device_id_type=MESH_ID)

    y[...] = tokens[...].astype(f32)
    move_rows(y, x, None, False)

    for layer in range(LAYERS):
        load(0, layer).wait()
        load(1, layer).wait()
        if layer == 0:
            pl.semaphore_wait(barrier, 1)

        def attend(window, carry, layer=layer):
            at = pl.ds(pl.multiple_of(window * CELL, CELL), CELL)
            normed, scale = row_norm(x[at, :])
            h1 = (normed * wide(gain1, layer) + wide(off1, layer)).astype(bf16)
            kept["n1"][layer, at, :] = normed.astype(bf16)
            kept["r1"][layer, at, :] = scale
            kept["h1"][layer, at, :] = h1
            kept["qkv"][layer, 0, at, :] = (
                nn(h1, qkv_w[layer, 0]) + qv_b[layer, 0:1, :].astype(f32)
            ).astype(bf16)
            kept["qkv"][layer, 1, at, :] = nn(h1, qkv_w[layer, 1]).astype(bf16)
            kept["qkv"][layer, 2, at, :] = (
                nn(h1, qkv_w[layer, 2]) + qv_b[layer, 1:2, :].astype(f32)
            ).astype(bf16)
            same = mask[window] if layer == 1 else None
            for tile in range(heads_width // LANES):
                cols = slice(tile * LANES, (tile + 1) * LANES)

                def store(head, prob, tile=tile):
                    kept["prob"][layer, window, tile * PER_TILE + head] = prob

                kept["mix"][layer, at, cols] = forward_attention(
                    kept["qkv"][layer, 0, at, cols],
                    kept["qkv"][layer, 1, at, cols],
                    kept["qkv"][layer, 2, at, cols],
                    lambda head, tile=tile: bias[layer * heads + tile * PER_TILE + head],
                    same,
                    store,
                ).astype(bf16)
            send[2 * layer, window] = nn(kept["mix"][layer, at, :], proj_w[layer]).astype(bf16)
            swap(2 * layer, window).start()
            return carry

        lax.fori_loop(0, WINDOWS, attend, 0)
        for name in ("h1", "n1", "r1", "qkv", "prob", "mix"):
            keep(name, layer).start()
        load(2, layer).wait()
        load(3, layer).wait()

        def expand(window, carry, layer=layer):
            at = pl.ds(pl.multiple_of(window * CELL, CELL), CELL)
            swap(2 * layer, window).wait_recv()
            total = send[2 * layer, window].astype(f32) + recv[2 * layer, window].astype(f32)
            middle = x[at, :] + total + wide(proj_b, layer)
            x[at, :] = middle
            normed, scale = row_norm(middle)
            h2 = (normed * wide(gain2, layer) + wide(off2, layer)).astype(bf16)
            kept["n2"][layer, at, :] = normed.astype(bf16)
            kept["r2"][layer, at, :] = scale
            kept["h2"][layer, at, :] = h2
            u = nn(h2, up_w[layer]) + wide(up_b, layer)
            phi = 0.5 + 0.5 * lax.erf(u * 0.7071067811865476)
            hidden = (u * phi).astype(bf16)
            kept["slope"][layer, at, :] = (
                phi + u * jnp.exp(u * u * -0.5) * 0.3989422804014327
            ).astype(bf16)
            kept["hid"][layer, at, :] = hidden
            send[2 * layer + 1, window] = nn(hidden, down_w[layer]).astype(bf16)
            swap(2 * layer + 1, window).start()
            return carry

        lax.fori_loop(0, WINDOWS, expand, 0)
        for name in ("h2", "n2", "r2", "hid", "slope"):
            keep(name, layer).start()
        target = y if layer == 0 else out

        def finish(window, carry, layer=layer, target=target):
            at = pl.ds(pl.multiple_of(window * CELL, CELL), CELL)
            swap(2 * layer + 1, window).wait_recv()
            total = send[2 * layer + 1, window].astype(f32) + recv[2 * layer + 1, window].astype(f32)
            target[at, :] = x[at, :] + total + wide(down_b, layer)
            return carry

        lax.fori_loop(0, WINDOWS, finish, 0)
        if layer == 0:
            move_rows(y, x, False, True)

    for turn in range(2 * LAYERS):
        for window in range(WINDOWS):
            swap(turn, window).wait_send()
    for layer in range(LAYERS):
        for name in SAVED:
            keep(name, layer).wait()


def run_forward(tokens, vectors, bias, mask, weights):
    width = tokens.shape[1]
    heads_width = weights[1].shape[1]
    hidden = weights[2].shape[2]
    shapes = saved_shapes(width, heads_width, hidden)
    vmem = pl.BlockSpec(memory_space=pltpu.VMEM)
    hbm = pl.BlockSpec(memory_space=pl.ANY)
    kept = [jax.ShapeDtypeStruct((LAYERS,) + shapes[name][0], shapes[name][1]) for name in SAVED]
    swaps = (2 * LAYERS, WINDOWS)
    outs = pl.pallas_call(
        forward_kernel,
        out_shape=[jax.ShapeDtypeStruct((ROWS, width), f32)] + kept,
        in_specs=[vmem] * 11 + [hbm] * 4,
        out_specs=[vmem] + [hbm] * len(SAVED),
        scratch_shapes=[pltpu.VMEM(w.shape, bf16) for w in weights]
        + [pltpu.VMEM(s.shape, s.dtype) for s in kept]
        + [
            pltpu.VMEM((ROWS, width), f32),
            pltpu.VMEM((ROWS, width), f32),
            pltpu.VMEM(swaps + (CELL, width), bf16),
            pltpu.VMEM(swaps + (CELL, width), bf16),
            pltpu.SemaphoreType.DMA((4, LAYERS)),
            pltpu.SemaphoreType.DMA((len(SAVED), LAYERS)),
            pltpu.SemaphoreType.DMA(swaps),
            pltpu.SemaphoreType.DMA(swaps),
        ],
        compiler_params=pltpu.CompilerParams(
            collective_id=0, has_side_effects=True, vmem_limit_bytes=VMEM_LIMIT
        ),
        name="forward",
    )(tokens, *vectors, bias, mask, *weights)
    return outs[0], dict(zip(SAVED, outs[1:]))


BITS = 4
X_FIRST = (3, 2, 1, 0)
Y_FIRST = (2, 3, 1, 0)
Z_FIRST = (1, 0, 3, 2)
ORDERS = (X_FIRST, Y_FIRST, Z_FIRST, X_FIRST, Y_FIRST, Y_FIRST, X_FIRST, Y_FIRST)
VECTOR_ROWS = 24
REL_ROW = 9


def chunk_widths(heads_width, hidden):
    return (hidden // 2,) * 4 + (heads_width,) * 4


def norm_back(grad, normed, scale, gain):
    c = grad * gain
    inner = c - jnp.mean(c, axis=-1, keepdims=True)
    return scale * (inner - normed * jnp.mean(c * normed, axis=-1, keepdims=True))


def column_sum(values):
    return jnp.sum(values, axis=0, keepdims=True)


def backward_attention(q, k, v, grad, prob, add_score):
    stacked = jnp.concatenate([lane_head(v, head) for head in range(PER_TILE)], axis=0)
    grad_prob = nt(stacked, grad)
    k_t = k.T
    grad_q, grad_k, grad_v = [], None, None
    for head in range(PER_TILE):
        p = prob(head)
        weighted = p.astype(f32) * grad_prob[head * CELL : (head + 1) * CELL]
        score = weighted - p.astype(f32) * column_sum(weighted)
        add_score(head, score)
        low = score.astype(bf16)
        part_v = nn(p, lane_head(grad, head))
        part_k = nn(low, lane_head(q, head))
        grad_v = part_v if grad_v is None else grad_v + part_v
        grad_k = part_k if grad_k is None else grad_k + part_k
        grad_q.append(nn(k_t[head * HD : (head + 1) * HD], low))
    return jnp.concatenate(grad_q, axis=0).T * SCALE, grad_k * SCALE, grad_v


def backward_kernel(shift, *refs):
    it = iter(refs)

    def take(count):
        return [next(it) for _ in range(count)]

    cot, valid, gain1, gain2, index_t = take(5)
    weights_hbm = take(4)
    kept_hbm = dict(zip(SAVED, take(len(SAVED))))
    out, reduced, vectors_out = take(3)
    weights = take(4)
    kept = dict(zip(SAVED, take(len(SAVED))))
    chunks = len(ORDERS)
    grads = [take(chunks) for _ in range(LAYERS)]
    landed = [take(BITS) for _ in range(chunks)]
    dy, low, pre, send, recv, grad_mix, grad_qkv, grad_bias, table, vectors, vectors_in = take(11)
    weight_sem, kept_sem, send_sem, recv_sem = take(4)
    chunk_send, chunk_recv, credit, vector_send, vector_recv = take(5)
    qkv_w, proj_w, up_w, down_w = weights
    heads_width = proj_w.shape[0]
    hidden = up_w.shape[1]
    width = dy.shape[1]
    heads = heads_width // HD
    part = width >> BITS
    widths = chunk_widths(heads_width, hidden)

    me = lax.axis_index("dp")
    other = 1 - lax.axis_index("tensor")
    places = [1 << (shift + BITS - 1 - dim) for dim in range(BITS)]
    mine = [lax.rem(lax.div(me, place), 2) for place in places]
    partner = [me + place - 2 * place * bit for place, bit in zip(places, mine)]

    def load(slot, layer):
        return pltpu.make_async_copy(weights_hbm[slot].at[layer], weights[slot], weight_sem.at[slot])

    def fetch(name, layer):
        return pltpu.make_async_copy(
            kept_hbm[name].at[layer], kept[name], kept_sem.at[SAVED.index(name)]
        )

    def swap(turn, window):
        return pltpu.make_async_remote_copy(
            src_ref=send.at[turn % 2, window],
            dst_ref=recv.at[turn % 2, window],
            send_sem=send_sem.at[turn, window],
            recv_sem=recv_sem.at[turn, window],
            device_id={"tensor": other},
            device_id_type=MESH_ID,
        )

    step = {}

    def region(chunk, phase, bit):
        order = ORDERS[chunk]
        index = [slice(None)] * BITS
        for dim in order[:phase]:
            index[dim] = mine[dim]
        index[order[phase]] = bit
        return tuple(index)

    def chunk_copy(layer, chunk, phase):
        dim = ORDERS[chunk][phase]
        return pltpu.make_async_remote_copy(
            src_ref=grads[layer][chunk].at[region(chunk, phase, 1 - mine[dim])],
            dst_ref=landed[chunk][phase],
            send_sem=chunk_send.at[layer, chunk, phase],
            recv_sem=chunk_recv.at[layer, chunk, phase],
            device_id={"dp": partner[dim]},
            device_id_type=MESH_ID,
        )

    def begin(layer, chunk, phase):
        if layer == 0:
            while step.get((LAYERS - 1, chunk), BITS) <= phase:
                advance(LAYERS - 1, chunk)
            pl.semaphore_wait(credit.at[chunk, phase], 1)
        chunk_copy(layer, chunk, phase).start()
        step[layer, chunk] = phase

    def advance(layer, chunk):
        phase = step[layer, chunk]
        dim = ORDERS[chunk][phase]
        chunk_copy(layer, chunk, phase).wait()
        keep = region(chunk, phase, mine[dim])
        free = [d for d in range(BITS) if isinstance(keep[d], slice)]
        ref, arrived = grads[layer][chunk], landed[chunk][phase]
        first = sum(widths[:chunk])
        for number in range(1 << len(free)):
            bits = [(number >> (len(free) - 1 - n)) & 1 for n in range(len(free))]
            index = list(keep)
            for d, bit in zip(free, bits):
                index[d] = bit
            here = ref[tuple(index)]
            there = arrived[tuple(bits)] if bits else arrived[...]
            if phase < BITS - 1:
                ref[tuple(index)] = here + there
            else:
                reduced[layer, :, first : first + widths[chunk]] = here.astype(f32) + there.astype(f32)
        if layer == LAYERS - 1:
            pl.semaphore_signal(
                credit.at[chunk, phase], inc=1, device_id={"dp": partner[dim]}, device_id_type=MESH_ID
            )
        if phase < BITS - 1:
            begin(layer, chunk, phase + 1)
        else:
            del step[layer, chunk]

    def finish_chunk(layer, chunk, left, right):
        half = width // 2
        for top in range(2):
            value = tn(left[:, top * half : (top + 1) * half], right)
            grads[layer][chunk][top] = value.astype(bf16).reshape(2, 2, 2, part, widths[chunk])
        begin(layer, chunk, 0)

    def pump(count):
        for layer, chunk in list(step)[:count]:
            advance(layer, chunk)

    def vector_copy(phase):
        return pltpu.make_async_remote_copy(
            src_ref=vectors.at[phase],
            dst_ref=vectors_in.at[phase],
            send_sem=vector_send.at[phase],
            recv_sem=vector_recv.at[phase],
            device_id={"dp": partner[phase]},
            device_id_type=MESH_ID,
        )

    def vector_step(phase):
        vector_copy(phase).wait()
        total = vectors[phase] + vectors_in[phase]
        if phase < BITS - 1:
            vectors[phase + 1] = total
            vector_copy(phase + 1).start()
        else:
            vectors_out[...] = total

    first_order = ("hid", "slope", "h2", "n2", "r2", "mix", "prob", "qkv", "h1", "n1", "r1")
    top = LAYERS - 1
    fetch("hid", top).start()
    load(3, top).start()
    fetch("slope", top).start()
    load(2, top).start()
    for name in first_order[2:6]:
        fetch(name, top).start()
    load(1, top).start()
    for name in first_order[6:]:
        fetch(name, top).start()
    load(0, top).start()
    barrier = pltpu.get_barrier_semaphore()
    pl.semaphore_signal(barrier, inc=1, device_id={"tensor": other}, device_id_type=MESH_ID)
    for dim in range(BITS):
        pl.semaphore_signal(barrier, inc=1, device_id={"dp": partner[dim]}, device_id_type=MESH_ID)

    out[...] = cot[...].astype(f32) * valid[0].astype(f32)
    move_rows(out, dy, None, True)
    vectors[0] = jnp.zeros(vectors.shape[1:], f32)
    grad_bias[...] = jnp.zeros_like(grad_bias)
    pl.semaphore_wait(barrier, 1 + BITS)

    def rows_of(window):
        return pl.ds(pl.multiple_of(window * CELL, CELL), CELL)

    for layer in reversed(range(LAYERS)):
        turn = 2 * (LAYERS - 1 - layer)

        def add_row(row, value, first=0, layer=layer):
            cols = slice(first, first + value.shape[1])
            vectors[0, layer, row : row + 1, cols] += value

        def free(name, layer=layer):
            if layer > 0:
                fetch(name, layer - 1).start()

        def free_weight(slot, layer=layer):
            if layer > 0:
                load(slot, layer - 1).start()

        add_row(5, column_sum(dy[...]))
        low[...] = dy[...].astype(bf16)
        fetch("hid", layer).wait()
        finish_chunk(layer, 0, low[...], kept["hid"][:, : hidden // 2])
        finish_chunk(layer, 1, low[...], kept["hid"][:, hidden // 2 :])
        free("hid")
        fetch("slope", layer).wait()
        load(3, layer).wait()
        load(2, layer).wait()

        def mlp(window, carry, turn=turn, add_row=add_row):
            at = rows_of(window)
            grad = nt(low[at, :], down_w[...]) * kept["slope"][at, :].astype(f32)
            add_row(7, column_sum(grad[:, :width]))
            add_row(8, column_sum(grad[:, width:]))
            pre[at, :] = grad.astype(bf16)
            send[turn % 2, window] = nt(pre[at, :], up_w[...]).astype(bf16)
            swap(turn, window).start()
            return carry

        lax.fori_loop(0, WINDOWS, mlp, 0)
        free("slope")
        free_weight(3)
        free_weight(2)
        pump(2 if layer == 0 else 0)
        fetch("h2", layer).wait()
        finish_chunk(layer, 2, kept["h2"][...], pre[:, : hidden // 2])
        finish_chunk(layer, 3, kept["h2"][...], pre[:, hidden // 2 :])
        free("h2")
        for name in ("n2", "r2", "mix"):
            fetch(name, layer).wait()
        load(1, layer).wait()

        def norm_two(window, carry, turn=turn, layer=layer, add_row=add_row):
            at = rows_of(window)
            swap(turn, window).wait_recv()
            grad = send[turn % 2, window].astype(f32) + recv[turn % 2, window].astype(f32)
            normed = kept["n2"][at, :].astype(f32)
            add_row(3, column_sum(grad * normed))
            add_row(4, column_sum(grad))
            total = dy[at, :] + norm_back(grad, normed, kept["r2"][at, :], wide(gain2, layer))
            dy[at, :] = total
            add_row(2, column_sum(total))
            low[at, :] = total.astype(bf16)
            grad_mix[at, :] = nt(low[at, :], proj_w[...]).astype(bf16)
            return carry

        lax.fori_loop(0, WINDOWS, norm_two, 0)
        free("n2")
        free("r2")
        free_weight(1)
        finish_chunk(layer, 4, low[...], kept["mix"][...])
        free("mix")
        pump(2)

        fetch("prob", layer).wait()
        fetch("qkv", layer).wait()

        def attend(window, carry, layer=layer, add_row=add_row):
            at = rows_of(window)
            for tile in range(heads_width // LANES):
                cols = slice(tile * LANES, (tile + 1) * LANES)

                def add_score(head, score, tile=tile):
                    grad_bias[layer * heads + tile * PER_TILE + head] += score

                parts = backward_attention(
                    kept["qkv"][0, at, cols],
                    kept["qkv"][1, at, cols],
                    kept["qkv"][2, at, cols],
                    grad_mix[at, cols],
                    lambda head, tile=tile: kept["prob"][window, tile * PER_TILE + head],
                    add_score,
                )
                for slot, value in enumerate(parts):
                    grad_qkv[slot, at, cols] = value.astype(bf16)
                add_row(6, column_sum(parts[0]), tile * LANES)
                add_row(6, column_sum(parts[2]), heads_width + tile * LANES)
            return carry

        lax.fori_loop(0, WINDOWS, attend, 0)
        free("prob")
        free("qkv")
        pump(2)
        load(0, layer).wait()

        def project(window, carry, turn=turn):
            at = rows_of(window)
            total = nt(grad_qkv[0, at, :], qkv_w[0])
            total = total + nt(grad_qkv[1, at, :], qkv_w[1])
            total = total + nt(grad_qkv[2, at, :], qkv_w[2])
            send[(turn + 1) % 2, window] = total.astype(bf16)
            swap(turn + 1, window).start()
            return carry

        lax.fori_loop(0, WINDOWS, project, 0)
        free_weight(0)
        fetch("h1", layer).wait()
        finish_chunk(layer, 5, kept["h1"][...], grad_qkv[2])
        finish_chunk(layer, 6, kept["h1"][...], grad_qkv[0])
        finish_chunk(layer, 7, kept["h1"][...], grad_qkv[1])
        free("h1")
        fetch("n1", layer).wait()
        fetch("r1", layer).wait()
        target = out

        def norm_one(window, carry, turn=turn, layer=layer, add_row=add_row):
            at = rows_of(window)
            swap(turn + 1, window).wait_recv()
            grad = send[(turn + 1) % 2, window].astype(f32) + recv[(turn + 1) % 2, window].astype(f32)
            normed = kept["n1"][at, :].astype(f32)
            add_row(0, column_sum(grad * normed))
            add_row(1, column_sum(grad))
            out[at, :] = dy[at, :] + norm_back(grad, normed, kept["r1"][at, :], wide(gain1, layer))
            return carry

        lax.fori_loop(0, WINDOWS, norm_one, 0)
        free("n1")
        free("r1")
        for window in range(WINDOWS):
            swap(turn, window).wait_send()
            swap(turn + 1, window).wait_send()
        if layer > 0:
            move_rows(out, dy, True, False)
            pump(3)

    pump(4)

    table[...] = jnp.zeros_like(table)
    groups = table.shape[0] // (LAYERS * heads)

    def scatter(step_index, carry):
        total = None
        for lane in range(4):
            j = step_index * 4 + lane
            row = index_t[pl.ds(j, 1), :]
            low_part = jnp.broadcast_to(row & 127, (128, CELL))
            hot = (lax.broadcasted_iota(jnp.int32, (128, CELL), 0) == low_part).astype(f32).astype(bf16)
            score = grad_bias[:, pl.ds(j, 1), :].reshape(LAYERS * heads, CELL)
            high = jnp.broadcast_to(row >> 7, score.shape)
            left = jnp.concatenate(
                [jnp.where(high == group, score, 0.0) for group in range(groups)], axis=0
            ).astype(bf16)
            value = nt(left, hot)
            total = value if total is None else total + value
        table[...] += total
        return carry

    lax.fori_loop(0, CELL // 4, scatter, 0)
    for layer in range(LAYERS):
        for group in range(groups):
            first = (group * LAYERS + layer) * heads
            vectors[0, layer, REL_ROW : REL_ROW + heads, group * 128 : (group + 1) * 128] = table[
                first : first + heads, :
            ]
    vector_copy(0).start()
    for phase in range(BITS):
        pump(4)
        vector_step(phase)
    while step:
        pump(4)


def run_backward(shift, cot, valid, gain1, gain2, index_t, weights, kept):
    width = cot.shape[1]
    heads_width = weights[1].shape[1]
    hidden = weights[2].shape[2]
    heads = heads_width // HD
    rows = -(-529 // 128) * 128
    part = width >> BITS
    widths = chunk_widths(heads_width, hidden)
    shapes = saved_shapes(width, heads_width, hidden)
    vmem = pl.BlockSpec(memory_space=pltpu.VMEM)
    hbm = pl.BlockSpec(memory_space=pl.ANY)
    smem = pl.BlockSpec(memory_space=pltpu.SMEM)
    grads = [pltpu.VMEM((2,) * BITS + (part, w), bf16) for w in widths] * LAYERS
    landed = [
        pltpu.VMEM((2,) * (BITS - 1 - phase) + (part, w), bf16) for w in widths for phase in range(BITS)
    ]
    swaps = (2, WINDOWS, CELL, width)
    rounds = (2 * LAYERS, WINDOWS)
    vectors = (LAYERS, VECTOR_ROWS, width)
    chunk_rounds = (LAYERS, len(widths), BITS)
    return pl.pallas_call(
        functools.partial(backward_kernel, shift),
        out_shape=(
            jax.ShapeDtypeStruct((ROWS, width), f32),
            jax.ShapeDtypeStruct((LAYERS, part, sum(widths)), f32),
            jax.ShapeDtypeStruct(vectors, f32),
        ),
        in_specs=[vmem, smem, vmem, vmem, vmem] + [hbm] * (4 + len(SAVED)),
        out_specs=(vmem,) * 3,
        scratch_shapes=[pltpu.VMEM(w.shape[1:], bf16) for w in weights]
        + [pltpu.VMEM(shapes[name][0], shapes[name][1]) for name in SAVED]
        + grads
        + landed
        + [
            pltpu.VMEM((ROWS, width), f32),
            pltpu.VMEM((ROWS, width), bf16),
            pltpu.VMEM((ROWS, hidden), bf16),
            pltpu.VMEM(swaps, bf16),
            pltpu.VMEM(swaps, bf16),
            pltpu.VMEM((ROWS, heads_width), bf16),
            pltpu.VMEM((3, ROWS, heads_width), bf16),
            pltpu.VMEM((LAYERS * heads, CELL, CELL), f32),
            pltpu.VMEM((rows // 128 * LAYERS * heads, 128), f32),
            pltpu.VMEM((BITS,) + vectors, f32),
            pltpu.VMEM((BITS,) + vectors, f32),
            pltpu.SemaphoreType.DMA((4,)),
            pltpu.SemaphoreType.DMA((len(SAVED),)),
            pltpu.SemaphoreType.DMA(rounds),
            pltpu.SemaphoreType.DMA(rounds),
            pltpu.SemaphoreType.DMA(chunk_rounds),
            pltpu.SemaphoreType.DMA(chunk_rounds),
            pltpu.SemaphoreType.REGULAR(chunk_rounds[1:]),
            pltpu.SemaphoreType.DMA((BITS,)),
            pltpu.SemaphoreType.DMA((BITS,)),
        ],
        compiler_params=pltpu.CompilerParams(
            collective_id=1, has_side_effects=True, vmem_limit_bytes=VMEM_LIMIT
        ),
        name="backward",
    )(cot, valid, gain1, gain2, index_t, *weights, *[kept[name] for name in SAVED])


def result_kernel(x_ref, dx_ref, reduced, vectors, *outs):
    (output, input_grad, g1, o1, qkv_g, qv_g, rel_g, proj_g, pb_g, g2, o2, up_g, ub_g, down_g, db_g) = outs
    move_rows(x_ref, output, True, None)
    move_rows(dx_ref, input_grad, False, None)
    hidden = up_g.shape[2]
    heads_width = proj_g.shape[1]
    width = g1.shape[1]
    table_rows, heads = rel_g.shape[1:]
    for layer in range(LAYERS):
        row = slice(layer, layer + 1)
        for number, ref in enumerate((g1, o1, pb_g, g2, o2, db_g)):
            ref[row, :] = vectors[layer, number : number + 1, :]
        qv_g[layer, 0:1, :] = vectors[layer, 6:7, :heads_width]
        qv_g[layer, 1:2, :] = vectors[layer, 6:7, heads_width:]
        ub_g[row, :width] = vectors[layer, 7:8, :]
        ub_g[row, width:] = vectors[layer, 8:9, :]
        rel = vectors[layer, REL_ROW : REL_ROW + heads, :].T
        rel_g[layer] = rel[:table_rows, :]
        down_g[layer] = reduced[layer, :, :hidden].T
        up_g[layer] = reduced[layer, :, hidden : 2 * hidden]
        last = 2 * hidden
        proj_g[layer] = reduced[layer, :, last : last + heads_width].T
        for slot, place in ((2, 1), (0, 2), (1, 3)):
            first = last + place * heads_width
            qkv_g[layer, slot] = reduced[layer, :, first : first + heads_width]


def per_device(
    tokens,
    region_ids,
    rel_index,
    valid,
    ln1_gain,
    ln1_bias,
    qkv_weight,
    qv_bias,
    rel_table,
    proj_weight,
    proj_bias,
    ln2_gain,
    ln2_bias,
    fc1_weight,
    fc1_bias,
    fc2_weight,
    fc2_bias,
    cotangent,
):
    devices = lax.axis_size("dp")
    group = devices >> BITS
    shift = group.bit_length() - 1
    width = tokens.shape[1]
    heads_width = proj_weight.shape[1]
    hidden = fc1_weight.shape[2]
    count = SIDE // WIN
    region = (
        region_ids.reshape(count, WIN, count, WIN).transpose(0, 2, 1, 3).reshape(WINDOWS, CELL)
    )
    bias, mask, index_t = make_bias(rel_table, rel_index, region)
    weights = (qkv_weight, proj_weight, fc1_weight, fc2_weight)
    vectors = (ln1_gain, ln1_bias, qv_bias, proj_bias, ln2_gain, ln2_bias, fc1_bias, fc2_bias)
    x, kept = run_forward(tokens, vectors, bias, mask, weights)
    dx, reduced, sums = run_backward(
        shift, cotangent, valid, ln1_gain, ln2_gain, index_t, weights, kept
    )
    if group > 1:
        sets = [list(range(first, first + group)) for first in range(0, devices, group)]
        reduced = lax.psum_scatter(
            reduced, "dp", scatter_dimension=1, axis_index_groups=sets, tiled=True
        )
        sums = lax.psum(sums, "dp", axis_index_groups=sets)
    part = width // devices
    shapes = (
        (ROWS, width),
        (ROWS, width),
        (LAYERS, width),
        (LAYERS, width),
        (LAYERS, 3, part, heads_width),
        (LAYERS, 2, heads_width),
        rel_table.shape,
        (LAYERS, heads_width, part),
        (LAYERS, width),
        (LAYERS, width),
        (LAYERS, width),
        (LAYERS, part, hidden),
        (LAYERS, hidden),
        (LAYERS, hidden, part),
        (LAYERS, width),
    )
    vmem = pl.BlockSpec(memory_space=pltpu.VMEM)
    return tuple(
        pl.pallas_call(
            result_kernel,
            out_shape=[jax.ShapeDtypeStruct(shape, f32) for shape in shapes],
            in_specs=[vmem] * 4,
            out_specs=[vmem] * len(shapes),
            compiler_params=pltpu.CompilerParams(vmem_limit_bytes=VMEM_LIMIT),
            name="results",
        )(x, dx, reduced, sums)
    )


def solution(mesh):
    return jax.shard_map(
        per_device,
        mesh=mesh,
        in_specs=(
            P("dp", None),
            P(),
            P(),
            P("dp"),
            P(),
            P(),
            P(None, None, None, "tensor"),
            P(None, None, "tensor"),
            P(None, None, "tensor"),
            P(None, "tensor", None),
            P(),
            P(),
            P(),
            P(None, None, "tensor"),
            P(None, "tensor"),
            P(None, "tensor", None),
            P(),
            P("dp", None),
        ),
        out_specs=(
            P("dp", None),
            P("dp", None),
            P(),
            P(),
            P(None, None, "dp", "tensor"),
            P(None, None, "tensor"),
            P(None, None, "tensor"),
            P(None, "tensor", "dp"),
            P(),
            P(),
            P(),
            P(None, "dp", "tensor"),
            P(None, "tensor"),
            P(None, "tensor", "dp"),
            P(),
        ),
        check_vma=False,
    )
```

```python
import functools

import jax
import jax.numpy as jnp
from jax import lax
from jax.experimental import pallas as pl
from jax.experimental.pallas import tpu as pltpu
from jax.sharding import PartitionSpec as P

HD = 32
WIN = 12
SIDE = 24
LAYERS = 2
SHIFT = 6
ROWS = SIDE * SIDE
CELL = WIN * WIN
WINDOWS = ROWS // CELL
PER_TILE = 4
LANES = PER_TILE * HD
EPSILON = 1e-05
UNROLL = 8
LOG2E = 1.4426950408889634
SCALE = HD**-0.5
VMEM_LIMIT = 62 * 1024 * 1024
MESH_ID = pl.DeviceIdType.MESH

f32 = jnp.float32
bf16 = jnp.bfloat16


def nn(a, b):
    return jnp.dot(a, b, preferred_element_type=f32)


def nt(a, b):
    return lax.dot_general(a, b, (((1,), (1,)), ((), ())), preferred_element_type=f32)


def tn(a, b):
    return lax.dot_general(a, b, (((0,), (0,)), ((), ())), preferred_element_type=f32)


def window_row(i, j, shifted):
    if shifted:
        i, j = (i - SHIFT) % SIDE, (j - SHIFT) % SIDE
    return ((i // WIN) * (SIDE // WIN) + j // WIN) * CELL + (i % WIN) * WIN + j % WIN


def pieces(source, target):
    found = []
    for i in range(SIDE):
        for j in range(0, SIDE, SHIFT):
            row = [i * SIDE + j if o is None else window_row(i, j, o) for o in (source, target)]
            found.append(tuple(row))
    return found


def move_rows(source_ref, target_ref, source, target):
    for here, there in pieces(source, target):
        target_ref[there : there + SHIFT, :] = source_ref[here : here + SHIFT, :]


def lane_head(values, head):
    lane = lax.broadcasted_iota(jnp.int32, values.shape, 1)
    return jnp.where((lane >= HD * head) & (lane < HD * (head + 1)), values, jnp.zeros_like(values))


def row_norm(values):
    center = values - jnp.mean(values, axis=-1, keepdims=True)
    scale = lax.rsqrt(jnp.mean(center * center, axis=-1, keepdims=True) + EPSILON)
    return center * scale, scale


def wide(ref, layer):
    return ref[layer : layer + 1, :].astype(f32)


def hot_rows(index_t, key):
    row = index_t[pl.ds(key, 1), :]
    low = jnp.broadcast_to(row & 127, (128, CELL))
    hot = (lax.broadcasted_iota(jnp.int32, (128, CELL), 0) == low).astype(f32).astype(bf16)
    return hot, row >> 7


def fill_index(index, index_t):
    index_t[...] = index[...].astype(f32).T.astype(jnp.int32)


def fill_bias(table, index_t, bias, rows):
    heads, _, entries = table.shape
    groups = rows.shape[1] // 128
    rows[...] = jnp.zeros_like(rows)
    values = table[...].astype(f32)
    for layer in range(LAYERS):
        rows[layer * heads : (layer + 1) * heads, :entries] = values[:, layer, :]
    count = LAYERS * heads
    left = jnp.concatenate(
        [rows[:, group * 128 : (group + 1) * 128] for group in range(groups)], axis=0
    ).astype(bf16)

    def one(step, carry):
        for lane in range(UNROLL):
            key = step * UNROLL + lane
            hot, high = hot_rows(index_t, key)
            high = jnp.broadcast_to(high, (count, CELL))
            got = nn(left, hot)
            value = got[:count]
            for group in range(1, groups):
                value = jnp.where(high == group, got[group * count : (group + 1) * count], value)
            bias[:, pl.ds(key, 1), :] = (value * LOG2E).reshape(count, 1, CELL)
        return carry

    lax.fori_loop(0, CELL // UNROLL, one, 0)


def fill_mask(region, mask):
    values = region[...].astype(f32)
    count = SIDE // WIN
    for window in range(WINDOWS):
        first = (window // count) * WIN * SIDE + (window % count) * WIN
        row = jnp.concatenate(
            [values[:, first + i * SIDE : first + i * SIDE + WIN] for i in range(WIN)], axis=1
        )
        row = jnp.broadcast_to(row, (CELL, CELL))
        mask[window] = (row == row.T).astype(f32)


def forward_attention(q, k, v, bias, mask, store):
    stacked = jnp.concatenate([lane_head(k, head) for head in range(PER_TILE)], axis=0)
    scores = nt(stacked, q)
    v_t = v.T
    mixed = []
    for head in range(PER_TILE):
        s = scores[head * CELL : (head + 1) * CELL] * (SCALE * LOG2E) + bias(head)
        if mask is not None:
            s = jnp.where(mask > 0.5, s, -1000000000.0 * LOG2E)
        e = jnp.exp2(s - jnp.max(s, axis=0, keepdims=True))
        prob = (e * (1.0 / jnp.sum(e, axis=0, keepdims=True))).astype(bf16)
        store(head, prob)
        mixed.append(nn(v_t[head * HD : (head + 1) * HD], prob))
    return jnp.concatenate(mixed, axis=0).T


SAVED = ("h1", "n1", "r1", "qkv", "prob", "mix", "h2", "n2", "r2", "hid", "slope")


def saved_shapes(width, heads_width, hidden):
    heads = heads_width // HD
    return {
        "h1": ((ROWS, width), bf16),
        "n1": ((ROWS, width), bf16),
        "r1": ((ROWS, 1), f32),
        "qkv": ((3, ROWS, heads_width), bf16),
        "prob": ((WINDOWS, heads, CELL, CELL), bf16),
        "mix": ((ROWS, heads_width), bf16),
        "h2": ((ROWS, width), bf16),
        "n2": ((ROWS, width), bf16),
        "r2": ((ROWS, 1), f32),
        "hid": ((ROWS, hidden), bf16),
        "slope": ((ROWS, hidden), bf16),
    }


def forward_kernel(*refs):
    it = iter(refs)
    tokens, gain1, off1, qv_b, proj_b, gain2, off2, up_b, down_b = (next(it) for _ in range(9))
    table, index, region = (next(it) for _ in range(3))
    weights_hbm = [next(it) for _ in range(4)]
    out = next(it)
    kept_hbm = {name: next(it) for name in SAVED}
    weights = [next(it) for _ in range(4)]
    kept = {name: next(it) for name in SAVED}
    x, y, send, recv, bias, mask, index_t, table_rows = (next(it) for _ in range(8))
    weight_sem, kept_sem, send_sem, recv_sem = (next(it) for _ in range(4))
    qkv_w, proj_w, up_w, down_w = weights
    heads_width = proj_w.shape[1]
    heads = heads_width // HD
    other = 1 - lax.axis_index("tensor")

    def load(slot, layer):
        return pltpu.make_async_copy(
            weights_hbm[slot].at[layer], weights[slot].at[layer], weight_sem.at[slot, layer]
        )

    def keep(name, layer):
        return pltpu.make_async_copy(
            kept[name].at[layer], kept_hbm[name].at[layer], kept_sem.at[SAVED.index(name), layer]
        )

    def swap(turn, window):
        return pltpu.make_async_remote_copy(
            src_ref=send.at[turn, window],
            dst_ref=recv.at[turn, window],
            send_sem=send_sem.at[turn, window],
            recv_sem=recv_sem.at[turn, window],
            device_id={"tensor": other},
            device_id_type=MESH_ID,
        )

    for layer in range(LAYERS):
        for slot in range(4):
            load(slot, layer).start()
    barrier = pltpu.get_barrier_semaphore()
    pl.semaphore_signal(barrier, inc=1, device_id={"tensor": other}, device_id_type=MESH_ID)

    y[...] = tokens[...].astype(f32)
    move_rows(y, x, None, False)
    fill_index(index, index_t)
    fill_bias(table, index_t, bias, table_rows)
    fill_mask(region, mask)

    for layer in range(LAYERS):
        load(0, layer).wait()
        load(1, layer).wait()
        if layer == 0:
            pl.semaphore_wait(barrier, 1)

        def attend(window, layer=layer):
            at = slice(window * CELL, (window + 1) * CELL)
            normed, scale = row_norm(x[at, :])
            h1 = (normed * wide(gain1, layer) + wide(off1, layer)).astype(bf16)
            kept["n1"][layer, at, :] = normed.astype(bf16)
            kept["r1"][layer, at, :] = scale
            kept["h1"][layer, at, :] = h1
            kept["qkv"][layer, 0, at, :] = (
                nn(h1, qkv_w[layer, 0]) + qv_b[layer, 0:1, :].astype(f32)
            ).astype(bf16)
            kept["qkv"][layer, 1, at, :] = nn(h1, qkv_w[layer, 1]).astype(bf16)
            kept["qkv"][layer, 2, at, :] = (
                nn(h1, qkv_w[layer, 2]) + qv_b[layer, 1:2, :].astype(f32)
            ).astype(bf16)
            same = mask[window] if layer == 1 else None
            for tile in range(heads_width // LANES):
                cols = slice(tile * LANES, (tile + 1) * LANES)

                def store(head, prob, tile=tile):
                    kept["prob"][layer, window, tile * PER_TILE + head] = prob

                kept["mix"][layer, at, cols] = forward_attention(
                    kept["qkv"][layer, 0, at, cols],
                    kept["qkv"][layer, 1, at, cols],
                    kept["qkv"][layer, 2, at, cols],
                    lambda head, tile=tile: bias[layer * heads + tile * PER_TILE + head],
                    same,
                    store,
                ).astype(bf16)
            send[2 * layer, window] = nn(kept["mix"][layer, at, :], proj_w[layer]).astype(bf16)
            swap(2 * layer, window).start()

        for window in range(WINDOWS):
            attend(window)
        for name in ("h1", "n1", "r1", "qkv", "prob", "mix"):
            keep(name, layer).start()
        load(2, layer).wait()
        load(3, layer).wait()

        def expand(window, layer=layer):
            at = slice(window * CELL, (window + 1) * CELL)
            swap(2 * layer, window).wait_recv()
            total = send[2 * layer, window].astype(f32) + recv[2 * layer, window].astype(f32)
            middle = x[at, :] + total + wide(proj_b, layer)
            x[at, :] = middle
            normed, scale = row_norm(middle)
            h2 = (normed * wide(gain2, layer) + wide(off2, layer)).astype(bf16)
            kept["n2"][layer, at, :] = normed.astype(bf16)
            kept["r2"][layer, at, :] = scale
            kept["h2"][layer, at, :] = h2
            u = nn(h2, up_w[layer]) + wide(up_b, layer)
            phi = 0.5 + 0.5 * lax.erf(u * 0.7071067811865476)
            hidden = (u * phi).astype(bf16)
            kept["slope"][layer, at, :] = (
                phi + u * jnp.exp(u * u * -0.5) * 0.3989422804014327
            ).astype(bf16)
            kept["hid"][layer, at, :] = hidden
            send[2 * layer + 1, window] = nn(hidden, down_w[layer]).astype(bf16)
            swap(2 * layer + 1, window).start()

        for window in range(WINDOWS):
            expand(window)
        for name in ("h2", "n2", "r2", "hid", "slope"):
            keep(name, layer).start()
        target = y if layer == 0 else out

        def finish(window, layer=layer, target=target):
            at = slice(window * CELL, (window + 1) * CELL)
            swap(2 * layer + 1, window).wait_recv()
            total = send[2 * layer + 1, window].astype(f32) + recv[2 * layer + 1, window].astype(f32)
            target[at, :] = x[at, :] + total + wide(down_b, layer)

        for window in range(WINDOWS):
            finish(window)
        if layer == 0:
            move_rows(y, x, False, True)

    for turn in range(2 * LAYERS):
        for window in range(WINDOWS):
            swap(turn, window).wait_send()
    for layer in range(LAYERS):
        for name in SAVED:
            keep(name, layer).wait()


def run_forward(tokens, vectors, tables, weights):
    width = tokens.shape[1]
    heads_width = weights[1].shape[1]
    heads = heads_width // HD
    entries = -(-tables[0].shape[2] // 128) * 128
    hidden = weights[2].shape[2]
    shapes = saved_shapes(width, heads_width, hidden)
    vmem = pl.BlockSpec(memory_space=pltpu.VMEM)
    hbm = pl.BlockSpec(memory_space=pl.ANY)
    kept = [jax.ShapeDtypeStruct((LAYERS,) + shapes[name][0], shapes[name][1]) for name in SAVED]
    swaps = (2 * LAYERS, WINDOWS)
    outs = pl.pallas_call(
        forward_kernel,
        out_shape=[jax.ShapeDtypeStruct((ROWS, width), f32)] + kept,
        in_specs=[vmem] * 12 + [hbm] * 4,
        out_specs=[vmem] + [hbm] * len(SAVED),
        scratch_shapes=[pltpu.VMEM(w.shape, bf16) for w in weights]
        + [pltpu.VMEM(s.shape, s.dtype) for s in kept]
        + [
            pltpu.VMEM((ROWS, width), f32),
            pltpu.VMEM((ROWS, width), f32),
            pltpu.VMEM(swaps + (CELL, width), bf16),
            pltpu.VMEM(swaps + (CELL, width), bf16),
            pltpu.VMEM((LAYERS * heads, CELL, CELL), f32),
            pltpu.VMEM((WINDOWS, CELL, CELL), f32),
            pltpu.VMEM((CELL, CELL), jnp.int32),
            pltpu.VMEM((LAYERS * heads, entries), f32),
            pltpu.SemaphoreType.DMA((4, LAYERS)),
            pltpu.SemaphoreType.DMA((len(SAVED), LAYERS)),
            pltpu.SemaphoreType.DMA(swaps),
            pltpu.SemaphoreType.DMA(swaps),
        ],
        compiler_params=pltpu.CompilerParams(
            collective_id=0, has_side_effects=True, vmem_limit_bytes=VMEM_LIMIT
        ),
        name="forward",
    )(tokens, *vectors, *tables, *weights)
    return outs[0], dict(zip(SAVED, outs[1:]))


BITS = 4
ORDERS = (
    (3, 2, 1, 0),
    (1, 3, 2, 0),
    (2, 1, 3, 0),
    (3, 2, 1, 0),
    (3, 2, 1, 0),
    (3, 2, 1, 0),
    (2, 3, 1, 0),
    (2, 3, 1, 0),
)
VECTOR_ROWS = 24
HALVES = 2
START = 100
VECTORS = 99

SCHEDULE = (
    (108,),
    (109,),
    (),
    (),
    (110,),
    (111,),
    (),
    (),
    (),
    (),
    (),
    (112, 8, 108, 9),
    (),
    (),
    (),
    (),
    (114, 10, 109, 110),
    (115,),
    (),
    (),
    (),
    (113, 8, 108, 11, 111),
    (101, 10),
    (12, 110, 112, 8, 108, 14),
    (114,),
    (102,),
    (9, 15),
    (),
    (115,),
    (),
    (13, 11, 100, 111, 1),
    (10, 109, 110, 8, 12, 112),
    (14, 114),
    (113, 11, 111),
    (15, 101, 115, 10),
    (),
    (12, 112),
    (),
    (14,),
    (106, 114),
    (),
    (103, 11, 2, 107, 102),
    (9, 109, 12, 13, 113, 14, 15, 0, 100),
    (115, 1, 104, 101, 2, 6, 9),
    (13, 113, 15, 7, 102, 99, 105, 3, 103, 0, 100, 13, 1, 101, 99, 106, 4, 104, 0, 107, 100, 2, 102, 3, 103, 1, 99, 0, 5, 105, 4, 104, 2, 6, 106, 3, 103, 5, 105, 7, 107, 4, 6, 99, 104, 3, 106, 5, 105, 7, 107, 4, 6, 5, 7),
)
REL_ROW = 9


def chunk_widths(heads_width, hidden):
    return (hidden // 2,) * 4 + (heads_width,) * 4


def norm_back(grad, normed, scale, gain):
    c = grad * gain
    inner = c - jnp.mean(c, axis=-1, keepdims=True)
    return scale * (inner - normed * jnp.mean(c * normed, axis=-1, keepdims=True))


def column_sum(values):
    return jnp.sum(values, axis=0, keepdims=True)


def backward_attention(q, k, v, grad, prob, add_score):
    stacked = jnp.concatenate([lane_head(v, head) for head in range(PER_TILE)], axis=0)
    grad_prob = nt(stacked, grad)
    k_t = k.T
    grad_q, grad_k, grad_v = [], None, None
    for head in range(PER_TILE):
        p = prob(head)
        weighted = p.astype(f32) * grad_prob[head * CELL : (head + 1) * CELL]
        score = weighted - p.astype(f32) * column_sum(weighted)
        add_score(head, score)
        low = score.astype(bf16)
        part_v = nn(p, lane_head(grad, head))
        part_k = nn(low, lane_head(q, head))
        grad_v = part_v if grad_v is None else grad_v + part_v
        grad_k = part_k if grad_k is None else grad_k + part_k
        grad_q.append(nn(k_t[head * HD : (head + 1) * HD], low))
    return jnp.concatenate(grad_q, axis=0).T * SCALE, grad_k * SCALE, grad_v


def backward_kernel(shift, *refs):
    it = iter(refs)

    def take(count):
        return [next(it) for _ in range(count)]

    cot, valid, gain1, gain2, index = take(5)
    weights_hbm = take(4)
    kept_hbm = dict(zip(SAVED, take(len(SAVED))))
    out, reduced, vectors_out = take(3)
    weights = take(4)
    kept = dict(zip(SAVED, take(len(SAVED))))
    chunks = len(ORDERS)
    grads = [take(chunks) for _ in range(LAYERS)]
    landed = [take(BITS) for _ in range(chunks)]
    dy, low, pre, send, recv, grad_mix, grad_qkv, grad_bias, table, vectors, vectors_in, index_t = take(12)
    weight_sem, kept_sem, send_sem, recv_sem = take(4)
    chunk_send, chunk_recv, credit, vector_send, vector_recv = take(5)
    qkv_w, proj_w, up_w, down_w = weights
    heads_width = proj_w.shape[0]
    hidden = up_w.shape[1]
    width = dy.shape[1]
    heads = heads_width // HD
    part = width >> BITS
    widths = chunk_widths(heads_width, hidden)

    me = lax.axis_index("dp")
    other = 1 - lax.axis_index("tensor")
    places = [1 << (shift + BITS - 1 - dim) for dim in range(BITS)]
    mine = [lax.rem(lax.div(me, place), 2) for place in places]
    partner = [me + place - 2 * place * bit for place, bit in zip(places, mine)]

    def load(slot, layer):
        return pltpu.make_async_copy(weights_hbm[slot].at[layer], weights[slot], weight_sem.at[slot])

    def fetch(name, layer):
        return pltpu.make_async_copy(
            kept_hbm[name].at[layer], kept[name], kept_sem.at[SAVED.index(name)]
        )

    def swap(turn, half):
        return pltpu.make_async_remote_copy(
            src_ref=send.at[turn % 2, half],
            dst_ref=recv.at[turn % 2, half],
            send_sem=send_sem.at[turn, half],
            recv_sem=recv_sem.at[turn, half],
            device_id={"tensor": other},
            device_id_type=MESH_ID,
        )

    step = {}

    def region(chunk, phase, bit):
        order = ORDERS[chunk]
        index = [slice(None)] * BITS
        for dim in order[:phase]:
            index[dim] = mine[dim]
        index[order[phase]] = bit
        return tuple(index)

    def chunk_copy(layer, chunk, phase):
        dim = ORDERS[chunk][phase]
        return pltpu.make_async_remote_copy(
            src_ref=grads[layer][chunk].at[region(chunk, phase, 1 - mine[dim])],
            dst_ref=landed[chunk][phase],
            send_sem=chunk_send.at[layer, chunk, phase],
            recv_sem=chunk_recv.at[layer, chunk, phase],
            device_id={"dp": partner[dim]},
            device_id_type=MESH_ID,
        )

    def begin(layer, chunk):
        if layer < LAYERS - 1:
            pl.semaphore_wait(credit.at[chunk, step[layer, chunk]], 1)
        chunk_copy(layer, chunk, step[layer, chunk]).start()

    def advance(layer, chunk):
        phase = step[layer, chunk]
        dim = ORDERS[chunk][phase]
        chunk_copy(layer, chunk, phase).wait()
        keep = region(chunk, phase, mine[dim])
        free = [d for d in range(BITS) if isinstance(keep[d], slice)]
        ref, arrived = grads[layer][chunk], landed[chunk][phase]
        first = sum(widths[:chunk])
        for number in range(1 << len(free)):
            bits = [(number >> (len(free) - 1 - n)) & 1 for n in range(len(free))]
            index = list(keep)
            for d, bit in zip(free, bits):
                index[d] = bit
            here = ref[tuple(index)]
            there = arrived[tuple(bits)] if bits else arrived[...]
            if phase < BITS - 1:
                ref[tuple(index)] = here + there
            else:
                reduced[layer, :, first : first + widths[chunk]] = here.astype(f32) + there.astype(f32)
        if layer == LAYERS - 1:
            pl.semaphore_signal(
                credit.at[chunk, phase], inc=1, device_id={"dp": partner[dim]}, device_id_type=MESH_ID
            )
        step[layer, chunk] = phase + 1

    def finish_chunk(layer, chunk, left, right):
        half = width // 2
        for top in range(2):
            value = tn(left[:, top * half : (top + 1) * half], right)
            grads[layer][chunk][top] = value.astype(bf16).reshape(2, 2, 2, part, widths[chunk])
        step[layer, chunk] = 0
        point()

    place = iter(SCHEDULE)

    def point():
        for action in next(place):
            if action == VECTORS:
                vector_step()
                continue
            chosen = divmod(action % START, chunks)
            if action >= START:
                begin(*chosen)
            else:
                advance(*chosen)

    def vector_copy(phase):
        return pltpu.make_async_remote_copy(
            src_ref=vectors.at[phase],
            dst_ref=vectors_in.at[phase],
            send_sem=vector_send.at[phase],
            recv_sem=vector_recv.at[phase],
            device_id={"dp": partner[phase]},
            device_id_type=MESH_ID,
        )

    rounds = iter(range(BITS))

    def vector_step():
        phase = next(rounds)
        vector_copy(phase).wait()
        total = vectors[phase] + vectors_in[phase]
        if phase < BITS - 1:
            vectors[phase + 1] = total
            vector_copy(phase + 1).start()
        else:
            vectors_out[...] = total

    first_order = ("hid", "slope", "h2", "n2", "r2", "mix", "prob", "qkv", "h1", "n1", "r1")
    top = LAYERS - 1
    fetch("hid", top).start()
    load(3, top).start()
    fetch("slope", top).start()
    load(2, top).start()
    for name in first_order[2:6]:
        fetch(name, top).start()
    load(1, top).start()
    for name in first_order[6:]:
        fetch(name, top).start()
    load(0, top).start()
    barrier = pltpu.get_barrier_semaphore()
    pl.semaphore_signal(barrier, inc=1, device_id={"tensor": other}, device_id_type=MESH_ID)
    for dim in range(BITS):
        pl.semaphore_signal(barrier, inc=1, device_id={"dp": partner[dim]}, device_id_type=MESH_ID)

    out[...] = cot[...].astype(f32) * valid[0].astype(f32)
    move_rows(out, dy, None, True)
    vectors[0] = jnp.zeros(vectors.shape[1:], f32)
    grad_bias[...] = jnp.zeros_like(grad_bias)
    pl.semaphore_wait(barrier, 1 + BITS)

    def rows_of(part_index, count):
        size = ROWS // count
        return slice(part_index * size, (part_index + 1) * size)

    for layer in reversed(range(LAYERS)):
        turn = 2 * (LAYERS - 1 - layer)

        def add_row(row, value, first=0):
            cols = slice(first, first + value.shape[1])
            vectors[0, layer, row : row + 1, cols] += value

        def free(*names):
            for name in names if layer > 0 else ():
                fetch(name, layer - 1).start()

        def free_weight(slot):
            if layer > 0:
                load(slot, layer - 1).start()

        add_row(5, column_sum(dy[...]))
        low[...] = dy[...].astype(bf16)
        fetch("hid", layer).wait()
        finish_chunk(layer, 0, low[...], kept["hid"][:, : hidden // 2])
        finish_chunk(layer, 1, low[...], kept["hid"][:, hidden // 2 :])
        free("hid")
        fetch("slope", layer).wait()
        load(3, layer).wait()
        load(2, layer).wait()
        for half in range(HALVES):
            at = rows_of(half, HALVES)
            grad = nt(low[at, :], down_w[...]) * kept["slope"][at, :].astype(f32)
            add_row(7, column_sum(grad[:, :width]))
            add_row(8, column_sum(grad[:, width:]))
            pre[at, :] = grad.astype(bf16)
            send[turn % 2, half] = nt(pre[at, :], up_w[...]).astype(bf16)
            swap(turn, half).start()
            point()
        free("slope")
        free_weight(3)
        free_weight(2)
        fetch("h2", layer).wait()
        finish_chunk(layer, 2, kept["h2"][...], pre[:, : hidden // 2])
        finish_chunk(layer, 3, kept["h2"][...], pre[:, hidden // 2 :])
        free("h2")
        for name in ("n2", "r2", "mix"):
            fetch(name, layer).wait()
        load(1, layer).wait()
        for half in range(HALVES):
            at = rows_of(half, HALVES)
            swap(turn, half).wait_recv()
            grad = send[turn % 2, half].astype(f32) + recv[turn % 2, half].astype(f32)
            normed = kept["n2"][at, :].astype(f32)
            add_row(3, column_sum(grad * normed))
            add_row(4, column_sum(grad))
            total = dy[at, :] + norm_back(grad, normed, kept["r2"][at, :], wide(gain2, layer))
            dy[at, :] = total
            add_row(2, column_sum(total))
            low[at, :] = total.astype(bf16)
            grad_mix[at, :] = nt(low[at, :], proj_w[...]).astype(bf16)
            point()
        free("n2", "r2")
        free_weight(1)
        finish_chunk(layer, 4, low[...], kept["mix"][...])
        free("mix")

        fetch("prob", layer).wait()
        fetch("qkv", layer).wait()
        for window in range(WINDOWS):
            at = rows_of(window, WINDOWS)
            for tile in range(heads_width // LANES):
                cols = slice(tile * LANES, (tile + 1) * LANES)

                def add_score(head, score):
                    grad_bias[layer * heads + tile * PER_TILE + head] += score

                parts = backward_attention(
                    kept["qkv"][0, at, cols],
                    kept["qkv"][1, at, cols],
                    kept["qkv"][2, at, cols],
                    grad_mix[at, cols],
                    lambda head: kept["prob"][window, tile * PER_TILE + head],
                    add_score,
                )
                for slot, value in enumerate(parts):
                    grad_qkv[slot, at, cols] = value.astype(bf16)
                add_row(6, column_sum(parts[0]), tile * LANES)
                add_row(6, column_sum(parts[2]), heads_width + tile * LANES)
            point()
        free("prob", "qkv")
        load(0, layer).wait()
        for half in range(HALVES):
            at = rows_of(half, HALVES)
            total = nt(grad_qkv[0, at, :], qkv_w[0])
            total = total + nt(grad_qkv[1, at, :], qkv_w[1])
            total = total + nt(grad_qkv[2, at, :], qkv_w[2])
            send[(turn + 1) % 2, half] = total.astype(bf16)
            swap(turn + 1, half).start()
            point()
        free_weight(0)
        fetch("h1", layer).wait()
        for chunk, slot in ((5, 2), (6, 0), (7, 1)):
            finish_chunk(layer, chunk, kept["h1"][...], grad_qkv[slot])
        free("h1")
        fetch("n1", layer).wait()
        fetch("r1", layer).wait()
        for half in range(HALVES):
            at = rows_of(half, HALVES)
            swap(turn + 1, half).wait_recv()
            grad = send[(turn + 1) % 2, half].astype(f32) + recv[(turn + 1) % 2, half].astype(f32)
            normed = kept["n1"][at, :].astype(f32)
            add_row(0, column_sum(grad * normed))
            add_row(1, column_sum(grad))
            out[at, :] = dy[at, :] + norm_back(grad, normed, kept["r1"][at, :], wide(gain1, layer))
            point()
        free("n1", "r1")
        for half in range(HALVES):
            swap(turn, half).wait_send()
            swap(turn + 1, half).wait_send()
        if layer > 0:
            move_rows(out, dy, True, False)
        point()

    fill_index(index, index_t)
    table[...] = jnp.zeros_like(table)
    groups = table.shape[0] // (LAYERS * heads)

    def scatter(step_index, carry):
        total = None
        for lane in range(UNROLL):
            key = step_index * UNROLL + lane
            hot, high = hot_rows(index_t, key)
            score = grad_bias[:, pl.ds(key, 1), :].reshape(LAYERS * heads, CELL)
            high = jnp.broadcast_to(high, score.shape)
            left = jnp.concatenate(
                [jnp.where(high == group, score, 0.0) for group in range(groups)], axis=0
            ).astype(bf16)
            value = nt(left, hot)
            total = value if total is None else total + value
        table[...] += total
        return carry

    steps = CELL // UNROLL
    for quarter in range(2):
        lax.fori_loop(quarter * steps // 2, (quarter + 1) * steps // 2, scatter, 0)
        point()
    for layer in range(LAYERS):
        for group in range(groups):
            first = (group * LAYERS + layer) * heads
            vectors[0, layer, REL_ROW : REL_ROW + heads, group * 128 : (group + 1) * 128] = table[
                first : first + heads, :
            ]
    vector_copy(0).start()
    point()


def run_backward(shift, entries, cot, valid, gain1, gain2, index, weights, kept):
    width = cot.shape[1]
    heads_width = weights[1].shape[1]
    hidden = weights[2].shape[2]
    heads = heads_width // HD
    rows = -(-entries // 128) * 128
    part = width >> BITS
    widths = chunk_widths(heads_width, hidden)
    shapes = saved_shapes(width, heads_width, hidden)
    vmem = pl.BlockSpec(memory_space=pltpu.VMEM)
    hbm = pl.BlockSpec(memory_space=pl.ANY)
    smem = pl.BlockSpec(memory_space=pltpu.SMEM)
    grads = [pltpu.VMEM((2,) * BITS + (part, w), bf16) for w in widths] * LAYERS
    landed = [
        pltpu.VMEM((2,) * (BITS - 1 - phase) + (part, w), bf16) for w in widths for phase in range(BITS)
    ]
    swaps = (2, HALVES, ROWS // HALVES, width)
    rounds = (2 * LAYERS, HALVES)
    vectors = (LAYERS, VECTOR_ROWS, width)
    chunk_rounds = (LAYERS, len(widths), BITS)
    return pl.pallas_call(
        functools.partial(backward_kernel, shift),
        out_shape=(
            jax.ShapeDtypeStruct((ROWS, width), f32),
            jax.ShapeDtypeStruct((LAYERS, part, sum(widths)), f32),
            jax.ShapeDtypeStruct(vectors, f32),
        ),
        in_specs=[vmem, smem, vmem, vmem, vmem] + [hbm] * (4 + len(SAVED)),
        out_specs=(vmem,) * 3,
        scratch_shapes=[pltpu.VMEM(w.shape[1:], bf16) for w in weights]
        + [pltpu.VMEM(shapes[name][0], shapes[name][1]) for name in SAVED]
        + grads
        + landed
        + [
            pltpu.VMEM((ROWS, width), f32),
            pltpu.VMEM((ROWS, width), bf16),
            pltpu.VMEM((ROWS, hidden), bf16),
            pltpu.VMEM(swaps, bf16),
            pltpu.VMEM(swaps, bf16),
            pltpu.VMEM((ROWS, heads_width), bf16),
            pltpu.VMEM((3, ROWS, heads_width), bf16),
            pltpu.VMEM((LAYERS * heads, CELL, CELL), f32),
            pltpu.VMEM((rows // 128 * LAYERS * heads, 128), f32),
            pltpu.VMEM((BITS,) + vectors, f32),
            pltpu.VMEM((BITS,) + vectors, f32),
            pltpu.VMEM((CELL, CELL), jnp.int32),
            pltpu.SemaphoreType.DMA((4,)),
            pltpu.SemaphoreType.DMA((len(SAVED),)),
            pltpu.SemaphoreType.DMA(rounds),
            pltpu.SemaphoreType.DMA(rounds),
            pltpu.SemaphoreType.DMA(chunk_rounds),
            pltpu.SemaphoreType.DMA(chunk_rounds),
            pltpu.SemaphoreType.REGULAR(chunk_rounds[1:]),
            pltpu.SemaphoreType.DMA((BITS,)),
            pltpu.SemaphoreType.DMA((BITS,)),
        ],
        compiler_params=pltpu.CompilerParams(
            collective_id=1, has_side_effects=True, vmem_limit_bytes=VMEM_LIMIT
        ),
        name="backward",
    )(cot, valid, gain1, gain2, index, *weights, *[kept[name] for name in SAVED])


def result_kernel(x_ref, dx_ref, reduced, vectors, *outs):
    (output, input_grad, g1, o1, qkv_g, qv_g, rel_g, proj_g, pb_g, g2, o2, up_g, ub_g, down_g, db_g) = outs
    move_rows(x_ref, output, True, None)
    move_rows(dx_ref, input_grad, False, None)
    hidden = up_g.shape[2]
    heads_width = proj_g.shape[2]
    width = g1.shape[1]
    heads, _, entries = rel_g.shape
    for layer in range(LAYERS):
        row = slice(layer, layer + 1)
        for number, ref in enumerate((g1, o1, pb_g, g2, o2, db_g)):
            ref[row, :] = vectors[layer, number : number + 1, :]
        qv_g[layer, 0:1, :] = vectors[layer, 6:7, :heads_width]
        qv_g[layer, 1:2, :] = vectors[layer, 6:7, heads_width:]
        ub_g[row, :width] = vectors[layer, 7:8, :]
        ub_g[row, width:] = vectors[layer, 8:9, :]
        rel_g[:, layer, :] = vectors[layer, REL_ROW : REL_ROW + heads, :entries]
        down_g[layer] = reduced[layer, :, :hidden]
        up_g[layer] = reduced[layer, :, hidden : 2 * hidden]
        last = 2 * hidden
        proj_g[layer] = reduced[layer, :, last : last + heads_width]
        for slot, place in ((2, 1), (0, 2), (1, 3)):
            first = last + place * heads_width
            qkv_g[layer, slot] = reduced[layer, :, first : first + heads_width]


def per_device(
    tokens,
    region_ids,
    rel_index,
    valid,
    ln1_gain,
    ln1_bias,
    qkv_weight,
    qv_bias,
    rel_table,
    proj_weight,
    proj_bias,
    ln2_gain,
    ln2_bias,
    fc1_weight,
    fc1_bias,
    fc2_weight,
    fc2_bias,
    cotangent,
):
    devices = lax.axis_size("dp")
    group = devices >> BITS
    shift = group.bit_length() - 1
    width = tokens.shape[1]
    heads_width = proj_weight.shape[1]
    hidden = fc1_weight.shape[2]
    tables = (rel_table.transpose(2, 0, 1), rel_index, region_ids.reshape(1, ROWS))
    weights = (qkv_weight, proj_weight, fc1_weight, fc2_weight)
    vectors = (ln1_gain, ln1_bias, qv_bias, proj_bias, ln2_gain, ln2_bias, fc1_bias, fc2_bias)
    x, kept = run_forward(tokens, vectors, tables, weights)
    dx, reduced, sums = run_backward(
        shift, rel_table.shape[1], cotangent, valid, ln1_gain, ln2_gain, rel_index, weights, kept
    )
    if group > 1:
        sets = [list(range(first, first + group)) for first in range(0, devices, group)]
        reduced = lax.psum_scatter(
            reduced, "dp", scatter_dimension=1, axis_index_groups=sets, tiled=True
        )
        sums = lax.psum(sums, "dp", axis_index_groups=sets)
    part = width // devices
    shapes = (
        (ROWS, width),
        (ROWS, width),
        (LAYERS, width),
        (LAYERS, width),
        (LAYERS, 3, part, heads_width),
        (LAYERS, 2, heads_width),
        tables[0].shape,
        (LAYERS, part, heads_width),
        (LAYERS, width),
        (LAYERS, width),
        (LAYERS, width),
        (LAYERS, part, hidden),
        (LAYERS, hidden),
        (LAYERS, part, hidden),
        (LAYERS, width),
    )
    vmem = pl.BlockSpec(memory_space=pltpu.VMEM)
    outs = list(
        pl.pallas_call(
            result_kernel,
            out_shape=[jax.ShapeDtypeStruct(shape, f32) for shape in shapes],
            in_specs=[vmem] * 4,
            out_specs=[vmem] * len(shapes),
            compiler_params=pltpu.CompilerParams(vmem_limit_bytes=VMEM_LIMIT),
            name="results",
        )(x, dx, reduced, sums)
    )
    outs[6] = outs[6].transpose(1, 2, 0)
    outs[7] = outs[7].transpose(0, 2, 1)
    outs[13] = outs[13].transpose(0, 2, 1)
    return tuple(outs)


def solution(mesh):
    return jax.shard_map(
        per_device,
        mesh=mesh,
        in_specs=(
            P("dp", None),
            P(),
            P(),
            P("dp"),
            P(),
            P(),
            P(None, None, None, "tensor"),
            P(None, None, "tensor"),
            P(None, None, "tensor"),
            P(None, "tensor", None),
            P(),
            P(),
            P(),
            P(None, None, "tensor"),
            P(None, "tensor"),
            P(None, "tensor", None),
            P(),
            P("dp", None),
        ),
        out_specs=(
            P("dp", None),
            P("dp", None),
            P(),
            P(),
            P(None, None, "dp", "tensor"),
            P(None, None, "tensor"),
            P(None, None, "tensor"),
            P(None, "tensor", "dp"),
            P(),
            P(),
            P(),
            P(None, "dp", "tensor"),
            P(None, "tensor"),
            P(None, "tensor", "dp"),
            P(),
        ),
        check_vma=False,
    )
```

```python
import functools

import jax
import jax.numpy as jnp
from jax import lax
from jax.experimental import pallas as pl
from jax.experimental.pallas import tpu as pltpu
from jax.sharding import PartitionSpec as P

HD = 32
WIN = 12
SIDE = 24
LAYERS = 2
SHIFT = 6
ROWS = SIDE * SIDE
CELL = WIN * WIN
WINDOWS = ROWS // CELL
PER_TILE = 4
LANES = PER_TILE * HD
EPSILON = 1e-05
UNROLL = 8
LOG2E = 1.4426950408889634
SCALE = HD**-0.5
VMEM_LIMIT = 62 * 1024 * 1024
MESH_ID = pl.DeviceIdType.MESH

f32 = jnp.float32
bf16 = jnp.bfloat16


def nn(a, b):
    return jnp.dot(a, b, preferred_element_type=f32)


def nt(a, b):
    return lax.dot_general(a, b, (((1,), (1,)), ((), ())), preferred_element_type=f32)


def tn(a, b):
    return lax.dot_general(a, b, (((0,), (0,)), ((), ())), preferred_element_type=f32)


def window_row(i, j, shifted):
    if shifted:
        i, j = (i - SHIFT) % SIDE, (j - SHIFT) % SIDE
    return ((i // WIN) * (SIDE // WIN) + j // WIN) * CELL + (i % WIN) * WIN + j % WIN


def pieces(source, target):
    found = []
    for i in range(SIDE):
        for j in range(0, SIDE, SHIFT):
            row = [i * SIDE + j if o is None else window_row(i, j, o) for o in (source, target)]
            found.append(tuple(row))
    return found


def move_rows(source_ref, target_ref, source, target):
    for here, there in pieces(source, target):
        target_ref[there : there + SHIFT, :] = source_ref[here : here + SHIFT, :]


def lane_head(values, head):
    lane = lax.broadcasted_iota(jnp.int32, values.shape, 1)
    return jnp.where((lane >= HD * head) & (lane < HD * (head + 1)), values, jnp.zeros_like(values))


def head_stack(values):
    return jnp.concatenate([lane_head(values, head) for head in range(PER_TILE)], axis=0)


def head_pick(values):
    rows = values.shape[0] // PER_TILE
    total = None
    for head in range(PER_TILE):
        own = lane_head(values[head * rows : (head + 1) * rows], head)
        total = own if total is None else total + own
    return total


def staggered(items, stages):
    for tick in range(len(items) + len(stages) - 1):
        for number, stage in enumerate(stages):
            if 0 <= tick - number < len(items):
                stage(*items[tick - number])


def row_norm(values):
    center = values - jnp.mean(values, axis=-1, keepdims=True)
    scale = lax.rsqrt(jnp.mean(center * center, axis=-1, keepdims=True) + EPSILON)
    return center * scale, scale


def wide(ref, layer):
    return ref[layer : layer + 1, :].astype(f32)


def hot_rows(index_t, key):
    row = index_t[pl.ds(key, 1), :]
    low = jnp.broadcast_to(row & 127, (128, CELL))
    hot = (lax.broadcasted_iota(jnp.int32, (128, CELL), 0) == low).astype(f32).astype(bf16)
    return hot, row >> 7


def fill_index(index, index_t):
    index_t[...] = index[...].astype(f32).T.astype(jnp.int32)


def fill_bias(table, index_t, bias, rows, packed):
    heads, _, entries = table.shape
    groups = rows.shape[1] // 128
    rows[...] = jnp.zeros_like(rows)
    values = table[...].astype(f32)
    for layer in range(LAYERS):
        rows[layer * heads : (layer + 1) * heads, :entries] = values[:, layer, :]
    count = LAYERS * heads
    left = jnp.concatenate(
        [rows[:, group * 128 : (group + 1) * 128] for group in range(groups)], axis=0
    ).astype(bf16)

    def one(step, carry):
        for lane in range(UNROLL):
            key = step * UNROLL + lane
            hot, high = hot_rows(index_t, key)
            high = jnp.broadcast_to(high, (count, CELL))
            got = nn(left, hot)
            value = got[:count]
            for group in range(1, groups):
                value = jnp.where(high == group, got[group * count : (group + 1) * count], value)
            bias[:, pl.ds(key, 1), :] = (value * LOG2E).reshape(count, 1, CELL)
        return carry

    lax.fori_loop(0, CELL // UNROLL, one, 0)
    for first in range(0, count, PER_TILE):
        packed[first // PER_TILE] = jnp.concatenate(
            [bias[first + head] for head in range(PER_TILE)], axis=1
        )


def fill_mask(region, mask):
    values = region[...].astype(f32)
    count = SIDE // WIN
    for window in range(WINDOWS):
        first = (window // count) * WIN * SIDE + (window % count) * WIN
        row = jnp.concatenate(
            [values[:, first + i * SIDE : first + i * SIDE + WIN] for i in range(WIN)], axis=1
        )
        row = jnp.broadcast_to(row, (CELL, CELL))
        same = (row == row.T).astype(f32)
        mask[window] = jnp.concatenate([same] * PER_TILE, axis=1)


SAVED = ("h1", "n1", "r1", "qkv", "prob", "mix", "h2", "n2", "r2", "hid", "slope")


def saved_shapes(width, heads_width, hidden):
    heads = heads_width // HD
    return {
        "h1": ((ROWS, width), bf16),
        "n1": ((ROWS, width), bf16),
        "r1": ((ROWS, 1), f32),
        "qkv": ((3, ROWS, heads_width), bf16),
        "prob": ((WINDOWS, heads // PER_TILE, CELL, PER_TILE * CELL), bf16),
        "mix": ((ROWS, heads_width), bf16),
        "h2": ((ROWS, width), bf16),
        "n2": ((ROWS, width), bf16),
        "r2": ((ROWS, 1), f32),
        "hid": ((ROWS, hidden), bf16),
        "slope": ((ROWS, hidden), bf16),
    }


def forward_kernel(*refs):
    it = iter(refs)
    tokens, gain1, off1, qv_b, proj_b, gain2, off2, up_b, down_b = (next(it) for _ in range(9))
    table, index, region = (next(it) for _ in range(3))
    weights_hbm = [next(it) for _ in range(4)]
    middle_hbm = next(it)
    kept_hbm = {name: next(it) for name in SAVED}
    weights = [next(it) for _ in range(4)]
    kept = {name: next(it) for name in SAVED}
    x, y, send, recv, bias, packed, mask, index_t, table_rows = (next(it) for _ in range(9))
    weight_sem, kept_sem, row_sem, middle_sem, send_sem, recv_sem = (next(it) for _ in range(6))
    qkv_w, proj_w, up_w, down_w = weights
    heads_width = proj_w.shape[1]
    tiles = heads_width // LANES
    top = LAYERS - 1
    other = 1 - lax.axis_index("tensor")

    def load(slot, layer):
        return pltpu.make_async_copy(
            weights_hbm[slot].at[layer], weights[slot].at[layer], weight_sem.at[slot, layer]
        )

    def keep(name, layer):
        return pltpu.make_async_copy(
            kept[name].at[layer], kept_hbm[name].at[layer], kept_sem.at[SAVED.index(name), layer]
        )

    late = ("h2", "n2", "r2", "hid", "slope")

    def keep_rows(name, window):
        at = pl.ds(window * CELL, CELL)
        return pltpu.make_async_copy(
            kept[name].at[top, at], kept_hbm[name].at[top, at], row_sem.at[late.index(name), window]
        )

    def keep_middle(window):
        at = pl.ds(window * CELL, CELL)
        return pltpu.make_async_copy(x.at[at], middle_hbm.at[at], middle_sem.at[window])

    def swap(turn, window):
        return pltpu.make_async_remote_copy(
            src_ref=send.at[turn, window],
            dst_ref=recv.at[turn, window],
            send_sem=send_sem.at[turn, window],
            recv_sem=recv_sem.at[turn, window],
            device_id={"tensor": other},
            device_id_type=MESH_ID,
        )

    for layer in range(LAYERS):
        for slot in range(4 if layer < top else 3):
            load(slot, layer).start()
    barrier = pltpu.get_barrier_semaphore()
    pl.semaphore_signal(barrier, inc=1, device_id={"tensor": other}, device_id_type=MESH_ID)

    y[...] = tokens[...].astype(f32)
    move_rows(y, x, None, False)
    fill_index(index, index_t)
    fill_bias(table, index_t, bias, table_rows, packed)
    fill_mask(region, mask)

    for layer in range(LAYERS):
        load(0, layer).wait()
        load(1, layer).wait()
        if layer == 0:
            pl.semaphore_wait(barrier, 1)

        for window in range(WINDOWS):
            at = slice(window * CELL, (window + 1) * CELL)
            normed, scale = row_norm(x[at, :])
            h1 = (normed * wide(gain1, layer) + wide(off1, layer)).astype(bf16)
            kept["n1"][layer, at, :] = normed.astype(bf16)
            kept["r1"][layer, at, :] = scale
            kept["h1"][layer, at, :] = h1
            kept["qkv"][layer, 0, at, :] = (
                nn(h1, qkv_w[layer, 0]) + qv_b[layer, 0:1, :].astype(f32)
            ).astype(bf16)
            kept["qkv"][layer, 1, at, :] = nn(h1, qkv_w[layer, 1]).astype(bf16)
            kept["qkv"][layer, 2, at, :] = (
                nn(h1, qkv_w[layer, 2]) + qv_b[layer, 1:2, :].astype(f32)
            ).astype(bf16)
        for name in ("h1", "n1", "r1", "qkv"):
            keep(name, layer).start()

        scores, probs = {}, {}

        def operand(slot, window, tile):
            at = slice(window * CELL, (window + 1) * CELL)
            return kept["qkv"][layer, slot, at, tile * LANES : (tile + 1) * LANES]

        def score(window, tile):
            scores[window, tile] = nt(operand(1, window, tile), head_stack(operand(0, window, tile)))

        def soften(window, tile):
            s = scores.pop((window, tile)) * (SCALE * LOG2E) + packed[layer * tiles + tile]
            if layer == 1:
                s = jnp.where(mask[window] > 0.5, s, -1000000000.0 * LOG2E)
            e = jnp.exp2(s - jnp.max(s, axis=0, keepdims=True))
            prob = (e * (1.0 / jnp.sum(e, axis=0, keepdims=True))).astype(bf16)
            kept["prob"][layer, window, tile] = prob
            probs[window, tile] = prob

        def mix(window, tile):
            at = slice(window * CELL, (window + 1) * CELL)
            value = head_pick(tn(probs.pop((window, tile)), operand(2, window, tile)))
            kept["mix"][layer, at, tile * LANES : (tile + 1) * LANES] = value.astype(bf16)
            if tile == tiles - 1:
                send[2 * layer, window] = nn(kept["mix"][layer, at, :], proj_w[layer]).astype(bf16)
                swap(2 * layer, window).start()

        staggered(
            [(window, tile) for window in range(WINDOWS) for tile in range(tiles)],
            (score, soften, mix),
        )
        for name in ("prob", "mix"):
            keep(name, layer).start()
        load(2, layer).wait()
        if layer < top:
            load(3, layer).wait()

        def join(window):
            at = slice(window * CELL, (window + 1) * CELL)
            swap(2 * layer, window).wait_recv()
            total = send[2 * layer, window].astype(f32) + recv[2 * layer, window].astype(f32)
            middle = x[at, :] + total + wide(proj_b, layer)
            x[at, :] = middle
            normed, scale = row_norm(middle)
            kept["n2"][layer, at, :] = normed.astype(bf16)
            kept["r2"][layer, at, :] = scale
            kept["h2"][layer, at, :] = (normed * wide(gain2, layer) + wide(off2, layer)).astype(bf16)
            if layer == top:
                keep_middle(window).start()
                for name in late[:3]:
                    keep_rows(name, window).start()

        def expand(window):
            at = slice(window * CELL, (window + 1) * CELL)
            u = nn(kept["h2"][layer, at, :], up_w[layer]) + wide(up_b, layer)
            phi = 0.5 + 0.5 * lax.erf(u * 0.7071067811865476)
            kept["slope"][layer, at, :] = (
                phi + u * jnp.exp(u * u * -0.5) * 0.3989422804014327
            ).astype(bf16)
            kept["hid"][layer, at, :] = (u * phi).astype(bf16)
            if layer == top:
                for name in late[3:]:
                    keep_rows(name, window).start()

        def shrink(window):
            at = slice(window * CELL, (window + 1) * CELL)
            send[2 * layer + 1, window] = nn(kept["hid"][layer, at, :], down_w[layer]).astype(bf16)
            swap(2 * layer + 1, window).start()

        every = [(window,) for window in range(WINDOWS)]
        if layer == top:
            staggered(every, (join, expand))
            continue
        staggered(every, (join, expand, shrink))
        for name in late:
            keep(name, layer).start()
        for window in range(WINDOWS):
            at = slice(window * CELL, (window + 1) * CELL)
            swap(2 * layer + 1, window).wait_recv()
            total = send[2 * layer + 1, window].astype(f32) + recv[2 * layer + 1, window].astype(f32)
            y[at, :] = x[at, :] + total + wide(down_b, layer)
        move_rows(y, x, False, True)

    for turn in range(2 * LAYERS - 1):
        for window in range(WINDOWS):
            swap(turn, window).wait_send()
    for layer in range(LAYERS):
        for name in SAVED:
            if layer < top or name not in late:
                keep(name, layer).wait()
    for window in range(WINDOWS):
        keep_middle(window).wait()
        for name in late:
            keep_rows(name, window).wait()


def run_forward(tokens, vectors, tables, weights):
    width = tokens.shape[1]
    heads_width = weights[1].shape[1]
    heads = heads_width // HD
    entries = -(-tables[0].shape[2] // 128) * 128
    hidden = weights[2].shape[2]
    shapes = saved_shapes(width, heads_width, hidden)
    vmem = pl.BlockSpec(memory_space=pltpu.VMEM)
    hbm = pl.BlockSpec(memory_space=pl.ANY)
    kept = [jax.ShapeDtypeStruct((LAYERS,) + shapes[name][0], shapes[name][1]) for name in SAVED]
    swaps = (2 * LAYERS - 1, WINDOWS)
    outs = pl.pallas_call(
        forward_kernel,
        out_shape=[jax.ShapeDtypeStruct((ROWS, width), f32)] + kept,
        in_specs=[vmem] * 12 + [hbm] * 4,
        out_specs=[hbm] * (1 + len(SAVED)),
        scratch_shapes=[pltpu.VMEM(w.shape, bf16) for w in weights]
        + [pltpu.VMEM(s.shape, s.dtype) for s in kept]
        + [
            pltpu.VMEM((ROWS, width), f32),
            pltpu.VMEM((ROWS, width), f32),
            pltpu.VMEM(swaps + (CELL, width), bf16),
            pltpu.VMEM(swaps + (CELL, width), bf16),
            pltpu.VMEM((LAYERS * heads, CELL, CELL), f32),
            pltpu.VMEM((LAYERS * heads // PER_TILE, CELL, PER_TILE * CELL), f32),
            pltpu.VMEM((WINDOWS, CELL, PER_TILE * CELL), f32),
            pltpu.VMEM((CELL, CELL), jnp.int32),
            pltpu.VMEM((LAYERS * heads, entries), f32),
            pltpu.SemaphoreType.DMA((4, LAYERS)),
            pltpu.SemaphoreType.DMA((len(SAVED), LAYERS)),
            pltpu.SemaphoreType.DMA((5, WINDOWS)),
            pltpu.SemaphoreType.DMA((WINDOWS,)),
            pltpu.SemaphoreType.DMA(swaps),
            pltpu.SemaphoreType.DMA(swaps),
        ],
        compiler_params=pltpu.CompilerParams(
            collective_id=0, has_side_effects=True, vmem_limit_bytes=VMEM_LIMIT
        ),
        name="forward",
    )(tokens, *vectors, *tables, *weights)
    return outs[0], dict(zip(SAVED, outs[1:]))


BITS = 4
X_FIRST = (3, 2, 1, 0)
Y_FIRST = (2, 3, 1, 0)
Z_FIRST = (1, 0, 3, 2)
PARTS = ((1, 1, 1, 1), (1, 1, 1, 1), (1,), (1, 1, 1))
ORDERS = (
    (3, 1, 2, 0),
    (1, 3, 2, 0),
    (2, 3, 1, 0),
    (3, 2, 1, 0),
    (2, 3, 1, 0),
    (3, 1, 2, 0),
    (3, 2, 1, 0),
    (1, 2, 3, 0),
    (2, 3, 1, 0),
    (2, 3, 1, 0),
    (2, 3, 1, 0),
    (1, 0, 3, 2),
)
VECTOR_ROWS = 24
HALVES = 2
START = 100
VECTORS = 99

SCHEDULE = (
    (112,),
    (113,),
    (114,),
    (),
    (),
    (115,),
    (116,),
    (),
    (),
    (119,),
    (),
    (),
    (117,),
    (120, 13, 12, 112),
    (14,),
    (),
    (),
    (),
    (),
    (),
    (113,),
    (123, 15),
    (121, 16, 19),
    (),
    (114,),
    (12,),
    (101,),
    (),
    (118,),
    (119, 20, 17),
    (13, 117),
    (122,),
    (23, 123),
    (),
    (),
    (105, 14),
    (21,),
    (114,),
    (),
    (112, 19),
    (),
    (119, 108, 107, 1),
    (18,),
    (121,),
    (),
    (23,),
    (),
    (),
    (101, 22, 17),
    (118, 111, 12, 112, 14, 114),
    (122, 117, 19, 119, 5),
    (100, 115, 21),
    (12, 8, 14, 102, 7, 105, 1, 19, 18, 17, 117, 22, 122, 15, 106, 104, 115, 11, 111, 17, 121, 0, 5, 100, 2, 102, 105, 99, 22, 122, 15, 120, 109, 118, 115, 11, 4, 116, 6, 22, 21, 121, 5, 105, 2, 103, 102, 15, 0, 100, 99, 21, 106, 20, 120, 18, 118, 5, 2, 108, 110, 102, 16, 116, 9, 0, 104, 100, 18, 99, 2, 20, 109, 113, 120, 6, 106, 3, 16, 103, 116, 0, 8, 123, 108, 10, 110, 107, 4, 104, 6, 106, 13, 101, 113, 99, 9, 109, 20, 8, 108, 3, 103, 23, 111, 123, 16, 6, 4, 104, 7, 107, 10, 110, 13, 1, 101, 23, 8, 9, 109, 11, 111, 3, 103, 4, 7, 107, 1, 10, 110, 11, 9, 3, 7, 10),
)
REL_ROW = 9


def chunk_widths(unit):
    return [unit * count for group in PARTS for count in group]


def norm_back(grad, normed, scale, gain):
    c = grad * gain
    inner = c - jnp.mean(c, axis=-1, keepdims=True)
    return scale * (inner - normed * jnp.mean(c * normed, axis=-1, keepdims=True))


def column_sum(values):
    return jnp.sum(values, axis=0, keepdims=True)


def backward_kernel(shift, *refs):
    it = iter(refs)

    def take(count):
        return [next(it) for _ in range(count)]

    cot, valid, gain1, gain2, down_b, index = take(6)
    middle_hbm = take(1)[0]
    weights_hbm = take(4)
    kept_hbm = dict(zip(SAVED, take(len(SAVED))))
    output_hbm, input_grad_hbm, reduced_hbm, vectors_out = take(4)
    weights = take(4)
    kept = dict(zip(SAVED, take(len(SAVED))))
    chunks = len(ORDERS)
    grads = [take(chunks) for _ in range(LAYERS)]
    landed = [take(BITS) for _ in range(chunks)]
    dy, low, pre, send, recv, grad_mix, grad_qkv, grad_bias, table, vectors, vectors_in, index_t, grad_score = take(13)
    out, reduced, last_send, last_recv = take(4)
    weight_sem, kept_sem, send_sem, recv_sem = take(4)
    chunk_send, chunk_recv, credit, vector_send, vector_recv = take(5)
    last_send_sem, last_recv_sem, row_sem, chunk_out = take(4)
    qkv_w, proj_w, up_w, down_w = weights
    heads_width = proj_w.shape[0]
    hidden = up_w.shape[1]
    width = dy.shape[1]
    heads = heads_width // HD
    tiles = heads_width // LANES
    part = width >> BITS
    widths = chunk_widths(heads_width)

    me = lax.axis_index("dp")
    other = 1 - lax.axis_index("tensor")
    places = [1 << (shift + BITS - 1 - dim) for dim in range(BITS)]
    mine = [lax.rem(lax.div(me, place), 2) for place in places]
    partner = [me + place - 2 * place * bit for place, bit in zip(places, mine)]

    def load(slot, layer):
        return pltpu.make_async_copy(weights_hbm[slot].at[layer], weights[slot], weight_sem.at[slot])

    def fetch(name, layer):
        return pltpu.make_async_copy(
            kept_hbm[name].at[layer], kept[name], kept_sem.at[SAVED.index(name)]
        )

    def swap(turn, half):
        return pltpu.make_async_remote_copy(
            src_ref=send.at[turn % 2, half],
            dst_ref=recv.at[turn % 2, half],
            send_sem=send_sem.at[turn, half],
            recv_sem=recv_sem.at[turn, half],
            device_id={"tensor": other},
            device_id_type=MESH_ID,
        )

    def last_swap(half):
        return pltpu.make_async_remote_copy(
            src_ref=last_send.at[half],
            dst_ref=last_recv.at[half],
            send_sem=last_send_sem.at[half],
            recv_sem=last_recv_sem.at[half],
            device_id={"tensor": other},
            device_id_type=MESH_ID,
        )

    step = {}

    def region(chunk, phase, bit):
        order = ORDERS[chunk]
        index = [slice(None)] * BITS
        for dim in order[:phase]:
            index[dim] = mine[dim]
        index[order[phase]] = bit
        return tuple(index)

    def chunk_copy(layer, chunk, phase):
        dim = ORDERS[chunk][phase]
        return pltpu.make_async_remote_copy(
            src_ref=grads[layer][chunk].at[region(chunk, phase, 1 - mine[dim])],
            dst_ref=landed[chunk][phase],
            send_sem=chunk_send.at[layer, chunk, phase],
            recv_sem=chunk_recv.at[layer, chunk, phase],
            device_id={"dp": partner[dim]},
            device_id_type=MESH_ID,
        )

    def chunk_result(layer, chunk):
        cols = pl.ds(sum(widths[:chunk]), widths[chunk])
        return pltpu.make_async_copy(
            reduced.at[layer, :, cols], reduced_hbm.at[layer, :, cols], chunk_out.at[layer, chunk]
        )

    def begin(layer, chunk):
        if layer < LAYERS - 1:
            pl.semaphore_wait(credit.at[chunk, step[layer, chunk]], 1)
        chunk_copy(layer, chunk, step[layer, chunk]).start()

    def advance(layer, chunk):
        phase = step[layer, chunk]
        dim = ORDERS[chunk][phase]
        chunk_copy(layer, chunk, phase).wait()
        keep = region(chunk, phase, mine[dim])
        free = [d for d in range(BITS) if isinstance(keep[d], slice)]
        ref, arrived = grads[layer][chunk], landed[chunk][phase]
        first = sum(widths[:chunk])
        for number in range(1 << len(free)):
            bits = [(number >> (len(free) - 1 - n)) & 1 for n in range(len(free))]
            index = list(keep)
            for d, bit in zip(free, bits):
                index[d] = bit
            here = ref[tuple(index)]
            there = arrived[tuple(bits)] if bits else arrived[...]
            if phase < BITS - 1:
                ref[tuple(index)] = here + there
            else:
                reduced[layer, :, first : first + widths[chunk]] = here.astype(f32) + there.astype(f32)
                chunk_result(layer, chunk).start()
        if layer == LAYERS - 1:
            pl.semaphore_signal(
                credit.at[chunk, phase], inc=1, device_id={"dp": partner[dim]}, device_id_type=MESH_ID
            )
        step[layer, chunk] = phase + 1

    entered = []

    def finish_chunk(layer, chunk, left, right):
        half = width // 2
        for top in range(2):
            value = tn(left[:, top * half : (top + 1) * half], right)
            grads[layer][chunk][top] = value.astype(bf16).reshape(2, 2, 2, part, widths[chunk])
        step[layer, chunk] = 0
        if not entered:
            pl.semaphore_wait(barrier, 1 + BITS)
            entered.append(True)
        point()

    def finish_group(layer, group, left, right):
        chunk = sum(len(counts) for counts in PARTS[:group])
        first = 0
        for size in PARTS[group]:
            size *= heads_width
            finish_chunk(layer, chunk, left, right[:, first : first + size])
            first += size
            chunk += 1

    place = iter(SCHEDULE)

    def point():
        for action in next(place):
            if action == VECTORS:
                vector_step()
                continue
            chosen = divmod(action % START, chunks)
            if action >= START:
                begin(*chosen)
            else:
                advance(*chosen)

    def vector_copy(phase):
        return pltpu.make_async_remote_copy(
            src_ref=vectors.at[phase],
            dst_ref=vectors_in.at[phase],
            send_sem=vector_send.at[phase],
            recv_sem=vector_recv.at[phase],
            device_id={"dp": partner[BITS - 1 - phase]},
            device_id_type=MESH_ID,
        )

    rounds = iter(range(BITS))

    def vector_step():
        phase = next(rounds)
        vector_copy(phase).wait()
        total = vectors[phase] + vectors_in[phase]
        if phase < BITS - 1:
            vectors[phase + 1] = total
            vector_copy(phase + 1).start()
        else:
            vectors_out[...] = total

    top = LAYERS - 1
    fetch("hid", top).start()
    barrier = pltpu.get_barrier_semaphore()
    pl.semaphore_signal(barrier, inc=1, device_id={"tensor": other}, device_id_type=MESH_ID)
    for dim in range(BITS):
        pl.semaphore_signal(barrier, inc=1, device_id={"dp": partner[dim]}, device_id_type=MESH_ID)

    out[...] = cot[...].astype(f32) * valid[0].astype(f32)
    move_rows(out, dy, None, True)
    vectors[0] = jnp.zeros(vectors.shape[1:], f32)

    def rows_of(part_index, count):
        size = ROWS // count
        return slice(part_index * size, (part_index + 1) * size)

    for layer in reversed(range(LAYERS)):
        turn = 2 * (LAYERS - 1 - layer)

        def add_row(row, value, first=0):
            cols = slice(first, first + value.shape[1])
            vectors[0, layer, row : row + 1, cols] += value

        def free(*names):
            for name in names if layer > 0 else ():
                fetch(name, layer - 1).start()

        def free_weight(slot):
            if layer > 0:
                load(slot, layer - 1).start()

        low[...] = dy[...].astype(bf16)
        fetch("hid", layer).wait()
        if layer == top:
            load(3, top).start()
            fetch("slope", top).start()
            load(2, top).start()
        finish_group(layer, 0, low[...], kept["hid"])
        add_row(5, column_sum(dy[...]))
        load(3, layer).wait()
        if layer == top:
            for half in range(HALVES):
                rows = kept["hid"][rows_of(half, HALVES), :]
                last_send[half] = nn(rows, down_w[...]).astype(bf16)
                last_swap(half).start()
        free("hid")
        fetch("slope", layer).wait()
        load(2, layer).wait()
        if layer == top:
            for name in ("h2", "n2", "r2", "mix"):
                fetch(name, top).start()
            load(1, top).start()
            for name in ("prob", "qkv"):
                fetch(name, top).start()
        for half in range(HALVES):
            at = rows_of(half, HALVES)
            grad = nt(low[at, :], down_w[...]) * kept["slope"][at, :].astype(f32)
            add_row(7, column_sum(grad[:, :width]))
            add_row(8, column_sum(grad[:, width:]))
            pre[at, :] = grad.astype(bf16)
            send[turn % 2, half] = nt(pre[at, :], up_w[...]).astype(bf16)
            swap(turn, half).start()
            point()
        free("slope")
        free_weight(3)
        free_weight(2)
        fetch("h2", layer).wait()
        finish_group(layer, 1, kept["h2"][...], pre)
        free("h2")
        for name in ("n2", "r2", "mix"):
            fetch(name, layer).wait()
        load(1, layer).wait()
        for half in range(HALVES):
            at = rows_of(half, HALVES)
            swap(turn, half).wait_recv()
            grad = send[turn % 2, half].astype(f32) + recv[turn % 2, half].astype(f32)
            normed = kept["n2"][at, :].astype(f32)
            add_row(3, column_sum(grad * normed))
            add_row(4, column_sum(grad))
            total = dy[at, :] + norm_back(grad, normed, kept["r2"][at, :], wide(gain2, layer))
            dy[at, :] = total
            add_row(2, column_sum(total))
            low[at, :] = total.astype(bf16)
            grad_mix[at, :] = nt(low[at, :], proj_w[...]).astype(bf16)
            point()
        free("n2", "r2")
        free_weight(1)
        finish_group(layer, 2, low[...], kept["mix"])
        free("mix")

        fetch("prob", layer).wait()
        fetch("qkv", layer).wait()
        if layer == top:
            load(0, top).start()
            for name in ("h1", "n1", "r1"):
                fetch(name, top).start()
        stacks, drops, lows = {}, {}, {}

        def operand(ref, window, tile):
            return ref[rows_of(window, WINDOWS), tile * LANES : (tile + 1) * LANES]

        def pull(window, tile):
            stacks[window, tile] = head_stack(operand(grad_mix, window, tile))
            drops[window, tile] = nt(operand(kept["qkv"].at[2], window, tile), stacks[window, tile])

        def harden(window, tile):
            prob = kept["prob"][window, tile].astype(f32)
            weighted = prob * drops.pop((window, tile))
            value = weighted - prob * column_sum(weighted)
            if window == 0:
                grad_score[tile] = value
            else:
                grad_score[tile] += value
            lows[window, tile] = value.astype(bf16)

        def split(window, tile):
            value = lows.pop((window, tile))
            grad_v = nn(kept["prob"][window, tile], stacks.pop((window, tile)))
            grad_k = nn(value, head_stack(operand(kept["qkv"].at[0], window, tile))) * SCALE
            grad_q = head_pick(tn(value, operand(kept["qkv"].at[1], window, tile))) * SCALE
            for slot, part_grad in enumerate((grad_q, grad_k, grad_v)):
                grad_qkv[slot, rows_of(window, WINDOWS), tile * LANES : (tile + 1) * LANES] = (
                    part_grad.astype(bf16)
                )
            add_row(6, column_sum(grad_q), tile * LANES)
            add_row(6, column_sum(grad_v), heads_width + tile * LANES)
            if tile == tiles - 1:
                point()

        staggered(
            [(window, tile) for window in range(WINDOWS) for tile in range(tiles)],
            (pull, harden, split),
        )
        for head in range(heads):
            lane = head % PER_TILE * CELL
            grad_bias[layer * heads + head] = grad_score[head // PER_TILE, :, lane : lane + CELL]
        free("prob", "qkv")
        load(0, layer).wait()
        for half in range(HALVES):
            at = rows_of(half, HALVES)
            total = nt(grad_qkv[0, at, :], qkv_w[0])
            total = total + nt(grad_qkv[1, at, :], qkv_w[1])
            total = total + nt(grad_qkv[2, at, :], qkv_w[2])
            send[(turn + 1) % 2, half] = total.astype(bf16)
            swap(turn + 1, half).start()
            point()
        free_weight(0)
        fetch("h1", layer).wait()
        for place_index, slot in enumerate((2, 0, 1)):
            finish_chunk(layer, chunks - 3 + place_index, kept["h1"][...], grad_qkv[slot])
        free("h1")
        fetch("n1", layer).wait()
        fetch("r1", layer).wait()
        for half in range(HALVES):
            at = rows_of(half, HALVES)
            swap(turn + 1, half).wait_recv()
            grad = send[(turn + 1) % 2, half].astype(f32) + recv[(turn + 1) % 2, half].astype(f32)
            normed = kept["n1"][at, :].astype(f32)
            add_row(0, column_sum(grad * normed))
            add_row(1, column_sum(grad))
            out[at, :] = dy[at, :] + norm_back(grad, normed, kept["r1"][at, :], wide(gain1, layer))
            point()
        free("n1", "r1")
        for half in range(HALVES):
            swap(turn, half).wait_send()
            swap(turn + 1, half).wait_send()
        if layer > 0:
            move_rows(out, dy, True, False)
        point()

    def write(source, target, number):
        return pltpu.make_async_copy(source, target, row_sem.at[number])

    fill_index(index, index_t)
    table[...] = jnp.zeros_like(table)
    groups = table.shape[0] // (LAYERS * heads)

    def scatter(step_index, carry):
        total = None
        for lane in range(UNROLL):
            key = step_index * UNROLL + lane
            hot, high = hot_rows(index_t, key)
            score = grad_bias[:, pl.ds(key, 1), :].reshape(LAYERS * heads, CELL)
            high = jnp.broadcast_to(high, score.shape)
            left = jnp.concatenate(
                [jnp.where(high == group, score, 0.0) for group in range(groups)], axis=0
            ).astype(bf16)
            value = nt(left, hot)
            total = value if total is None else total + value
        table[...] += total
        return carry

    steps = CELL // UNROLL
    for quarter in range(2):
        lax.fori_loop(quarter * steps // 2, (quarter + 1) * steps // 2, scatter, 0)
        if quarter == 0:
            move_rows(out, dy, False, None)
            write(dy, input_grad_hbm, 0).start()
            write(middle_hbm, out, 1).start()
        point()
    for layer in range(LAYERS):
        for group in range(groups):
            first = (group * LAYERS + layer) * heads
            vectors[0, layer, REL_ROW : REL_ROW + heads, group * 128 : (group + 1) * 128] = table[
                first : first + heads, :
            ]
    vector_copy(0).start()
    write(middle_hbm, out, 1).wait()
    for half in range(HALVES):
        last_swap(half).wait()

    def join(half, carry):
        at = pl.ds(pl.multiple_of(half * (ROWS // HALVES), 8), ROWS // HALVES)
        out[at, :] += last_send[half].astype(f32) + last_recv[half].astype(f32) + wide(down_b, top)
        return carry

    lax.fori_loop(0, HALVES, join, 0)
    write(dy, input_grad_hbm, 0).wait()
    move_rows(out, dy, True, None)
    write(dy, output_hbm, 2).start()
    point()
    for layer in range(LAYERS):
        for chunk in range(chunks):
            chunk_result(layer, chunk).wait()
    write(dy, output_hbm, 2).wait()


def run_backward(shift, entries, cot, valid, gain1, gain2, down_b, index, middle, weights, kept):
    width = cot.shape[1]
    heads_width = weights[1].shape[1]
    hidden = weights[2].shape[2]
    heads = heads_width // HD
    rows = -(-entries // 128) * 128
    part = width >> BITS
    widths = chunk_widths(heads_width)
    shapes = saved_shapes(width, heads_width, hidden)
    vmem = pl.BlockSpec(memory_space=pltpu.VMEM)
    hbm = pl.BlockSpec(memory_space=pl.ANY)
    smem = pl.BlockSpec(memory_space=pltpu.SMEM)
    grads = [pltpu.VMEM((2,) * BITS + (part, w), bf16) for w in widths] * LAYERS
    landed = [
        pltpu.VMEM((2,) * (BITS - 1 - phase) + (part, w), bf16) for w in widths for phase in range(BITS)
    ]
    swaps = (2, HALVES, ROWS // HALVES, width)
    rounds = (2 * LAYERS, HALVES)
    vectors = (LAYERS, VECTOR_ROWS, width)
    chunk_rounds = (LAYERS, len(widths), BITS)
    return pl.pallas_call(
        functools.partial(backward_kernel, shift),
        out_shape=(
            jax.ShapeDtypeStruct((ROWS, width), f32),
            jax.ShapeDtypeStruct((ROWS, width), f32),
            jax.ShapeDtypeStruct((LAYERS, part, sum(widths)), f32),
            jax.ShapeDtypeStruct(vectors, f32),
        ),
        in_specs=[vmem, smem, vmem, vmem, vmem, vmem] + [hbm] * (5 + len(SAVED)),
        out_specs=(hbm, hbm, hbm, vmem),
        scratch_shapes=[pltpu.VMEM(w.shape[1:], bf16) for w in weights]
        + [pltpu.VMEM(shapes[name][0], shapes[name][1]) for name in SAVED]
        + grads
        + landed
        + [
            pltpu.VMEM((ROWS, width), f32),
            pltpu.VMEM((ROWS, width), bf16),
            pltpu.VMEM((ROWS, hidden), bf16),
            pltpu.VMEM(swaps, bf16),
            pltpu.VMEM(swaps, bf16),
            pltpu.VMEM((ROWS, heads_width), bf16),
            pltpu.VMEM((3, ROWS, heads_width), bf16),
            pltpu.VMEM((LAYERS * heads, CELL, CELL), f32),
            pltpu.VMEM((rows // 128 * LAYERS * heads, 128), f32),
            pltpu.VMEM((BITS,) + vectors, f32),
            pltpu.VMEM((BITS,) + vectors, f32),
            pltpu.VMEM((CELL, CELL), jnp.int32),
            pltpu.VMEM((heads // PER_TILE, CELL, PER_TILE * CELL), f32),
            pltpu.VMEM((ROWS, width), f32),
            pltpu.VMEM((LAYERS, part, sum(widths)), f32),
            pltpu.VMEM(swaps[1:], bf16),
            pltpu.VMEM(swaps[1:], bf16),
            pltpu.SemaphoreType.DMA((4,)),
            pltpu.SemaphoreType.DMA((len(SAVED),)),
            pltpu.SemaphoreType.DMA(rounds),
            pltpu.SemaphoreType.DMA(rounds),
            pltpu.SemaphoreType.DMA(chunk_rounds),
            pltpu.SemaphoreType.DMA(chunk_rounds),
            pltpu.SemaphoreType.REGULAR(chunk_rounds[1:]),
            pltpu.SemaphoreType.DMA((BITS,)),
            pltpu.SemaphoreType.DMA((BITS,)),
            pltpu.SemaphoreType.DMA((HALVES,)),
            pltpu.SemaphoreType.DMA((HALVES,)),
            pltpu.SemaphoreType.DMA((3,)),
            pltpu.SemaphoreType.DMA(chunk_rounds[:2]),
        ],
        compiler_params=pltpu.CompilerParams(
            collective_id=1, has_side_effects=True, vmem_limit_bytes=VMEM_LIMIT
        ),
        name="backward",
    )(cot, valid, gain1, gain2, down_b, index, middle, *weights, *[kept[name] for name in SAVED])


def result_kernel(x, dx, reduced, vectors, *outs):
    (output, input_grad, g1, o1, qkv_g, qv_g, rel_g, proj_g, pb_g, g2, o2, up_g, ub_g, down_g, db_g) = outs
    hidden = up_g.shape[2]
    heads_width = proj_g.shape[2]
    width = g1.shape[1]
    heads, _, entries = rel_g.shape
    output[...] = x[...]
    input_grad[...] = dx[...]
    for layer in range(LAYERS):
        first = 0
        for target, size in (
            (down_g.at[layer], hidden),
            (up_g.at[layer], hidden),
            (proj_g.at[layer], heads_width),
            (qkv_g.at[layer, 2], heads_width),
            (qkv_g.at[layer, 0], heads_width),
            (qkv_g.at[layer, 1], heads_width),
        ):
            target[...] = reduced[layer, :, first : first + size]
            first += size
        row = slice(layer, layer + 1)
        for number, ref in enumerate((g1, o1, pb_g, g2, o2, db_g)):
            ref[row, :] = vectors[layer, number : number + 1, :]
        qv_g[layer, 0:1, :] = vectors[layer, 6:7, :heads_width]
        qv_g[layer, 1:2, :] = vectors[layer, 6:7, heads_width:]
        ub_g[row, :width] = vectors[layer, 7:8, :]
        ub_g[row, width:] = vectors[layer, 8:9, :]
        rel_g[:, layer, :] = vectors[layer, REL_ROW : REL_ROW + heads, :entries]


def per_device(
    tokens,
    region_ids,
    rel_index,
    valid,
    ln1_gain,
    ln1_bias,
    qkv_weight,
    qv_bias,
    rel_table,
    proj_weight,
    proj_bias,
    ln2_gain,
    ln2_bias,
    fc1_weight,
    fc1_bias,
    fc2_weight,
    fc2_bias,
    cotangent,
):
    devices = lax.axis_size("dp")
    group = devices >> BITS
    shift = group.bit_length() - 1
    width = tokens.shape[1]
    heads_width = proj_weight.shape[1]
    hidden = fc1_weight.shape[2]
    tables = (rel_table.transpose(2, 0, 1), rel_index, region_ids.reshape(1, ROWS))
    weights = (qkv_weight, proj_weight, fc1_weight, fc2_weight)
    vectors = (ln1_gain, ln1_bias, qv_bias, proj_bias, ln2_gain, ln2_bias, fc1_bias, fc2_bias)
    middle, kept = run_forward(tokens, vectors, tables, weights)
    x, dx, reduced, sums = run_backward(
        shift,
        rel_table.shape[1],
        cotangent,
        valid,
        ln1_gain,
        ln2_gain,
        fc2_bias,
        rel_index,
        middle,
        weights,
        kept,
    )
    if group > 1:
        sets = [list(range(first, first + group)) for first in range(0, devices, group)]
        reduced = lax.psum_scatter(
            reduced, "dp", scatter_dimension=1, axis_index_groups=sets, tiled=True
        )
        sums = lax.psum(sums, "dp", axis_index_groups=sets)
    part = width // devices
    shapes = (
        (ROWS, width),
        (ROWS, width),
        (LAYERS, width),
        (LAYERS, width),
        (LAYERS, 3, part, heads_width),
        (LAYERS, 2, heads_width),
        tables[0].shape,
        (LAYERS, part, heads_width),
        (LAYERS, width),
        (LAYERS, width),
        (LAYERS, width),
        (LAYERS, part, hidden),
        (LAYERS, hidden),
        (LAYERS, part, hidden),
        (LAYERS, width),
    )
    vmem = pl.BlockSpec(memory_space=pltpu.VMEM)
    outs = list(
        pl.pallas_call(
            result_kernel,
            out_shape=[jax.ShapeDtypeStruct(shape, f32) for shape in shapes],
            in_specs=[vmem] * 4,
            out_specs=[vmem] * len(shapes),
            compiler_params=pltpu.CompilerParams(vmem_limit_bytes=VMEM_LIMIT),
            name="results",
        )(x, dx, reduced, sums)
    )
    outs[6] = outs[6].transpose(1, 2, 0)
    outs[7] = outs[7].transpose(0, 2, 1)
    outs[13] = outs[13].transpose(0, 2, 1)
    return tuple(outs)


def solution(mesh):
    return jax.shard_map(
        per_device,
        mesh=mesh,
        in_specs=(
            P("dp", None),
            P(),
            P(),
            P("dp"),
            P(),
            P(),
            P(None, None, None, "tensor"),
            P(None, None, "tensor"),
            P(None, None, "tensor"),
            P(None, "tensor", None),
            P(),
            P(),
            P(),
            P(None, None, "tensor"),
            P(None, "tensor"),
            P(None, "tensor", None),
            P(),
            P("dp", None),
        ),
        out_specs=(
            P("dp", None),
            P("dp", None),
            P(),
            P(),
            P(None, None, "dp", "tensor"),
            P(None, None, "tensor"),
            P(None, None, "tensor"),
            P(None, "tensor", "dp"),
            P(),
            P(),
            P(),
            P(None, "dp", "tensor"),
            P(None, "tensor"),
            P(None, "tensor", "dp"),
            P(),
        ),
        check_vma=False,
    )
```

```python
import functools

import jax
import jax.numpy as jnp
from jax import lax
from jax.experimental import pallas as pl
from jax.experimental.pallas import tpu as pltpu
from jax.sharding import PartitionSpec as P

HD = 32
WIN = 12
SIDE = 24
LAYERS = 2
SHIFT = 6
ROWS = SIDE * SIDE
CELL = WIN * WIN
WINDOWS = ROWS // CELL
PER_TILE = 4
LANES = PER_TILE * HD
EPSILON = 1e-05
UNROLL = 8
LOG2E = 1.4426950408889634
SCALE = HD**-0.5
VMEM_LIMIT = 62 * 1024 * 1024
MESH_ID = pl.DeviceIdType.MESH

f32 = jnp.float32
bf16 = jnp.bfloat16


def nn(a, b):
    return jnp.dot(a, b, preferred_element_type=f32)


def nt(a, b):
    return lax.dot_general(a, b, (((1,), (1,)), ((), ())), preferred_element_type=f32)


def tn(a, b):
    return lax.dot_general(a, b, (((0,), (0,)), ((), ())), preferred_element_type=f32)


def window_row(i, j, shifted):
    if shifted:
        i, j = (i - SHIFT) % SIDE, (j - SHIFT) % SIDE
    return ((i // WIN) * (SIDE // WIN) + j // WIN) * CELL + (i % WIN) * WIN + j % WIN


def pieces(source, target):
    found = []
    for i in range(SIDE):
        for j in range(0, SIDE, SHIFT):
            row = [i * SIDE + j if o is None else window_row(i, j, o) for o in (source, target)]
            found.append(tuple(row))
    return found


def move_rows(source_ref, target_ref, source, target):
    for here, there in pieces(source, target):
        target_ref[there : there + SHIFT, :] = source_ref[here : here + SHIFT, :]


def lane_head(values, head):
    lane = lax.broadcasted_iota(jnp.int32, values.shape, 1)
    return jnp.where((lane >= HD * head) & (lane < HD * (head + 1)), values, jnp.zeros_like(values))


def head_stack(values):
    return jnp.concatenate([lane_head(values, head) for head in range(PER_TILE)], axis=0)


def head_pick(values):
    rows = values.shape[0] // PER_TILE
    total = None
    for head in range(PER_TILE):
        own = lane_head(values[head * rows : (head + 1) * rows], head)
        total = own if total is None else total + own
    return total


def staggered(items, stages):
    for tick in range(len(items) + len(stages) - 1):
        for number, stage in enumerate(stages):
            if 0 <= tick - number < len(items):
                stage(*items[tick - number])


def row_norm(values):
    center = values - jnp.mean(values, axis=-1, keepdims=True)
    scale = lax.rsqrt(jnp.mean(center * center, axis=-1, keepdims=True) + EPSILON)
    return center * scale, scale


def wide(ref, layer):
    return ref[layer : layer + 1, :].astype(f32)


def hot_rows(index_t, key):
    row = index_t[pl.ds(key, 1), :]
    low = jnp.broadcast_to(row & 127, (128, CELL))
    hot = (lax.broadcasted_iota(jnp.int32, (128, CELL), 0) == low).astype(f32).astype(bf16)
    return hot, row >> 7


def fill_index(index, index_t):
    index_t[...] = index[...].astype(f32).T.astype(jnp.int32)


def fill_bias(table, index_t, bias, rows, packed):
    heads, _, entries = table.shape
    groups = rows.shape[1] // 128
    rows[...] = jnp.zeros_like(rows)
    values = table[...].astype(f32)
    for layer in range(LAYERS):
        rows[layer * heads : (layer + 1) * heads, :entries] = values[:, layer, :]
    count = LAYERS * heads
    left = jnp.concatenate(
        [rows[:, group * 128 : (group + 1) * 128] for group in range(groups)], axis=0
    ).astype(bf16)

    def one(step, carry):
        for lane in range(UNROLL):
            key = step * UNROLL + lane
            hot, high = hot_rows(index_t, key)
            high = jnp.broadcast_to(high, (count, CELL))
            got = nn(left, hot)
            value = got[:count]
            for group in range(1, groups):
                value = jnp.where(high == group, got[group * count : (group + 1) * count], value)
            bias[:, pl.ds(key, 1), :] = (value * LOG2E).reshape(count, 1, CELL)
        return carry

    lax.fori_loop(0, CELL // UNROLL, one, 0)
    for first in range(0, count, PER_TILE):
        packed[first // PER_TILE] = jnp.concatenate(
            [bias[first + head] for head in range(PER_TILE)], axis=1
        )


def fill_mask(region, mask):
    values = region[...].astype(f32).reshape(1, ROWS)
    count = SIDE // WIN
    for window in range(WINDOWS):
        first = (window // count) * WIN * SIDE + (window % count) * WIN
        row = jnp.concatenate(
            [values[:, first + i * SIDE : first + i * SIDE + WIN] for i in range(WIN)], axis=1
        )
        row = jnp.broadcast_to(row, (CELL, CELL))
        same = (row == row.T).astype(f32)
        mask[window] = jnp.concatenate([same] * PER_TILE, axis=1).astype(bf16)


SAVED = ("h1", "n1", "r1", "qkv", "prob", "mix", "h2", "n2", "r2", "hid", "slope")


def saved_shapes(width, heads_width, hidden):
    heads = heads_width // HD
    return {
        "h1": ((ROWS, width), bf16),
        "n1": ((ROWS, width), bf16),
        "r1": ((ROWS, 1), f32),
        "qkv": ((3, ROWS, heads_width), bf16),
        "prob": ((WINDOWS, heads // PER_TILE, CELL, PER_TILE * CELL), bf16),
        "mix": ((ROWS, heads_width), bf16),
        "h2": ((ROWS, width), bf16),
        "n2": ((ROWS, width), bf16),
        "r2": ((ROWS, 1), f32),
        "hid": ((ROWS, hidden), bf16),
        "slope": ((ROWS, hidden), bf16),
    }


BITS = 4
X_FIRST = (3, 2, 1, 0)
Y_FIRST = (2, 3, 1, 0)
Z_FIRST = (1, 0, 3, 2)
PARTS = ((1, 1, 1, 1), (1, 1, 1, 1), (1,), (1, 1, 1))
ORDERS = (
    (3, 1, 2, 0),
    (1, 3, 2, 0),
    (2, 3, 1, 0),
    (3, 2, 1, 0),
    (2, 3, 1, 0),
    (3, 1, 2, 0),
    (3, 2, 1, 0),
    (1, 2, 3, 0),
    (2, 3, 1, 0),
    (2, 3, 1, 0),
    (2, 3, 1, 0),
    (1, 0, 3, 2),
)
VECTOR_ROWS = 24
HALVES = 2
START = 100
VECTORS = 99

SCHEDULE = (
    (112,),
    (113,),
    (114,),
    (),
    (),
    (115,),
    (116,),
    (),
    (),
    (119,),
    (),
    (),
    (117,),
    (120, 13, 12, 112),
    (14,),
    (),
    (),
    (),
    (),
    (),
    (113,),
    (123, 15),
    (121, 16, 19),
    (),
    (114,),
    (12,),
    (101,),
    (),
    (118,),
    (119, 20, 17),
    (13, 117),
    (122,),
    (23, 123),
    (),
    (),
    (105, 14),
    (21,),
    (114,),
    (),
    (112, 19),
    (),
    (119, 108, 107, 1),
    (18,),
    (121,),
    (),
    (23,),
    (),
    (),
    (101, 22, 17),
    (118, 111, 12, 112, 14, 114),
    (122, 117, 19, 119, 5),
    (100, 115, 21),
    (12, 8, 14, 102, 7, 105, 1, 19, 18, 17, 117, 22, 122, 15, 106, 104, 115, 11, 111, 17, 121, 0, 5, 100, 2, 102, 105, 99, 22, 122, 15, 120, 109, 118, 115, 11, 4, 116, 6, 22, 21, 121, 5, 105, 2, 103, 102, 15, 0, 100, 99, 21, 106, 20, 120, 18, 118, 5, 2, 108, 110, 102, 16, 116, 9, 0, 104, 100, 18, 99, 2, 20, 109, 113, 120, 6, 106, 3, 16, 103, 116, 0, 8, 123, 108, 10, 110, 107, 4, 104, 6, 106, 13, 101, 113, 99, 9, 109, 20, 8, 108, 3, 103, 23, 111, 123, 16, 6, 4, 104, 7, 107, 10, 110, 13, 1, 101, 23, 8, 9, 109, 11, 111, 3, 103, 4, 7, 107, 1, 10, 110, 11, 9, 3, 7, 10),
)
REL_ROW = 9


def chunk_widths(unit):
    return [unit * count for group in PARTS for count in group]


def norm_back(grad, normed, scale, gain):
    c = grad * gain
    inner = c - jnp.mean(c, axis=-1, keepdims=True)
    return scale * (inner - normed * jnp.mean(c * normed, axis=-1, keepdims=True))


def column_sum(values):
    return jnp.sum(values, axis=0, keepdims=True)


def step_kernel(shift, *refs):
    it = iter(refs)

    def take(count):
        return [next(it) for _ in range(count)]

    tokens_hbm, cot_hbm, valid = take(3)
    gain1, off1, qv_b, proj_b, gain2, off2, up_b, down_b = take(8)
    table_in, index, region_ids = take(3)
    weights_hbm = take(4)
    output_hbm, input_grad_hbm, reduced_hbm, vectors_out = take(4)
    kept_hbm = dict(zip(SAVED, take(len(SAVED))))
    weights = take(4)
    kept = dict(zip(SAVED, take(len(SAVED))))
    chunks = sum(len(counts) for counts in PARTS)
    grads = [take(chunks) for _ in range(LAYERS)]
    landed = [take(BITS) for _ in range(chunks)]
    x, dy, out, low, send, recv, grad_mix, grad_qkv = take(8)
    bias, packed, mask, index_t, table_rows, grad_score, table = take(7)
    vectors, vectors_in, reduced = take(3)
    weight_sem, kept_sem, fetch_sem, send_sem, recv_sem = take(5)
    chunk_send, chunk_recv, credit, vector_send, vector_recv, row_sem, chunk_out = take(7)
    grad_bias = bias
    qkv_w, proj_w, up_w, down_w = weights
    heads_width = proj_w.shape[0]
    hidden = up_w.shape[1]
    width = dy.shape[1]
    heads = heads_width // HD
    tiles = heads_width // LANES
    part = width >> BITS
    widths = chunk_widths(heads_width)

    me = lax.axis_index("dp")
    other = 1 - lax.axis_index("tensor")
    places = [1 << (shift + BITS - 1 - dim) for dim in range(BITS)]
    mine = [lax.rem(lax.div(me, place), 2) for place in places]
    partner = [me + place - 2 * place * bit for place, bit in zip(places, mine)]

    top = LAYERS - 1

    def load(slot, layer):
        return pltpu.make_async_copy(weights_hbm[slot].at[layer], weights[slot], weight_sem.at[slot])

    def keep(name):
        return pltpu.make_async_copy(kept[name], kept_hbm[name], kept_sem.at[SAVED.index(name)])

    def fetch(name):
        return pltpu.make_async_copy(kept_hbm[name], kept[name], fetch_sem.at[SAVED.index(name)])

    def write(source, target, number):
        return pltpu.make_async_copy(source, target, row_sem.at[number])

    def swap(turn, first, count):
        at = pl.ds(first, count)
        return pltpu.make_async_remote_copy(
            src_ref=send.at[turn % 2, at],
            dst_ref=recv.at[turn % 2, at],
            send_sem=send_sem.at[turn, first],
            recv_sem=recv_sem.at[turn, first],
            device_id={"tensor": other},
            device_id_type=MESH_ID,
        )

    def give(turn, first, value):
        count = value.shape[0] // CELL
        for number in range(count):
            send[turn % 2, first + number] = value[number * CELL : (number + 1) * CELL].astype(bf16)
        swap(turn, first, count).start()

    def gather(turn, first, count):
        swap(turn, first, count).wait()
        parts = [
            send[turn % 2, first + number].astype(f32) + recv[turn % 2, first + number].astype(f32)
            for number in range(count)
        ]
        return parts[0] if count == 1 else jnp.concatenate(parts, axis=0)

    def rows_of(part_index, count):
        size = ROWS // count
        return slice(part_index * size, (part_index + 1) * size)

    step = {}

    def region(chunk, phase, bit):
        order = ORDERS[chunk]
        index = [slice(None)] * BITS
        for dim in order[:phase]:
            index[dim] = mine[dim]
        index[order[phase]] = bit
        return tuple(index)

    def chunk_copy(layer, chunk, phase):
        dim = ORDERS[chunk][phase]
        return pltpu.make_async_remote_copy(
            src_ref=grads[layer][chunk].at[region(chunk, phase, 1 - mine[dim])],
            dst_ref=landed[chunk][phase],
            send_sem=chunk_send.at[layer, chunk, phase],
            recv_sem=chunk_recv.at[layer, chunk, phase],
            device_id={"dp": partner[dim]},
            device_id_type=MESH_ID,
        )

    def chunk_result(layer, chunk):
        cols = pl.ds(sum(widths[:chunk]), widths[chunk])
        return pltpu.make_async_copy(
            reduced.at[layer, :, cols], reduced_hbm.at[layer, :, cols], chunk_out.at[layer, chunk]
        )

    def begin(layer, chunk):
        if layer < LAYERS - 1:
            pl.semaphore_wait(credit.at[chunk, step[layer, chunk]], 1)
        chunk_copy(layer, chunk, step[layer, chunk]).start()

    def advance(layer, chunk):
        phase = step[layer, chunk]
        dim = ORDERS[chunk][phase]
        chunk_copy(layer, chunk, phase).wait()
        keep = region(chunk, phase, mine[dim])
        free = [d for d in range(BITS) if isinstance(keep[d], slice)]
        ref, arrived = grads[layer][chunk], landed[chunk][phase]
        first = sum(widths[:chunk])
        for number in range(1 << len(free)):
            bits = [(number >> (len(free) - 1 - n)) & 1 for n in range(len(free))]
            index = list(keep)
            for d, bit in zip(free, bits):
                index[d] = bit
            here = ref[tuple(index)]
            there = arrived[tuple(bits)] if bits else arrived[...]
            if phase < BITS - 1:
                ref[tuple(index)] = here + there
            else:
                reduced[layer, :, first : first + widths[chunk]] = here.astype(f32) + there.astype(f32)
                chunk_result(layer, chunk).start()
        if layer == LAYERS - 1:
            pl.semaphore_signal(
                credit.at[chunk, phase], inc=1, device_id={"dp": partner[dim]}, device_id_type=MESH_ID
            )
        step[layer, chunk] = phase + 1

    def finish_chunk(layer, chunk, left, right):
        half = width // 2
        for top in range(2):
            value = tn(left[:, top * half : (top + 1) * half], right)
            grads[layer][chunk][top] = value.astype(bf16).reshape(2, 2, 2, part, widths[chunk])
        step[layer, chunk] = 0
        point()

    def finish_group(layer, group, left, right):
        chunk = sum(len(counts) for counts in PARTS[:group])
        first = 0
        for size in PARTS[group]:
            size *= heads_width
            finish_chunk(layer, chunk, left, right[:, first : first + size])
            first += size
            chunk += 1

    place = iter(SCHEDULE)

    def point():
        for action in next(place):
            if action == VECTORS:
                vector_step()
                continue
            chosen = divmod(action % START, chunks)
            if action >= START:
                begin(*chosen)
            else:
                advance(*chosen)

    def vector_copy(phase):
        return pltpu.make_async_remote_copy(
            src_ref=vectors.at[phase],
            dst_ref=vectors_in.at[phase],
            send_sem=vector_send.at[phase],
            recv_sem=vector_recv.at[phase],
            device_id={"dp": partner[BITS - 1 - phase]},
            device_id_type=MESH_ID,
        )

    rounds = iter(range(BITS))

    def vector_step():
        phase = next(rounds)
        vector_copy(phase).wait()
        total = vectors[phase] + vectors_in[phase]
        if phase < BITS - 1:
            vectors[phase + 1] = total
            vector_copy(phase + 1).start()
        else:
            vectors_out[...] = total

    write(tokens_hbm, kept["h2"], 0).start()
    write(cot_hbm, low, 1).start()
    for slot in range(4):
        load(slot, 0).start()
    barrier = pltpu.get_barrier_semaphore()
    pl.semaphore_signal(barrier, inc=1, device_id={"tensor": other}, device_id_type=MESH_ID)
    for dim in range(BITS):
        pl.semaphore_signal(barrier, inc=1, device_id={"dp": partner[dim]}, device_id_type=MESH_ID)
    fill_index(index, index_t)
    fill_bias(table_in, index_t, bias, table_rows, packed)
    fill_mask(region_ids, mask)
    vectors[0] = jnp.zeros(vectors.shape[1:], f32)
    write(tokens_hbm, kept["h2"], 0).wait()
    dy[...] = kept["h2"][...].astype(f32)
    move_rows(dy, x, None, False)
    pl.semaphore_wait(barrier, 1 + BITS)

    early, late = SAVED[:4], SAVED[6:]
    half_windows = WINDOWS // HALVES
    every = [(window,) for window in range(WINDOWS)]
    pairs = [(window, tile) for window in range(WINDOWS) for tile in range(tiles)]

    for layer in range(LAYERS):
        load(0, layer).wait()
        for name in early if layer > 0 else ():
            keep(name).wait()
        for window in range(WINDOWS):
            at = rows_of(window, WINDOWS)
            normed, scale = row_norm(x[at, :])
            h1 = (normed * wide(gain1, layer) + wide(off1, layer)).astype(bf16)
            kept["n1"][at, :] = normed.astype(bf16)
            kept["r1"][at, :] = scale
            kept["h1"][at, :] = h1
            kept["qkv"][0, at, :] = (nn(h1, qkv_w[0]) + qv_b[layer, 0:1, :].astype(f32)).astype(bf16)
            kept["qkv"][1, at, :] = nn(h1, qkv_w[1]).astype(bf16)
            kept["qkv"][2, at, :] = (nn(h1, qkv_w[2]) + qv_b[layer, 1:2, :].astype(f32)).astype(bf16)
        if layer < top:
            load(0, layer + 1).start()
            for name in early:
                keep(name).start()
        load(1, layer).wait()
        for name in SAVED[4:6] if layer > 0 else ():
            keep(name).wait()

        scores, probs = {}, {}

        def operand(slot, window, tile):
            return kept["qkv"][slot, rows_of(window, WINDOWS), tile * LANES : (tile + 1) * LANES]

        def score(window, tile):
            scores[window, tile] = nt(operand(1, window, tile), head_stack(operand(0, window, tile)))

        def soften(window, tile):
            s = scores.pop((window, tile)) * (SCALE * LOG2E) + packed[layer * tiles + tile]
            if layer == 1:
                s = jnp.where(mask[window].astype(f32) > 0.5, s, -1000000000.0 * LOG2E)
            e = jnp.exp2(s - jnp.max(s, axis=0, keepdims=True))
            prob = (e * (1.0 / jnp.sum(e, axis=0, keepdims=True))).astype(bf16)
            kept["prob"][window, tile] = prob
            probs[window, tile] = prob

        def mix(window, tile):
            at = rows_of(window, WINDOWS)
            value = head_pick(tn(probs.pop((window, tile)), operand(2, window, tile)))
            kept["mix"][at, tile * LANES : (tile + 1) * LANES] = value.astype(bf16)
            if tile == tiles - 1:
                give(2 * layer, window, nn(kept["mix"][at, :], proj_w[...]))

        staggered(pairs, (score, soften, mix))
        if layer < top:
            load(1, layer + 1).start()
            for name in SAVED[4:6]:
                keep(name).start()
        load(2, layer).wait()
        if layer < top:
            load(3, layer).wait()
        for name in late if layer > 0 else ():
            keep(name).wait()

        def join(window):
            at = rows_of(window, WINDOWS)
            middle = x[at, :] + gather(2 * layer, window, 1) + wide(proj_b, layer)
            x[at, :] = middle
            normed, scale = row_norm(middle)
            kept["n2"][at, :] = normed.astype(bf16)
            kept["r2"][at, :] = scale
            kept["h2"][at, :] = (normed * wide(gain2, layer) + wide(off2, layer)).astype(bf16)

        def expand(window):
            at = rows_of(window, WINDOWS)
            u = nn(kept["h2"][at, :], up_w[...]) + wide(up_b, layer)
            phi = 0.5 + 0.5 * lax.erf(u * 0.7071067811865476)
            kept["slope"][at, :] = (phi + u * jnp.exp(u * u * -0.5) * 0.3989422804014327).astype(bf16)
            kept["hid"][at, :] = (u * phi).astype(bf16)

        def shrink(window):
            give(2 * layer + 1, window, nn(kept["hid"][rows_of(window, WINDOWS), :], down_w[...]))

        if layer == top:
            staggered(every, (join, expand))
            continue
        staggered(every, (join, expand, shrink))
        for slot in (2, 3):
            load(slot, layer + 1).start()
        for name in late:
            keep(name).start()
        write(cot_hbm, low, 1).wait()
        out[...] = low[...].astype(f32) * valid[0].astype(f32)
        move_rows(out, dy, None, True)
        low[...] = dy[...].astype(bf16)
        for window in range(WINDOWS):
            at = rows_of(window, WINDOWS)
            out[at, :] = x[at, :] + gather(2 * layer + 1, window, 1) + wide(down_b, layer)
        move_rows(out, x, False, True)

    for layer in reversed(range(LAYERS)):
        turn = 2 * LAYERS + 2 * (LAYERS - 1 - layer)

        def add_row(row, value, first=0):
            cols = slice(first, first + value.shape[1])
            vectors[0, layer, row : row + 1, cols] += value

        def free(*names):
            for name in names if layer > 0 else ():
                fetch(name).start()

        def free_weight(slot):
            if layer > 0:
                load(slot, layer - 1).start()

        def ready(*names):
            for name in names if layer < top else ():
                fetch(name).wait()

        if layer < top:
            low[...] = dy[...].astype(bf16)
        ready("hid")
        finish_group(layer, 0, low[...], kept["hid"])
        add_row(5, column_sum(dy[...]))
        load(3, layer).wait()
        if layer == top:
            for half in range(HALVES):
                give(turn - 1, half * half_windows, nn(kept["hid"][rows_of(half, HALVES), :], down_w[...]))
        free("hid")
        ready("slope")
        if layer < top:
            load(2, layer).wait()
        for half in range(HALVES):
            at = rows_of(half, HALVES)
            grad = nt(low[at, :], down_w[...]) * kept["slope"][at, :].astype(f32)
            add_row(7, column_sum(grad[:, :width]))
            add_row(8, column_sum(grad[:, width:]))
            kept["slope"][at, :] = grad.astype(bf16)
            if layer == top and half == 0:
                for number in range(HALVES):
                    rows = rows_of(number, HALVES)
                    total = gather(turn - 1, number * half_windows, half_windows)
                    x[rows, :] = x[rows, :] + total + wide(down_b, top)
            give(turn, half * half_windows, nt(kept["slope"][at, :], up_w[...]))
            point()
        free_weight(3)
        free_weight(2)
        ready("h2")
        finish_group(layer, 1, kept["h2"][...], kept["slope"])
        free("h2", "slope")
        ready("n2", "r2", "mix")
        if layer < top:
            load(1, layer).wait()
        for half in range(HALVES):
            at = rows_of(half, HALVES)
            grad = gather(turn, half * half_windows, half_windows)
            normed = kept["n2"][at, :].astype(f32)
            add_row(3, column_sum(grad * normed))
            add_row(4, column_sum(grad))
            total = dy[at, :] + norm_back(grad, normed, kept["r2"][at, :], wide(gain2, layer))
            dy[at, :] = total
            add_row(2, column_sum(total))
            low[at, :] = total.astype(bf16)
            grad_mix[at, :] = nt(low[at, :], proj_w[...]).astype(bf16)
            point()
        free("n2", "r2")
        free_weight(1)
        finish_group(layer, 2, low[...], kept["mix"])
        free("mix")

        ready("prob", "qkv")
        stacks, drops, lows = {}, {}, {}

        def operand(ref, window, tile):
            return ref[rows_of(window, WINDOWS), tile * LANES : (tile + 1) * LANES]

        def pull(window, tile):
            stacks[window, tile] = head_stack(operand(grad_mix, window, tile))
            drops[window, tile] = nt(operand(kept["qkv"].at[2], window, tile), stacks[window, tile])

        def harden(window, tile):
            prob = kept["prob"][window, tile].astype(f32)
            weighted = prob * drops.pop((window, tile))
            value = weighted - prob * column_sum(weighted)
            if window == 0:
                grad_score[tile] = value
            else:
                grad_score[tile] += value
            lows[window, tile] = value.astype(bf16)

        def split(window, tile):
            value = lows.pop((window, tile))
            grad_v = nn(kept["prob"][window, tile], stacks.pop((window, tile)))
            grad_k = nn(value, head_stack(operand(kept["qkv"].at[0], window, tile))) * SCALE
            grad_q = head_pick(tn(value, operand(kept["qkv"].at[1], window, tile))) * SCALE
            for slot, part_grad in enumerate((grad_q, grad_k, grad_v)):
                grad_qkv[slot, rows_of(window, WINDOWS), tile * LANES : (tile + 1) * LANES] = (
                    part_grad.astype(bf16)
                )
            add_row(6, column_sum(grad_q), tile * LANES)
            add_row(6, column_sum(grad_v), heads_width + tile * LANES)
            if tile == tiles - 1:
                point()

        staggered(pairs, (pull, harden, split))
        for head in range(heads):
            lane = head % PER_TILE * CELL
            grad_bias[layer * heads + head] = grad_score[head // PER_TILE, :, lane : lane + CELL]
        free("prob", "qkv")
        if layer < top:
            load(0, layer).wait()
        for half in range(HALVES):
            at = rows_of(half, HALVES)
            total = nt(grad_qkv[0, at, :], qkv_w[0])
            total = total + nt(grad_qkv[1, at, :], qkv_w[1])
            total = total + nt(grad_qkv[2, at, :], qkv_w[2])
            give(turn + 1, half * half_windows, total)
            point()
        free_weight(0)
        ready("h1")
        for place_index, slot in enumerate((2, 0, 1)):
            finish_chunk(layer, chunks - 3 + place_index, kept["h1"][...], grad_qkv[slot])
        free("h1")
        ready("n1", "r1")
        for half in range(HALVES):
            at = rows_of(half, HALVES)
            grad = gather(turn + 1, half * half_windows, half_windows)
            normed = kept["n1"][at, :].astype(f32)
            add_row(0, column_sum(grad * normed))
            add_row(1, column_sum(grad))
            out[at, :] = dy[at, :] + norm_back(grad, normed, kept["r1"][at, :], wide(gain1, layer))
            point()
        free("n1", "r1")
        if layer > 0:
            move_rows(out, dy, True, False)
        point()

    table[...] = jnp.zeros_like(table)
    groups = table.shape[0] // (LAYERS * heads)

    def scatter(step_index, carry):
        total = None
        for lane in range(UNROLL):
            key = step_index * UNROLL + lane
            hot, high = hot_rows(index_t, key)
            score = grad_bias[:, pl.ds(key, 1), :].reshape(LAYERS * heads, CELL)
            high = jnp.broadcast_to(high, score.shape)
            left = jnp.concatenate(
                [jnp.where(high == group, score, 0.0) for group in range(groups)], axis=0
            ).astype(bf16)
            value = nt(left, hot)
            total = value if total is None else total + value
        table[...] += total
        return carry

    steps = CELL // UNROLL
    for quarter in range(2):
        lax.fori_loop(quarter * steps // 2, (quarter + 1) * steps // 2, scatter, 0)
        if quarter == 0:
            move_rows(out, dy, False, None)
            write(dy, input_grad_hbm, 0).start()
        else:
            move_rows(x, out, True, None)
            write(out, output_hbm, 1).start()
        point()
    for layer in range(LAYERS):
        for group in range(groups):
            first = (group * LAYERS + layer) * heads
            vectors[0, layer, REL_ROW : REL_ROW + heads, group * 128 : (group + 1) * 128] = table[
                first : first + heads, :
            ]
    vector_copy(0).start()
    point()
    for layer in range(LAYERS):
        for chunk in range(chunks):
            chunk_result(layer, chunk).wait()
    write(dy, input_grad_hbm, 0).wait()
    write(out, output_hbm, 1).wait()


def run_step(shift, tokens, cot, valid, vectors, tables, weights):
    width = cot.shape[1]
    heads_width = weights[1].shape[1]
    hidden = weights[2].shape[2]
    heads = heads_width // HD
    tiles = heads_width // LANES
    entries = -(-tables[0].shape[2] // 128) * 128
    part = width >> BITS
    widths = chunk_widths(heads_width)
    shapes = saved_shapes(width, heads_width, hidden)
    vmem = pl.BlockSpec(memory_space=pltpu.VMEM)
    hbm = pl.BlockSpec(memory_space=pl.ANY)
    smem = pl.BlockSpec(memory_space=pltpu.SMEM)
    grads = [pltpu.VMEM((2,) * BITS + (part, w), bf16) for w in widths] * LAYERS
    landed = [
        pltpu.VMEM((2,) * (BITS - 1 - phase) + (part, w), bf16) for w in widths for phase in range(BITS)
    ]
    swaps = (2, WINDOWS, CELL, width)
    rounds = (4 * LAYERS, WINDOWS)
    sums = (LAYERS, VECTOR_ROWS, width)
    chunk_rounds = (LAYERS, len(widths), BITS)
    reduced = (LAYERS, part, sum(widths))
    outs = pl.pallas_call(
        functools.partial(step_kernel, shift),
        out_shape=[
            jax.ShapeDtypeStruct((ROWS, width), f32),
            jax.ShapeDtypeStruct((ROWS, width), f32),
            jax.ShapeDtypeStruct(reduced, f32),
            jax.ShapeDtypeStruct(sums, f32),
        ]
        + [jax.ShapeDtypeStruct(*shapes[name]) for name in SAVED],
        in_specs=[hbm, hbm, smem] + [vmem] * 11 + [hbm] * 4,
        out_specs=[hbm, hbm, hbm, vmem] + [hbm] * len(SAVED),
        scratch_shapes=[pltpu.VMEM(w.shape[1:], bf16) for w in weights]
        + [pltpu.VMEM(*shapes[name]) for name in SAVED]
        + grads
        + landed
        + [
            pltpu.VMEM((ROWS, width), f32),
            pltpu.VMEM((ROWS, width), f32),
            pltpu.VMEM((ROWS, width), f32),
            pltpu.VMEM((ROWS, width), bf16),
            pltpu.VMEM(swaps, bf16),
            pltpu.VMEM(swaps, bf16),
            pltpu.VMEM((ROWS, heads_width), bf16),
            pltpu.VMEM((3, ROWS, heads_width), bf16),
            pltpu.VMEM((LAYERS * heads, CELL, CELL), f32),
            pltpu.VMEM((LAYERS * tiles, CELL, PER_TILE * CELL), f32),
            pltpu.VMEM((WINDOWS, CELL, PER_TILE * CELL), bf16),
            pltpu.VMEM((CELL, CELL), jnp.int32),
            pltpu.VMEM((LAYERS * heads, entries), f32),
            pltpu.VMEM((tiles, CELL, PER_TILE * CELL), f32),
            pltpu.VMEM((entries // 128 * LAYERS * heads, 128), f32),
            pltpu.VMEM((BITS,) + sums, f32),
            pltpu.VMEM((BITS,) + sums, f32),
            pltpu.VMEM(reduced, f32),
            pltpu.SemaphoreType.DMA((4,)),
            pltpu.SemaphoreType.DMA((len(SAVED),)),
            pltpu.SemaphoreType.DMA((len(SAVED),)),
            pltpu.SemaphoreType.DMA(rounds),
            pltpu.SemaphoreType.DMA(rounds),
            pltpu.SemaphoreType.DMA(chunk_rounds),
            pltpu.SemaphoreType.DMA(chunk_rounds),
            pltpu.SemaphoreType.REGULAR(chunk_rounds[1:]),
            pltpu.SemaphoreType.DMA((BITS,)),
            pltpu.SemaphoreType.DMA((BITS,)),
            pltpu.SemaphoreType.DMA((2,)),
            pltpu.SemaphoreType.DMA(chunk_rounds[:2]),
        ],
        compiler_params=pltpu.CompilerParams(
            collective_id=0, has_side_effects=True, vmem_limit_bytes=VMEM_LIMIT
        ),
        name="step",
    )(tokens, cot, valid, *vectors, *tables, *weights)
    return outs[:4]


def result_kernel(x, dx, reduced, vectors, *outs):
    (output, input_grad, g1, o1, qkv_g, qv_g, rel_g, proj_g, pb_g, g2, o2, up_g, ub_g, down_g, db_g) = outs
    hidden = up_g.shape[2]
    heads_width = proj_g.shape[2]
    width = g1.shape[1]
    heads, _, entries = rel_g.shape
    output[...] = x[...]
    input_grad[...] = dx[...]
    for layer in range(LAYERS):
        first = 0
        for target, size in (
            (down_g.at[layer], hidden),
            (up_g.at[layer], hidden),
            (proj_g.at[layer], heads_width),
            (qkv_g.at[layer, 2], heads_width),
            (qkv_g.at[layer, 0], heads_width),
            (qkv_g.at[layer, 1], heads_width),
        ):
            target[...] = reduced[layer, :, first : first + size]
            first += size
        row = slice(layer, layer + 1)
        for number, ref in enumerate((g1, o1, pb_g, g2, o2, db_g)):
            ref[row, :] = vectors[layer, number : number + 1, :]
        qv_g[layer, 0:1, :] = vectors[layer, 6:7, :heads_width]
        qv_g[layer, 1:2, :] = vectors[layer, 6:7, heads_width:]
        ub_g[row, :width] = vectors[layer, 7:8, :]
        ub_g[row, width:] = vectors[layer, 8:9, :]
        rel_g[:, layer, :] = vectors[layer, REL_ROW : REL_ROW + heads, :entries]


def per_device(
    tokens,
    region_ids,
    rel_index,
    valid,
    ln1_gain,
    ln1_bias,
    qkv_weight,
    qv_bias,
    rel_table,
    proj_weight,
    proj_bias,
    ln2_gain,
    ln2_bias,
    fc1_weight,
    fc1_bias,
    fc2_weight,
    fc2_bias,
    cotangent,
):
    devices = lax.axis_size("dp")
    group = devices >> BITS
    shift = group.bit_length() - 1
    width = tokens.shape[1]
    heads_width = proj_weight.shape[1]
    hidden = fc1_weight.shape[2]
    tables = (rel_table.transpose(2, 0, 1), rel_index, region_ids)
    weights = (qkv_weight, proj_weight, fc1_weight, fc2_weight)
    vectors = (ln1_gain, ln1_bias, qv_bias, proj_bias, ln2_gain, ln2_bias, fc1_bias, fc2_bias)
    x, dx, reduced, sums = run_step(shift, tokens, cotangent, valid, vectors, tables, weights)
    if group > 1:
        sets = [list(range(first, first + group)) for first in range(0, devices, group)]
        reduced = lax.psum_scatter(
            reduced, "dp", scatter_dimension=1, axis_index_groups=sets, tiled=True
        )
        sums = lax.psum(sums, "dp", axis_index_groups=sets)
    part = width // devices
    shapes = (
        (ROWS, width),
        (ROWS, width),
        (LAYERS, width),
        (LAYERS, width),
        (LAYERS, 3, part, heads_width),
        (LAYERS, 2, heads_width),
        tables[0].shape,
        (LAYERS, part, heads_width),
        (LAYERS, width),
        (LAYERS, width),
        (LAYERS, width),
        (LAYERS, part, hidden),
        (LAYERS, hidden),
        (LAYERS, part, hidden),
        (LAYERS, width),
    )
    vmem = pl.BlockSpec(memory_space=pltpu.VMEM)
    outs = list(
        pl.pallas_call(
            result_kernel,
            out_shape=[jax.ShapeDtypeStruct(shape, f32) for shape in shapes],
            in_specs=[vmem] * 4,
            out_specs=[vmem] * len(shapes),
            compiler_params=pltpu.CompilerParams(vmem_limit_bytes=VMEM_LIMIT),
            name="results",
        )(x, dx, reduced, sums)
    )
    outs[6] = outs[6].transpose(1, 2, 0)
    outs[7] = outs[7].transpose(0, 2, 1)
    outs[13] = outs[13].transpose(0, 2, 1)
    return tuple(outs)


def solution(mesh):
    return jax.shard_map(
        per_device,
        mesh=mesh,
        in_specs=(
            P("dp", None),
            P(),
            P(),
            P("dp"),
            P(),
            P(),
            P(None, None, None, "tensor"),
            P(None, None, "tensor"),
            P(None, None, "tensor"),
            P(None, "tensor", None),
            P(),
            P(),
            P(),
            P(None, None, "tensor"),
            P(None, "tensor"),
            P(None, "tensor", None),
            P(),
            P("dp", None),
        ),
        out_specs=(
            P("dp", None),
            P("dp", None),
            P(),
            P(),
            P(None, None, "dp", "tensor"),
            P(None, None, "tensor"),
            P(None, None, "tensor"),
            P(None, "tensor", "dp"),
            P(),
            P(),
            P(),
            P(None, "dp", "tensor"),
            P(None, "tensor"),
            P(None, "tensor", "dp"),
            P(),
        ),
        check_vma=False,
    )
```

```python
import functools

import jax
import jax.numpy as jnp
from jax import lax
from jax.experimental import pallas as pl
from jax.experimental.pallas import tpu as pltpu
from jax.sharding import PartitionSpec as P

HD = 32
WIN = 12
SIDE = 24
LAYERS = 2
SHIFT = 6
ROWS = SIDE * SIDE
CELL = WIN * WIN
WINDOWS = ROWS // CELL
PER_TILE = 4
LANES = PER_TILE * HD
EPSILON = 1e-05
UNROLL = 16
FILL = 48
LOG2E = 1.4426950408889634
SCALE = HD**-0.5
VMEM_LIMIT = 62 * 1024 * 1024
MESH_ID = pl.DeviceIdType.MESH

f32 = jnp.float32
bf16 = jnp.bfloat16


def nn(a, b):
    return jnp.dot(a, b, preferred_element_type=f32)


def nt(a, b):
    return lax.dot_general(a, b, (((1,), (1,)), ((), ())), preferred_element_type=f32)


def tn(a, b):
    return lax.dot_general(a, b, (((0,), (0,)), ((), ())), preferred_element_type=f32)


def window_row(i, j, shifted):
    if shifted:
        i, j = (i - SHIFT) % SIDE, (j - SHIFT) % SIDE
    return ((i // WIN) * (SIDE // WIN) + j // WIN) * CELL + (i % WIN) * WIN + j % WIN


def pieces(source, target):
    found = []
    for i in range(SIDE):
        for j in range(0, SIDE, SHIFT):
            row = [i * SIDE + j if o is None else window_row(i, j, o) for o in (source, target)]
            found.append(tuple(row))
    return found


def move_rows(source_ref, target_ref, source, target):
    for here, there in pieces(source, target):
        target_ref[there : there + SHIFT, :] = source_ref[here : here + SHIFT, :]


def lane_head(values, head):
    lane = lax.broadcasted_iota(jnp.int32, values.shape, 1)
    return jnp.where((lane >= HD * head) & (lane < HD * (head + 1)), values, jnp.zeros_like(values))


def head_stack(values):
    return jnp.concatenate([lane_head(values, head) for head in range(PER_TILE)], axis=0)


def head_pick(values):
    rows = values.shape[0] // PER_TILE
    total = None
    for head in range(PER_TILE):
        own = lane_head(values[head * rows : (head + 1) * rows], head)
        total = own if total is None else total + own
    return total


def staggered(items, stages):
    for tick in range(len(items) + len(stages) - 1):
        for number, stage in enumerate(stages):
            if 0 <= tick - number < len(items):
                stage(*items[tick - number])


def row_norm(values):
    center = values - jnp.mean(values, axis=-1, keepdims=True)
    scale = lax.rsqrt(jnp.mean(center * center, axis=-1, keepdims=True) + EPSILON)
    return center * scale, scale


def wide(ref, layer):
    return ref[layer : layer + 1, :].astype(f32)


def hot_rows(index_t, key):
    row = index_t[pl.ds(key, 1), :]
    low = jnp.broadcast_to((row & 127).astype(f32).astype(bf16), (128, CELL))
    entry = lax.broadcasted_iota(jnp.int32, (128, CELL), 0).astype(f32).astype(bf16)
    return jnp.where(entry == low, jnp.ones((), bf16), jnp.zeros((), bf16)), row >> 7


def fill_index(index, index_t):
    index_t[...] = index[...].astype(f32).T.astype(jnp.int32)


def fill_bias(table, index_t, bias, rows, packed):
    heads, _, entries = table.shape
    groups = rows.shape[1] // 128
    rows[...] = jnp.zeros_like(rows)
    values = table[...].astype(f32)
    for layer in range(LAYERS):
        rows[layer * heads : (layer + 1) * heads, :entries] = values[:, layer, :]
    count = LAYERS * heads
    left = jnp.concatenate(
        [rows[:, group * 128 : (group + 1) * 128] for group in range(groups)], axis=0
    ).astype(bf16)

    def some(step, carry):
        values = []
        for lane in range(FILL):
            hot, high = hot_rows(index_t, step * FILL + lane)
            high = jnp.broadcast_to(high, (count, CELL))
            got = nn(left, hot)
            value = got[:count]
            for group in range(1, groups):
                value = jnp.where(high == group, got[group * count : (group + 1) * count], value)
            values.append(value * LOG2E)
        at = pl.ds(pl.multiple_of(step * FILL, 8), FILL)
        bias[:, at, :] = jnp.stack(values, axis=0).transpose(1, 0, 2)
        return carry

    lax.fori_loop(0, CELL // FILL, some, 0)
    for first in range(0, count, PER_TILE):
        packed[first // PER_TILE] = jnp.concatenate(
            [bias[first + head] for head in range(PER_TILE)], axis=1
        )


def fill_mask(region, mask):
    values = region[...].astype(f32).reshape(1, ROWS)
    count = SIDE // WIN
    for window in range(WINDOWS):
        first = (window // count) * WIN * SIDE + (window % count) * WIN
        row = jnp.concatenate(
            [values[:, first + i * SIDE : first + i * SIDE + WIN] for i in range(WIN)], axis=1
        )
        row = jnp.broadcast_to(row, (CELL, CELL))
        same = (row == row.T).astype(f32)
        mask[window] = jnp.concatenate([same] * PER_TILE, axis=1).astype(bf16)


SAVED = ("h1", "n1", "r1", "qkv", "prob", "mix", "h2", "n2", "r2", "hid", "slope")


def saved_shapes(width, heads_width, hidden):
    heads = heads_width // HD
    return {
        "h1": ((ROWS, width), bf16),
        "n1": ((ROWS, width), bf16),
        "r1": ((ROWS, 1), f32),
        "qkv": ((3, ROWS, heads_width), bf16),
        "prob": ((WINDOWS, heads // PER_TILE, CELL, PER_TILE * CELL), bf16),
        "mix": ((ROWS, heads_width), bf16),
        "h2": ((ROWS, width), bf16),
        "n2": ((ROWS, width), bf16),
        "r2": ((ROWS, 1), f32),
        "hid": ((ROWS, hidden), bf16),
        "slope": ((ROWS, hidden), bf16),
    }


BITS = 4
X_FIRST = (3, 2, 1, 0)
Y_FIRST = (2, 3, 1, 0)
Z_FIRST = (1, 0, 3, 2)
PARTS = ((1, 1, 1, 1), (1, 1, 1, 1), (1,), (1, 1, 1))
ORDERS = (
    (3, 1, 2, 0),
    (1, 0, 3, 2),
    (3, 2, 1, 0),
    (2, 1, 3, 0),
    (2, 3, 1, 0),
    (2, 3, 1, 0),
    (3, 1, 2, 0),
    (2, 3, 1, 0),
    (1, 0, 3, 2),
    (3, 2, 1, 0),
    (2, 3, 1, 0),
    (3, 2, 1, 0),
)
VECTOR_ROWS = 24
HALVES = 2
START = 100
VECTORS = 99

SCHEDULE = (
    (112,),
    (113,),
    (),
    (115,),
    (114,),
    (),
    (116,),
    (),
    (),
    (12, 112),
    (118, 13, 113, 15, 115),
    (119,),
    (),
    (),
    (),
    (14,),
    (120,),
    (16, 116, 114, 12),
    (),
    (121,),
    (),
    (),
    (122, 18, 13),
    (118, 15),
    (19,),
    (123, 16),
    (116,),
    (),
    (14, 112),
    (103, 114, 101, 20, 120),
    (119, 21, 18),
    (),
    (22,),
    (16, 116),
    (),
    (122, 121, 12, 112),
    (23, 14, 114),
    (106, 118),
    (),
    (104, 20),
    (108, 19, 16, 3),
    (),
    (12,),
    (),
    (111, 21, 22),
    (14,),
    (110, 18, 118),
    (1, 101),
    (103,),
    (),
    (100, 18, 107, 6, 4),
    (121, 106, 8, 108),
    (11, 1, 10, 3, 104, 117, 0, 100, 21, 110, 121, 7, 99, 122, 8, 107, 6, 106, 119, 21, 4, 17, 117, 105, 104, 0, 10, 22, 109, 110, 122, 99, 19, 119, 7, 6, 106, 4, 100, 104, 17, 123, 22, 115, 117, 10, 102, 110, 19, 5, 107, 6, 0, 100, 4, 9, 109, 99, 15, 10, 23, 103, 111, 123, 17, 105, 0, 117, 7, 9, 120, 109, 107, 2, 102, 23, 113, 123, 3, 11, 111, 115, 99, 5, 105, 17, 20, 108, 120, 9, 109, 2, 102, 7, 13, 101, 113, 23, 11, 111, 15, 103, 20, 8, 108, 9, 5, 105, 13, 1, 101, 2, 102, 11, 8, 3, 1, 5, 2),
)
REL_ROW = 9


def chunk_widths(unit):
    return [unit * count for group in PARTS for count in group]


def norm_back(grad, normed, scale, gain):
    c = grad * gain
    inner = c - jnp.mean(c, axis=-1, keepdims=True)
    return scale * (inner - normed * jnp.mean(c * normed, axis=-1, keepdims=True))


def column_sum(values):
    return jnp.sum(values, axis=0, keepdims=True)


def step_kernel(shift, *refs):
    it = iter(refs)

    def take(count):
        return [next(it) for _ in range(count)]

    tokens_hbm, cot_hbm, valid = take(3)
    gain1, off1, qv_b, proj_b, gain2, off2, up_b, down_b = take(8)
    table_in, index, region_ids = take(3)
    weights_hbm = take(4)
    output_hbm, input_grad_hbm, reduced_hbm, vectors_out = take(4)
    kept_hbm = dict(zip(SAVED, take(len(SAVED))))
    weights = take(4)
    kept = dict(zip(SAVED, take(len(SAVED))))
    chunks = sum(len(counts) for counts in PARTS)
    grads = [take(chunks) for _ in range(LAYERS)]
    landed = [take(BITS) for _ in range(chunks)]
    x, dy, out, low, send, recv, grad_mix, grad_qkv = take(8)
    bias, packed, mask, index_t, table_rows, grad_score, table = take(7)
    vectors, vectors_in, reduced = take(3)
    weight_sem, kept_sem, fetch_sem, send_sem, recv_sem = take(5)
    chunk_send, chunk_recv, credit, vector_send, vector_recv, row_sem, chunk_out = take(7)
    grad_bias = bias
    qkv_w, proj_w, up_w, down_w = weights
    heads_width = proj_w.shape[0]
    hidden = up_w.shape[1]
    width = dy.shape[1]
    heads = heads_width // HD
    tiles = heads_width // LANES
    part = width >> BITS
    widths = chunk_widths(heads_width)

    me = lax.axis_index("dp")
    other = 1 - lax.axis_index("tensor")
    places = [1 << (shift + BITS - 1 - dim) for dim in range(BITS)]
    mine = [lax.rem(lax.div(me, place), 2) for place in places]
    partner = [me + place - 2 * place * bit for place, bit in zip(places, mine)]

    top = LAYERS - 1

    def load(slot, layer):
        return pltpu.make_async_copy(weights_hbm[slot].at[layer], weights[slot], weight_sem.at[slot])

    def keep(name):
        return pltpu.make_async_copy(kept[name], kept_hbm[name], kept_sem.at[SAVED.index(name)])

    def fetch(name):
        return pltpu.make_async_copy(kept_hbm[name], kept[name], fetch_sem.at[SAVED.index(name)])

    def write(source, target, number):
        return pltpu.make_async_copy(source, target, row_sem.at[number])

    def swap(turn, first, count):
        at = pl.ds(first, count)
        return pltpu.make_async_remote_copy(
            src_ref=send.at[turn % 2, at],
            dst_ref=recv.at[turn % 2, at],
            send_sem=send_sem.at[turn, first],
            recv_sem=recv_sem.at[turn, first],
            device_id={"tensor": other},
            device_id_type=MESH_ID,
        )

    def give(turn, first, value):
        count = value.shape[0] // CELL
        for number in range(count):
            send[turn % 2, first + number] = value[number * CELL : (number + 1) * CELL].astype(bf16)
        swap(turn, first, count).start()

    def gather(turn, first, count):
        swap(turn, first, count).wait()
        parts = [
            send[turn % 2, first + number].astype(f32) + recv[turn % 2, first + number].astype(f32)
            for number in range(count)
        ]
        return parts[0] if count == 1 else jnp.concatenate(parts, axis=0)

    def rows_of(part_index, count):
        size = ROWS // count
        return slice(part_index * size, (part_index + 1) * size)

    step = {}

    def region(chunk, phase, bit):
        order = ORDERS[chunk]
        index = [slice(None)] * BITS
        for dim in order[:phase]:
            index[dim] = mine[dim]
        index[order[phase]] = bit
        return tuple(index)

    def chunk_copy(layer, chunk, phase):
        dim = ORDERS[chunk][phase]
        return pltpu.make_async_remote_copy(
            src_ref=grads[layer][chunk].at[region(chunk, phase, 1 - mine[dim])],
            dst_ref=landed[chunk][phase],
            send_sem=chunk_send.at[layer, chunk, phase],
            recv_sem=chunk_recv.at[layer, chunk, phase],
            device_id={"dp": partner[dim]},
            device_id_type=MESH_ID,
        )

    def chunk_result(layer, chunk):
        cols = pl.ds(sum(widths[:chunk]), widths[chunk])
        return pltpu.make_async_copy(
            reduced.at[layer, :, cols], reduced_hbm.at[layer, :, cols], chunk_out.at[layer, chunk]
        )

    def begin(layer, chunk):
        if layer < LAYERS - 1:
            pl.semaphore_wait(credit.at[chunk, step[layer, chunk]], 1)
        chunk_copy(layer, chunk, step[layer, chunk]).start()

    def advance(layer, chunk):
        phase = step[layer, chunk]
        dim = ORDERS[chunk][phase]
        chunk_copy(layer, chunk, phase).wait()
        keep = region(chunk, phase, mine[dim])
        free = [d for d in range(BITS) if isinstance(keep[d], slice)]
        ref, arrived = grads[layer][chunk], landed[chunk][phase]
        first = sum(widths[:chunk])
        for number in range(1 << len(free)):
            bits = [(number >> (len(free) - 1 - n)) & 1 for n in range(len(free))]
            index = list(keep)
            for d, bit in zip(free, bits):
                index[d] = bit
            here = ref[tuple(index)]
            there = arrived[tuple(bits)] if bits else arrived[...]
            if phase < BITS - 1:
                ref[tuple(index)] = here + there
            else:
                reduced[layer, :, first : first + widths[chunk]] = here.astype(f32) + there.astype(f32)
                chunk_result(layer, chunk).start()
        if layer == LAYERS - 1:
            pl.semaphore_signal(
                credit.at[chunk, phase], inc=1, device_id={"dp": partner[dim]}, device_id_type=MESH_ID
            )
        step[layer, chunk] = phase + 1

    def finish_chunk(layer, chunk, left, right):
        half = width // 2
        for top in range(2):
            value = tn(left[:, top * half : (top + 1) * half], right)
            grads[layer][chunk][top] = value.astype(bf16).reshape(2, 2, 2, part, widths[chunk])
        step[layer, chunk] = 0
        point()

    def finish_group(layer, group, left, right):
        chunk = sum(len(counts) for counts in PARTS[:group])
        first = 0
        for size in PARTS[group]:
            size *= heads_width
            finish_chunk(layer, chunk, left, right[:, first : first + size])
            first += size
            chunk += 1

    place = iter(SCHEDULE)

    def point():
        for action in next(place):
            if action == VECTORS:
                vector_step()
                continue
            chosen = divmod(action % START, chunks)
            if action >= START:
                begin(*chosen)
            else:
                advance(*chosen)

    def vector_copy(phase):
        return pltpu.make_async_remote_copy(
            src_ref=vectors.at[phase],
            dst_ref=vectors_in.at[phase],
            send_sem=vector_send.at[phase],
            recv_sem=vector_recv.at[phase],
            device_id={"dp": partner[BITS - 1 - phase]},
            device_id_type=MESH_ID,
        )

    rounds = iter(range(BITS))

    def vector_step():
        phase = next(rounds)
        vector_copy(phase).wait()
        total = vectors[phase] + vectors_in[phase]
        if phase < BITS - 1:
            vectors[phase + 1] = total
            vector_copy(phase + 1).start()
        else:
            vectors_out[...] = total

    write(tokens_hbm, kept["h2"], 0).start()
    write(cot_hbm, low, 1).start()
    for slot in range(4):
        load(slot, 0).start()
    barrier = pltpu.get_barrier_semaphore()
    pl.semaphore_signal(barrier, inc=1, device_id={"tensor": other}, device_id_type=MESH_ID)
    for dim in range(BITS):
        pl.semaphore_signal(barrier, inc=1, device_id={"dp": partner[dim]}, device_id_type=MESH_ID)
    fill_index(index, index_t)
    fill_bias(table_in, index_t, bias, table_rows, packed)
    fill_mask(region_ids, mask)
    vectors[0] = jnp.zeros(vectors.shape[1:], f32)
    write(tokens_hbm, kept["h2"], 0).wait()
    dy[...] = kept["h2"][...].astype(f32)
    move_rows(dy, x, None, False)
    pl.semaphore_wait(barrier, 1 + BITS)

    early, late = SAVED[:4], SAVED[6:]
    half_windows = WINDOWS // HALVES
    every = [(window,) for window in range(WINDOWS)]
    pairs = [(window, tile) for window in range(WINDOWS) for tile in range(tiles)]

    for layer in range(LAYERS):
        load(0, layer).wait()
        for name in early if layer > 0 else ():
            keep(name).wait()
        for window in range(WINDOWS):
            at = rows_of(window, WINDOWS)
            normed, scale = row_norm(x[at, :])
            h1 = (normed * wide(gain1, layer) + wide(off1, layer)).astype(bf16)
            kept["n1"][at, :] = normed.astype(bf16)
            kept["r1"][at, :] = scale
            kept["h1"][at, :] = h1
            kept["qkv"][0, at, :] = (nn(h1, qkv_w[0]) + qv_b[layer, 0:1, :].astype(f32)).astype(bf16)
            kept["qkv"][1, at, :] = nn(h1, qkv_w[1]).astype(bf16)
            kept["qkv"][2, at, :] = (nn(h1, qkv_w[2]) + qv_b[layer, 1:2, :].astype(f32)).astype(bf16)
        if layer < top:
            load(0, layer + 1).start()
            for name in early:
                keep(name).start()
        load(1, layer).wait()
        for name in SAVED[4:6] if layer > 0 else ():
            keep(name).wait()

        scores, probs = {}, {}

        def operand(slot, window, tile):
            return kept["qkv"][slot, rows_of(window, WINDOWS), tile * LANES : (tile + 1) * LANES]

        def score(window, tile):
            scores[window, tile] = nt(operand(1, window, tile), head_stack(operand(0, window, tile)))

        def soften(window, tile):
            s = scores.pop((window, tile)) * (SCALE * LOG2E) + packed[layer * tiles + tile]
            if layer == 1:
                s = jnp.where(mask[window].astype(f32) > 0.5, s, -1000000000.0 * LOG2E)
            e = jnp.exp2(s - jnp.max(s, axis=0, keepdims=True))
            prob = (e * (1.0 / jnp.sum(e, axis=0, keepdims=True))).astype(bf16)
            kept["prob"][window, tile] = prob
            probs[window, tile] = prob

        def mix(window, tile):
            at = rows_of(window, WINDOWS)
            value = head_pick(tn(probs.pop((window, tile)), operand(2, window, tile)))
            kept["mix"][at, tile * LANES : (tile + 1) * LANES] = value.astype(bf16)
            if tile == tiles - 1:
                give(2 * layer, window, nn(kept["mix"][at, :], proj_w[...]))

        staggered(pairs, (score, soften, mix))
        if layer < top:
            load(1, layer + 1).start()
            for name in SAVED[4:6]:
                keep(name).start()
        load(2, layer).wait()
        if layer < top:
            load(3, layer).wait()
        for name in late if layer > 0 else ():
            keep(name).wait()

        def join(window):
            at = rows_of(window, WINDOWS)
            middle = x[at, :] + gather(2 * layer, window, 1) + wide(proj_b, layer)
            x[at, :] = middle
            normed, scale = row_norm(middle)
            kept["n2"][at, :] = normed.astype(bf16)
            kept["r2"][at, :] = scale
            kept["h2"][at, :] = (normed * wide(gain2, layer) + wide(off2, layer)).astype(bf16)

        def expand(window):
            at = rows_of(window, WINDOWS)
            u = nn(kept["h2"][at, :], up_w[...]) + wide(up_b, layer)
            phi = 0.5 + 0.5 * lax.erf(u * 0.7071067811865476)
            kept["slope"][at, :] = (phi + u * jnp.exp(u * u * -0.5) * 0.3989422804014327).astype(bf16)
            kept["hid"][at, :] = (u * phi).astype(bf16)

        def shrink(window):
            give(2 * layer + 1, window, nn(kept["hid"][rows_of(window, WINDOWS), :], down_w[...]))

        if layer == top:
            staggered(every, (join, expand))
            continue
        staggered(every, (join, expand, shrink))
        for slot in (2, 3):
            load(slot, layer + 1).start()
        for name in late:
            keep(name).start()
        write(cot_hbm, low, 1).wait()
        out[...] = low[...].astype(f32) * valid[0].astype(f32)
        move_rows(out, dy, None, True)
        low[...] = dy[...].astype(bf16)
        for window in range(WINDOWS):
            at = rows_of(window, WINDOWS)
            out[at, :] = x[at, :] + gather(2 * layer + 1, window, 1) + wide(down_b, layer)
        move_rows(out, x, False, True)

    for layer in reversed(range(LAYERS)):
        turn = 2 * LAYERS + 2 * (LAYERS - 1 - layer)

        def add_row(row, value, first=0):
            cols = slice(first, first + value.shape[1])
            vectors[0, layer, row : row + 1, cols] += value

        def free(*names):
            for name in names if layer > 0 else ():
                fetch(name).start()

        def free_weight(slot):
            if layer > 0:
                load(slot, layer - 1).start()

        def ready(*names):
            for name in names if layer < top else ():
                fetch(name).wait()

        if layer < top:
            low[...] = dy[...].astype(bf16)
        ready("hid")
        finish_group(layer, 0, low[...], kept["hid"])
        add_row(5, column_sum(dy[...]))
        load(3, layer).wait()
        if layer == top:
            for half in range(HALVES):
                give(turn - 1, half * half_windows, nn(kept["hid"][rows_of(half, HALVES), :], down_w[...]))
        free("hid")
        ready("slope")
        if layer < top:
            load(2, layer).wait()
        for half in range(HALVES):
            at = rows_of(half, HALVES)
            grad = nt(low[at, :], down_w[...]) * kept["slope"][at, :].astype(f32)
            add_row(7, column_sum(grad[:, :width]))
            add_row(8, column_sum(grad[:, width:]))
            kept["slope"][at, :] = grad.astype(bf16)
            if layer == top and half == 0:
                for number in range(HALVES):
                    rows = rows_of(number, HALVES)
                    total = gather(turn - 1, number * half_windows, half_windows)
                    x[rows, :] = x[rows, :] + total + wide(down_b, top)
            give(turn, half * half_windows, nt(kept["slope"][at, :], up_w[...]))
            point()
        free_weight(3)
        free_weight(2)
        ready("h2")
        finish_group(layer, 1, kept["h2"][...], kept["slope"])
        free("h2", "slope")
        ready("n2", "r2", "mix")
        if layer < top:
            load(1, layer).wait()
        for half in range(HALVES):
            at = rows_of(half, HALVES)
            grad = gather(turn, half * half_windows, half_windows)
            normed = kept["n2"][at, :].astype(f32)
            add_row(3, column_sum(grad * normed))
            add_row(4, column_sum(grad))
            total = dy[at, :] + norm_back(grad, normed, kept["r2"][at, :], wide(gain2, layer))
            dy[at, :] = total
            add_row(2, column_sum(total))
            low[at, :] = total.astype(bf16)
            grad_mix[at, :] = nt(low[at, :], proj_w[...]).astype(bf16)
            point()
        free("n2", "r2")
        free_weight(1)
        finish_group(layer, 2, low[...], kept["mix"])
        free("mix")

        ready("prob", "qkv")
        stacks, drops, lows = {}, {}, {}

        def operand(ref, window, tile):
            return ref[rows_of(window, WINDOWS), tile * LANES : (tile + 1) * LANES]

        def pull(window, tile):
            stacks[window, tile] = head_stack(operand(grad_mix, window, tile))
            drops[window, tile] = nt(operand(kept["qkv"].at[2], window, tile), stacks[window, tile])

        def harden(window, tile):
            prob = kept["prob"][window, tile].astype(f32)
            weighted = prob * drops.pop((window, tile))
            value = weighted - prob * column_sum(weighted)
            if window == 0:
                grad_score[tile] = value
            else:
                grad_score[tile] += value
            lows[window, tile] = value.astype(bf16)

        def split(window, tile):
            value = lows.pop((window, tile))
            grad_v = nn(kept["prob"][window, tile], stacks.pop((window, tile)))
            grad_k = nn(value, head_stack(operand(kept["qkv"].at[0], window, tile))) * SCALE
            grad_q = head_pick(tn(value, operand(kept["qkv"].at[1], window, tile))) * SCALE
            for slot, part_grad in enumerate((grad_q, grad_k, grad_v)):
                grad_qkv[slot, rows_of(window, WINDOWS), tile * LANES : (tile + 1) * LANES] = (
                    part_grad.astype(bf16)
                )
            add_row(6, column_sum(grad_q), tile * LANES)
            add_row(6, column_sum(grad_v), heads_width + tile * LANES)
            if tile == tiles - 1:
                point()

        staggered(pairs, (pull, harden, split))
        for head in range(heads):
            lane = head % PER_TILE * CELL
            grad_bias[layer * heads + head] = grad_score[head // PER_TILE, :, lane : lane + CELL]
        free("prob", "qkv")
        ready("h1")

        def finish_qkv():
            for place_index, slot in enumerate((2, 0, 1)):
                finish_chunk(layer, chunks - 3 + place_index, kept["h1"][...], grad_qkv[slot])

        if layer < top:
            finish_qkv()
            load(0, layer).wait()
        for half in range(HALVES):
            at = rows_of(half, HALVES)
            total = nt(grad_qkv[0, at, :], qkv_w[0])
            total = total + nt(grad_qkv[1, at, :], qkv_w[1])
            total = total + nt(grad_qkv[2, at, :], qkv_w[2])
            give(turn + 1, half * half_windows, total)
            point()
        free_weight(0)
        if layer == top:
            finish_qkv()
        free("h1")
        ready("n1", "r1")
        for half in range(HALVES):
            at = rows_of(half, HALVES)
            grad = gather(turn + 1, half * half_windows, half_windows)
            normed = kept["n1"][at, :].astype(f32)
            add_row(0, column_sum(grad * normed))
            add_row(1, column_sum(grad))
            out[at, :] = dy[at, :] + norm_back(grad, normed, kept["r1"][at, :], wide(gain1, layer))
            point()
        free("n1", "r1")
        if layer > 0:
            move_rows(out, dy, True, False)
        point()

    table[...] = jnp.zeros_like(table)
    groups = table.shape[0] // (LAYERS * heads)

    def scatter(step_index, carry):
        at = pl.ds(pl.multiple_of(step_index * UNROLL, 8), UNROLL)
        pair_sums = grad_bias[:, at, :].transpose(1, 0, 2)
        total = None
        for lane in range(UNROLL):
            hot, high = hot_rows(index_t, step_index * UNROLL + lane)
            score = pair_sums[lane]
            high = jnp.broadcast_to(high, score.shape)
            left = jnp.concatenate(
                [jnp.where(high == group, score, 0.0) for group in range(groups)], axis=0
            ).astype(bf16)
            value = nt(left, hot)
            total = value if total is None else total + value
        table[...] += total
        return carry

    steps = CELL // UNROLL
    for quarter in range(2):
        lax.fori_loop(quarter * steps // 2, (quarter + 1) * steps // 2, scatter, 0)
        if quarter == 0:
            move_rows(out, dy, False, None)
            write(dy, input_grad_hbm, 0).start()
        else:
            move_rows(x, out, True, None)
            write(out, output_hbm, 1).start()
        point()
    for layer in range(LAYERS):
        for group in range(groups):
            first = (group * LAYERS + layer) * heads
            vectors[0, layer, REL_ROW : REL_ROW + heads, group * 128 : (group + 1) * 128] = table[
                first : first + heads, :
            ]
    vector_copy(0).start()
    point()
    for layer in range(LAYERS):
        for chunk in range(chunks):
            chunk_result(layer, chunk).wait()
    write(dy, input_grad_hbm, 0).wait()
    write(out, output_hbm, 1).wait()


def run_step(shift, tokens, cot, valid, vectors, tables, weights):
    width = cot.shape[1]
    heads_width = weights[1].shape[1]
    hidden = weights[2].shape[2]
    heads = heads_width // HD
    tiles = heads_width // LANES
    entries = -(-tables[0].shape[2] // 128) * 128
    part = width >> BITS
    widths = chunk_widths(heads_width)
    shapes = saved_shapes(width, heads_width, hidden)
    vmem = pl.BlockSpec(memory_space=pltpu.VMEM)
    hbm = pl.BlockSpec(memory_space=pl.ANY)
    smem = pl.BlockSpec(memory_space=pltpu.SMEM)
    grads = [pltpu.VMEM((2,) * BITS + (part, w), bf16) for w in widths] * LAYERS
    landed = [
        pltpu.VMEM((2,) * (BITS - 1 - phase) + (part, w), bf16) for w in widths for phase in range(BITS)
    ]
    swaps = (2, WINDOWS, CELL, width)
    rounds = (4 * LAYERS, WINDOWS)
    sums = (LAYERS, VECTOR_ROWS, width)
    chunk_rounds = (LAYERS, len(widths), BITS)
    reduced = (LAYERS, part, sum(widths))
    outs = pl.pallas_call(
        functools.partial(step_kernel, shift),
        out_shape=[
            jax.ShapeDtypeStruct((ROWS, width), f32),
            jax.ShapeDtypeStruct((ROWS, width), f32),
            jax.ShapeDtypeStruct(reduced, f32),
            jax.ShapeDtypeStruct(sums, f32),
        ]
        + [jax.ShapeDtypeStruct(*shapes[name]) for name in SAVED],
        in_specs=[hbm, hbm, smem] + [vmem] * 11 + [hbm] * 4,
        out_specs=[hbm, hbm, hbm, vmem] + [hbm] * len(SAVED),
        scratch_shapes=[pltpu.VMEM(w.shape[1:], bf16) for w in weights]
        + [pltpu.VMEM(*shapes[name]) for name in SAVED]
        + grads
        + landed
        + [
            pltpu.VMEM((ROWS, width), f32),
            pltpu.VMEM((ROWS, width), f32),
            pltpu.VMEM((ROWS, width), f32),
            pltpu.VMEM((ROWS, width), bf16),
            pltpu.VMEM(swaps, bf16),
            pltpu.VMEM(swaps, bf16),
            pltpu.VMEM((ROWS, heads_width), bf16),
            pltpu.VMEM((3, ROWS, heads_width), bf16),
            pltpu.VMEM((LAYERS * heads, CELL, CELL), f32),
            pltpu.VMEM((LAYERS * tiles, CELL, PER_TILE * CELL), f32),
            pltpu.VMEM((WINDOWS, CELL, PER_TILE * CELL), bf16),
            pltpu.VMEM((CELL, CELL), jnp.int32),
            pltpu.VMEM((LAYERS * heads, entries), f32),
            pltpu.VMEM((tiles, CELL, PER_TILE * CELL), f32),
            pltpu.VMEM((entries // 128 * LAYERS * heads, 128), f32),
            pltpu.VMEM((BITS,) + sums, f32),
            pltpu.VMEM((BITS,) + sums, f32),
            pltpu.VMEM(reduced, f32),
            pltpu.SemaphoreType.DMA((4,)),
            pltpu.SemaphoreType.DMA((len(SAVED),)),
            pltpu.SemaphoreType.DMA((len(SAVED),)),
            pltpu.SemaphoreType.DMA(rounds),
            pltpu.SemaphoreType.DMA(rounds),
            pltpu.SemaphoreType.DMA(chunk_rounds),
            pltpu.SemaphoreType.DMA(chunk_rounds),
            pltpu.SemaphoreType.REGULAR(chunk_rounds[1:]),
            pltpu.SemaphoreType.DMA((BITS,)),
            pltpu.SemaphoreType.DMA((BITS,)),
            pltpu.SemaphoreType.DMA((2,)),
            pltpu.SemaphoreType.DMA(chunk_rounds[:2]),
        ],
        compiler_params=pltpu.CompilerParams(
            collective_id=0, has_side_effects=True, vmem_limit_bytes=VMEM_LIMIT
        ),
        name="step",
    )(tokens, cot, valid, *vectors, *tables, *weights)
    return outs[:4]


def result_kernel(x, dx, reduced, vectors, *outs):
    (output, input_grad, g1, o1, qkv_g, qv_g, rel_g, proj_g, pb_g, g2, o2, up_g, ub_g, down_g, db_g) = outs
    hidden = up_g.shape[2]
    heads_width = proj_g.shape[2]
    width = g1.shape[1]
    heads, _, entries = rel_g.shape
    output[...] = x[...]
    input_grad[...] = dx[...]
    for layer in range(LAYERS):
        first = 0
        for target, size in (
            (down_g.at[layer], hidden),
            (up_g.at[layer], hidden),
            (proj_g.at[layer], heads_width),
            (qkv_g.at[layer, 2], heads_width),
            (qkv_g.at[layer, 0], heads_width),
            (qkv_g.at[layer, 1], heads_width),
        ):
            target[...] = reduced[layer, :, first : first + size]
            first += size
        row = slice(layer, layer + 1)
        for number, ref in enumerate((g1, o1, pb_g, g2, o2, db_g)):
            ref[row, :] = vectors[layer, number : number + 1, :]
        qv_g[layer, 0:1, :] = vectors[layer, 6:7, :heads_width]
        qv_g[layer, 1:2, :] = vectors[layer, 6:7, heads_width:]
        ub_g[row, :width] = vectors[layer, 7:8, :]
        ub_g[row, width:] = vectors[layer, 8:9, :]
        rel_g[:, layer, :] = vectors[layer, REL_ROW : REL_ROW + heads, :entries]


def per_device(
    tokens,
    region_ids,
    rel_index,
    valid,
    ln1_gain,
    ln1_bias,
    qkv_weight,
    qv_bias,
    rel_table,
    proj_weight,
    proj_bias,
    ln2_gain,
    ln2_bias,
    fc1_weight,
    fc1_bias,
    fc2_weight,
    fc2_bias,
    cotangent,
):
    devices = lax.axis_size("dp")
    group = devices >> BITS
    shift = group.bit_length() - 1
    width = tokens.shape[1]
    heads_width = proj_weight.shape[1]
    hidden = fc1_weight.shape[2]
    tables = (rel_table.transpose(2, 0, 1), rel_index, region_ids)
    weights = (qkv_weight, proj_weight, fc1_weight, fc2_weight)
    vectors = (ln1_gain, ln1_bias, qv_bias, proj_bias, ln2_gain, ln2_bias, fc1_bias, fc2_bias)
    x, dx, reduced, sums = run_step(shift, tokens, cotangent, valid, vectors, tables, weights)
    if group > 1:
        sets = [list(range(first, first + group)) for first in range(0, devices, group)]
        reduced = lax.psum_scatter(
            reduced, "dp", scatter_dimension=1, axis_index_groups=sets, tiled=True
        )
        sums = lax.psum(sums, "dp", axis_index_groups=sets)
    part = width // devices
    shapes = (
        (ROWS, width),
        (ROWS, width),
        (LAYERS, width),
        (LAYERS, width),
        (LAYERS, 3, part, heads_width),
        (LAYERS, 2, heads_width),
        tables[0].shape,
        (LAYERS, part, heads_width),
        (LAYERS, width),
        (LAYERS, width),
        (LAYERS, width),
        (LAYERS, part, hidden),
        (LAYERS, hidden),
        (LAYERS, part, hidden),
        (LAYERS, width),
    )
    vmem = pl.BlockSpec(memory_space=pltpu.VMEM)
    outs = list(
        pl.pallas_call(
            result_kernel,
            out_shape=[jax.ShapeDtypeStruct(shape, f32) for shape in shapes],
            in_specs=[vmem] * 4,
            out_specs=[vmem] * len(shapes),
            compiler_params=pltpu.CompilerParams(vmem_limit_bytes=VMEM_LIMIT),
            name="results",
        )(x, dx, reduced, sums)
    )
    outs[6] = outs[6].transpose(1, 2, 0)
    outs[7] = outs[7].transpose(0, 2, 1)
    outs[13] = outs[13].transpose(0, 2, 1)
    return tuple(outs)


def solution(mesh):
    return jax.shard_map(
        per_device,
        mesh=mesh,
        in_specs=(
            P("dp", None),
            P(),
            P(),
            P("dp"),
            P(),
            P(),
            P(None, None, None, "tensor"),
            P(None, None, "tensor"),
            P(None, None, "tensor"),
            P(None, "tensor", None),
            P(),
            P(),
            P(),
            P(None, None, "tensor"),
            P(None, "tensor"),
            P(None, "tensor", None),
            P(),
            P("dp", None),
        ),
        out_specs=(
            P("dp", None),
            P("dp", None),
            P(),
            P(),
            P(None, None, "dp", "tensor"),
            P(None, None, "tensor"),
            P(None, None, "tensor"),
            P(None, "tensor", "dp"),
            P(),
            P(),
            P(),
            P(None, "dp", "tensor"),
            P(None, "tensor"),
            P(None, "tensor", "dp"),
            P(),
        ),
        check_vma=False,
    )
```

```python
import functools

import jax
import jax.numpy as jnp
from jax import lax
from jax.experimental import pallas as pl
from jax.experimental.pallas import tpu as pltpu
from jax.sharding import PartitionSpec as P

HD = 32
WIN = 12
SIDE = 24
LAYERS = 2
SHIFT = 6
ROWS = SIDE * SIDE
CELL = WIN * WIN
WINDOWS = ROWS // CELL
PER_TILE = 4
LANES = PER_TILE * HD
EPSILON = 1e-05
UNROLL = 16
FILL = 72
LOG2E = 1.4426950408889634
SCALE = HD**-0.5
VMEM_LIMIT = 62 * 1024 * 1024
MESH_ID = pl.DeviceIdType.MESH

f32 = jnp.float32
bf16 = jnp.bfloat16


def nn(a, b):
    return jnp.dot(a, b, preferred_element_type=f32)


def nt(a, b):
    return lax.dot_general(a, b, (((1,), (1,)), ((), ())), preferred_element_type=f32)


def tn(a, b):
    return lax.dot_general(a, b, (((0,), (0,)), ((), ())), preferred_element_type=f32)


def window_row(i, j, shifted):
    if shifted:
        i, j = (i - SHIFT) % SIDE, (j - SHIFT) % SIDE
    return ((i // WIN) * (SIDE // WIN) + j // WIN) * CELL + (i % WIN) * WIN + j % WIN


def pieces(source, target):
    found = []
    for i in range(SIDE):
        for j in range(0, SIDE, SHIFT):
            row = [i * SIDE + j if o is None else window_row(i, j, o) for o in (source, target)]
            found.append(tuple(row))
    return found


def move_rows(source_ref, target_ref, source, target):
    for here, there in pieces(source, target):
        target_ref[there : there + SHIFT, :] = source_ref[here : here + SHIFT, :]


def lane_head(values, head):
    lane = lax.broadcasted_iota(jnp.int32, values.shape, 1)
    return jnp.where((lane >= HD * head) & (lane < HD * (head + 1)), values, jnp.zeros_like(values))


def head_stack(values):
    return jnp.concatenate([lane_head(values, head) for head in range(PER_TILE)], axis=0)


def head_pick(values):
    rows = values.shape[0] // PER_TILE
    total = None
    for head in range(PER_TILE):
        own = lane_head(values[head * rows : (head + 1) * rows], head)
        total = own if total is None else total + own
    return total


def staggered(items, stages):
    for tick in range(len(items) + len(stages) - 1):
        for number, stage in enumerate(stages):
            if 0 <= tick - number < len(items):
                stage(*items[tick - number])


def row_norm(values):
    center = values - jnp.mean(values, axis=-1, keepdims=True)
    scale = lax.rsqrt(jnp.mean(center * center, axis=-1, keepdims=True) + EPSILON)
    return center * scale, scale


def wide(ref, layer):
    return ref[layer : layer + 1, :].astype(f32)


def hot_rows(index_t, key):
    row = index_t[pl.ds(key, 1), :]
    low = jnp.broadcast_to((row & 127).astype(f32).astype(bf16), (128, CELL))
    entry = lax.broadcasted_iota(jnp.int32, (128, CELL), 0).astype(f32).astype(bf16)
    return jnp.where(entry == low, jnp.ones((), bf16), jnp.zeros((), bf16)), row >> 7


def fill_index(index, index_t):
    index_t[...] = index[...].astype(f32).T.astype(jnp.int32)


def fill_bias(table, index_t, bias, rows, packed):
    heads, _, entries = table.shape
    groups = rows.shape[1] // 128
    rows[...] = jnp.zeros_like(rows)
    values = table[...].astype(f32)
    for layer in range(LAYERS):
        rows[layer * heads : (layer + 1) * heads, :entries] = values[:, layer, :]
    count = LAYERS * heads
    left = jnp.concatenate(
        [rows[:, group * 128 : (group + 1) * 128] for group in range(groups)], axis=0
    ).astype(bf16)

    def some(step, carry):
        values = []
        for lane in range(FILL):
            hot, high = hot_rows(index_t, step * FILL + lane)
            high = jnp.broadcast_to(high, (count, CELL))
            got = nn(left, hot)
            value = got[:count]
            for group in range(1, groups):
                value = jnp.where(high == group, got[group * count : (group + 1) * count], value)
            values.append(value * LOG2E)
        at = pl.ds(pl.multiple_of(step * FILL, 8), FILL)
        bias[:, at, :] = jnp.stack(values, axis=0).transpose(1, 0, 2)
        return carry

    lax.fori_loop(0, CELL // FILL, some, 0)
    for first in range(0, count, PER_TILE):
        packed[first // PER_TILE] = jnp.concatenate(
            [bias[first + head] for head in range(PER_TILE)], axis=1
        )


def fill_mask(region, mask):
    values = region[...].astype(f32).reshape(1, ROWS)
    count = SIDE // WIN
    for window in range(WINDOWS):
        first = (window // count) * WIN * SIDE + (window % count) * WIN
        row = jnp.concatenate(
            [values[:, first + i * SIDE : first + i * SIDE + WIN] for i in range(WIN)], axis=1
        )
        row = jnp.broadcast_to(row, (CELL, CELL))
        same = (row == row.T).astype(f32)
        mask[window] = jnp.concatenate([same] * PER_TILE, axis=1).astype(bf16)


SAVED = ("h1", "n1", "r1", "qkv", "prob", "mix", "h2", "n2", "r2", "hid", "slope")


def saved_shapes(width, heads_width, hidden):
    heads = heads_width // HD
    return {
        "h1": ((ROWS, width), bf16),
        "n1": ((ROWS, width), bf16),
        "r1": ((ROWS, 1), f32),
        "qkv": ((3, ROWS, heads_width), bf16),
        "prob": ((WINDOWS, heads // PER_TILE, CELL, PER_TILE * CELL), bf16),
        "mix": ((ROWS, heads_width), bf16),
        "h2": ((ROWS, width), bf16),
        "n2": ((ROWS, width), bf16),
        "r2": ((ROWS, 1), f32),
        "hid": ((ROWS, hidden), bf16),
        "slope": ((ROWS, hidden), bf16),
    }


BITS = 4
X_FIRST = (3, 2, 1, 0)
Y_FIRST = (2, 3, 1, 0)
Z_FIRST = (1, 0, 3, 2)
PARTS = ((1, 1, 1, 1), (1, 1, 1, 1), (1,), (1, 1, 1))
ORDERS = (
    (3, 1, 2, 0),
    (1, 0, 3, 2),
    (3, 2, 1, 0),
    (2, 1, 3, 0),
    (2, 3, 1, 0),
    (2, 3, 1, 0),
    (3, 1, 2, 0),
    (2, 3, 1, 0),
    (1, 0, 3, 2),
    (3, 2, 1, 0),
    (2, 3, 1, 0),
    (3, 2, 1, 0),
)
VECTOR_ROWS = 24
HALVES = 2
START = 100
VECTORS = 99

SCHEDULE = (
    (112,),
    (113,),
    (),
    (115,),
    (114,),
    (),
    (116,),
    (),
    (),
    (12, 112),
    (118, 13, 113, 15, 115),
    (119,),
    (),
    (),
    (),
    (14,),
    (120,),
    (16, 116, 114, 12),
    (),
    (121,),
    (),
    (),
    (122, 18, 13),
    (118, 15),
    (19,),
    (123, 16),
    (116,),
    (),
    (14, 112),
    (103, 114, 101, 20, 120),
    (119, 21, 18),
    (),
    (22,),
    (16, 116),
    (),
    (122, 121, 12, 112),
    (23, 14, 114),
    (106, 118),
    (),
    (104, 20),
    (108, 19, 16, 3),
    (),
    (12,),
    (),
    (111, 21, 22),
    (14,),
    (110, 18, 118),
    (1, 101),
    (103,),
    (),
    (100, 18, 107, 6, 4),
    (121, 106, 8, 108),
    (11, 1, 10, 3, 104, 117, 0, 100, 21, 110, 121, 7, 99, 122, 8, 107, 6, 106, 119, 21, 4, 17, 117, 105, 104, 0, 10, 22, 109, 110, 122, 99, 19, 119, 7, 6, 106, 4, 100, 104, 17, 123, 22, 115, 117, 10, 102, 110, 19, 5, 107, 6, 0, 100, 4, 9, 109, 99, 15, 10, 23, 103, 111, 123, 17, 105, 0, 117, 7, 9, 120, 109, 107, 2, 102, 23, 113, 123, 3, 11, 111, 115, 99, 5, 105, 17, 20, 108, 120, 9, 109, 2, 102, 7, 13, 101, 113, 23, 11, 111, 15, 103, 20, 8, 108, 9, 5, 105, 13, 1, 101, 2, 102, 11, 8, 3, 1, 5, 2),
)
REL_ROW = 9


def chunk_widths(unit):
    return [unit * count for group in PARTS for count in group]


def norm_back(grad, normed, scale, gain):
    c = grad * gain
    inner = c - jnp.mean(c, axis=-1, keepdims=True)
    return scale * (inner - normed * jnp.mean(c * normed, axis=-1, keepdims=True))


def column_sum(values):
    return jnp.sum(values, axis=0, keepdims=True)


def step_kernel(shift, *refs):
    it = iter(refs)

    def take(count):
        return [next(it) for _ in range(count)]

    tokens_hbm, cot_hbm, valid = take(3)
    gain1, off1, qv_b, proj_b, gain2, off2, up_b, down_b = take(8)
    table_in, index, region_ids = take(3)
    weights_hbm = take(4)
    output_hbm, input_grad_hbm, reduced_hbm, vectors_out = take(4)
    kept_hbm = dict(zip(SAVED, take(len(SAVED))))
    weights = take(4)
    kept = dict(zip(SAVED, take(len(SAVED))))
    chunks = sum(len(counts) for counts in PARTS)
    grads = [take(chunks) for _ in range(LAYERS)]
    landed = [take(BITS) for _ in range(chunks)]
    x, dy, out, low, send, recv, grad_mix, grad_qkv = take(8)
    bias, packed, mask, index_t, table_rows, grad_score, table = take(7)
    vectors, vectors_in, reduced = take(3)
    weight_sem, kept_sem, fetch_sem, send_sem, recv_sem = take(5)
    chunk_send, chunk_recv, credit, vector_send, vector_recv, row_sem, chunk_out = take(7)
    grad_bias = bias
    qkv_w, proj_w, up_w, down_w = weights
    heads_width = proj_w.shape[0]
    hidden = up_w.shape[1]
    width = dy.shape[1]
    heads = heads_width // HD
    tiles = heads_width // LANES
    part = width >> BITS
    widths = chunk_widths(heads_width)

    me = lax.axis_index("dp")
    other = 1 - lax.axis_index("tensor")
    places = [1 << (shift + BITS - 1 - dim) for dim in range(BITS)]
    mine = [lax.rem(lax.div(me, place), 2) for place in places]
    partner = [me + place - 2 * place * bit for place, bit in zip(places, mine)]

    top = LAYERS - 1

    def load(slot, layer):
        return pltpu.make_async_copy(weights_hbm[slot].at[layer], weights[slot], weight_sem.at[slot])

    def keep(name):
        return pltpu.make_async_copy(kept[name], kept_hbm[name], kept_sem.at[SAVED.index(name)])

    def fetch(name):
        return pltpu.make_async_copy(kept_hbm[name], kept[name], fetch_sem.at[SAVED.index(name)])

    def write(source, target, number):
        return pltpu.make_async_copy(source, target, row_sem.at[number])

    def swap(turn, first, count):
        at = pl.ds(first, count)
        return pltpu.make_async_remote_copy(
            src_ref=send.at[turn % 2, at],
            dst_ref=recv.at[turn % 2, at],
            send_sem=send_sem.at[turn, first],
            recv_sem=recv_sem.at[turn, first],
            device_id={"tensor": other},
            device_id_type=MESH_ID,
        )

    def give(turn, first, value):
        count = value.shape[0] // CELL
        for number in range(count):
            send[turn % 2, first + number] = value[number * CELL : (number + 1) * CELL].astype(bf16)
        swap(turn, first, count).start()

    def gather(turn, first, count):
        swap(turn, first, count).wait()
        parts = [
            send[turn % 2, first + number].astype(f32) + recv[turn % 2, first + number].astype(f32)
            for number in range(count)
        ]
        return parts[0] if count == 1 else jnp.concatenate(parts, axis=0)

    def rows_of(part_index, count):
        size = ROWS // count
        return slice(part_index * size, (part_index + 1) * size)

    step = {}

    def region(chunk, phase, bit):
        order = ORDERS[chunk]
        index = [slice(None)] * BITS
        for dim in order[:phase]:
            index[dim] = mine[dim]
        index[order[phase]] = bit
        return tuple(index)

    def chunk_copy(layer, chunk, phase):
        dim = ORDERS[chunk][phase]
        return pltpu.make_async_remote_copy(
            src_ref=grads[layer][chunk].at[region(chunk, phase, 1 - mine[dim])],
            dst_ref=landed[chunk][phase],
            send_sem=chunk_send.at[layer, chunk, phase],
            recv_sem=chunk_recv.at[layer, chunk, phase],
            device_id={"dp": partner[dim]},
            device_id_type=MESH_ID,
        )

    def chunk_result(layer, chunk):
        cols = pl.ds(sum(widths[:chunk]), widths[chunk])
        return pltpu.make_async_copy(
            reduced.at[layer, :, cols], reduced_hbm.at[layer, :, cols], chunk_out.at[layer, chunk]
        )

    def begin(layer, chunk):
        if layer < LAYERS - 1:
            pl.semaphore_wait(credit.at[chunk, step[layer, chunk]], 1)
        chunk_copy(layer, chunk, step[layer, chunk]).start()

    def advance(layer, chunk):
        phase = step[layer, chunk]
        dim = ORDERS[chunk][phase]
        chunk_copy(layer, chunk, phase).wait()
        keep = region(chunk, phase, mine[dim])
        free = [d for d in range(BITS) if isinstance(keep[d], slice)]
        ref, arrived = grads[layer][chunk], landed[chunk][phase]
        first = sum(widths[:chunk])
        for number in range(1 << len(free)):
            bits = [(number >> (len(free) - 1 - n)) & 1 for n in range(len(free))]
            index = list(keep)
            for d, bit in zip(free, bits):
                index[d] = bit
            here = ref[tuple(index)]
            there = arrived[tuple(bits)] if bits else arrived[...]
            if phase < BITS - 1:
                ref[tuple(index)] = here + there
            else:
                reduced[layer, :, first : first + widths[chunk]] = here.astype(f32) + there.astype(f32)
                chunk_result(layer, chunk).start()
        if layer == LAYERS - 1:
            pl.semaphore_signal(
                credit.at[chunk, phase], inc=1, device_id={"dp": partner[dim]}, device_id_type=MESH_ID
            )
        step[layer, chunk] = phase + 1

    def finish_chunk(layer, chunk, left, right):
        half = width // 2
        for top in range(2):
            value = tn(left[:, top * half : (top + 1) * half], right)
            grads[layer][chunk][top] = value.astype(bf16).reshape(2, 2, 2, part, widths[chunk])
        step[layer, chunk] = 0
        point()

    def finish_group(layer, group, left, right):
        chunk = sum(len(counts) for counts in PARTS[:group])
        first = 0
        for size in PARTS[group]:
            size *= heads_width
            finish_chunk(layer, chunk, left, right[:, first : first + size])
            first += size
            chunk += 1

    place = iter(SCHEDULE)

    def point():
        for action in next(place):
            if action == VECTORS:
                vector_step()
                continue
            chosen = divmod(action % START, chunks)
            if action >= START:
                begin(*chosen)
            else:
                advance(*chosen)

    def vector_copy(phase):
        return pltpu.make_async_remote_copy(
            src_ref=vectors.at[phase],
            dst_ref=vectors_in.at[phase],
            send_sem=vector_send.at[phase],
            recv_sem=vector_recv.at[phase],
            device_id={"dp": partner[BITS - 1 - phase]},
            device_id_type=MESH_ID,
        )

    rounds = iter(range(BITS))

    def vector_step():
        phase = next(rounds)
        vector_copy(phase).wait()
        total = vectors[phase] + vectors_in[phase]
        if phase < BITS - 1:
            vectors[phase + 1] = total
            vector_copy(phase + 1).start()
        else:
            vectors_out[...] = total

    write(tokens_hbm, kept["h2"], 0).start()
    write(cot_hbm, low, 1).start()
    for slot in range(4):
        load(slot, 0).start()
    barrier = pltpu.get_barrier_semaphore()
    pl.semaphore_signal(barrier, inc=1, device_id={"tensor": other}, device_id_type=MESH_ID)
    for dim in range(BITS):
        pl.semaphore_signal(barrier, inc=1, device_id={"dp": partner[dim]}, device_id_type=MESH_ID)
    fill_index(index, index_t)
    fill_bias(table_in, index_t, bias, table_rows, packed)
    fill_mask(region_ids, mask)
    vectors[0] = jnp.zeros(vectors.shape[1:], f32)
    write(tokens_hbm, kept["h2"], 0).wait()
    dy[...] = kept["h2"][...].astype(f32)
    move_rows(dy, x, None, False)
    pl.semaphore_wait(barrier, 1 + BITS)

    early, late = SAVED[:4], SAVED[6:]
    half_windows = WINDOWS // HALVES
    every = [(window,) for window in range(WINDOWS)]
    pairs = [(window, tile) for window in range(WINDOWS) for tile in range(tiles)]

    for layer in range(LAYERS):
        load(0, layer).wait()
        for name in early if layer > 0 else ():
            keep(name).wait()
        for window in range(WINDOWS):
            at = rows_of(window, WINDOWS)
            normed, scale = row_norm(x[at, :])
            h1 = (normed * wide(gain1, layer) + wide(off1, layer)).astype(bf16)
            kept["n1"][at, :] = normed.astype(bf16)
            kept["r1"][at, :] = scale
            kept["h1"][at, :] = h1
            kept["qkv"][0, at, :] = (nn(h1, qkv_w[0]) + qv_b[layer, 0:1, :].astype(f32)).astype(bf16)
            kept["qkv"][1, at, :] = nn(h1, qkv_w[1]).astype(bf16)
            kept["qkv"][2, at, :] = (nn(h1, qkv_w[2]) + qv_b[layer, 1:2, :].astype(f32)).astype(bf16)
        if layer < top:
            load(0, layer + 1).start()
            for name in early:
                keep(name).start()
        load(1, layer).wait()
        for name in SAVED[4:6] if layer > 0 else ():
            keep(name).wait()

        scores, probs = {}, {}

        def operand(slot, window, tile):
            return kept["qkv"][slot, rows_of(window, WINDOWS), tile * LANES : (tile + 1) * LANES]

        def score(window, tile):
            scores[window, tile] = nt(operand(1, window, tile), head_stack(operand(0, window, tile)))

        def soften(window, tile):
            s = scores.pop((window, tile)) * (SCALE * LOG2E) + packed[layer * tiles + tile]
            if layer == 1:
                s = jnp.where(mask[window].astype(f32) > 0.5, s, -1000000000.0 * LOG2E)
            e = jnp.exp2(s - jnp.max(s, axis=0, keepdims=True))
            prob = (e * (1.0 / jnp.sum(e, axis=0, keepdims=True))).astype(bf16)
            kept["prob"][window, tile] = prob
            probs[window, tile] = prob

        def mix(window, tile):
            at = rows_of(window, WINDOWS)
            value = head_pick(tn(probs.pop((window, tile)), operand(2, window, tile)))
            kept["mix"][at, tile * LANES : (tile + 1) * LANES] = value.astype(bf16)
            if tile == tiles - 1:
                give(2 * layer, window, nn(kept["mix"][at, :], proj_w[...]))

        staggered(pairs, (score, soften, mix))
        if layer < top:
            load(1, layer + 1).start()
            for name in SAVED[4:6]:
                keep(name).start()
        load(2, layer).wait()
        if layer < top:
            load(3, layer).wait()
        for name in late if layer > 0 else ():
            keep(name).wait()

        def join(window):
            at = rows_of(window, WINDOWS)
            middle = x[at, :] + gather(2 * layer, window, 1) + wide(proj_b, layer)
            x[at, :] = middle
            normed, scale = row_norm(middle)
            kept["n2"][at, :] = normed.astype(bf16)
            kept["r2"][at, :] = scale
            kept["h2"][at, :] = (normed * wide(gain2, layer) + wide(off2, layer)).astype(bf16)

        def expand(window):
            at = rows_of(window, WINDOWS)
            u = nn(kept["h2"][at, :], up_w[...]) + wide(up_b, layer)
            phi = 0.5 + 0.5 * lax.erf(u * 0.7071067811865476)
            kept["slope"][at, :] = (phi + u * jnp.exp(u * u * -0.5) * 0.3989422804014327).astype(bf16)
            kept["hid"][at, :] = (u * phi).astype(bf16)

        def shrink(window):
            give(2 * layer + 1, window, nn(kept["hid"][rows_of(window, WINDOWS), :], down_w[...]))

        if layer == top:
            staggered(every, (join, expand))
            continue
        staggered(every, (join, expand, shrink))
        for slot in (2, 3):
            load(slot, layer + 1).start()
        for name in late:
            keep(name).start()
        write(cot_hbm, low, 1).wait()
        out[...] = low[...].astype(f32) * valid[0].astype(f32)
        move_rows(out, dy, None, True)
        low[...] = dy[...].astype(bf16)
        for window in range(WINDOWS):
            at = rows_of(window, WINDOWS)
            out[at, :] = x[at, :] + gather(2 * layer + 1, window, 1) + wide(down_b, layer)
        move_rows(out, x, False, True)

    for layer in reversed(range(LAYERS)):
        turn = 2 * LAYERS + 2 * (LAYERS - 1 - layer)

        def add_row(row, value, first=0):
            cols = slice(first, first + value.shape[1])
            vectors[0, layer, row : row + 1, cols] += value

        def free(*names):
            for name in names if layer > 0 else ():
                fetch(name).start()

        def free_weight(slot):
            if layer > 0:
                load(slot, layer - 1).start()

        def ready(*names):
            for name in names if layer < top else ():
                fetch(name).wait()

        if layer < top:
            low[...] = dy[...].astype(bf16)
        ready("hid")
        finish_group(layer, 0, low[...], kept["hid"])
        add_row(5, column_sum(dy[...]))
        load(3, layer).wait()
        if layer == top:
            for half in range(HALVES):
                give(turn - 1, half * half_windows, nn(kept["hid"][rows_of(half, HALVES), :], down_w[...]))
        free("hid")
        ready("slope")
        if layer < top:
            load(2, layer).wait()
        for half in range(HALVES):
            at = rows_of(half, HALVES)
            grad = nt(low[at, :], down_w[...]) * kept["slope"][at, :].astype(f32)
            add_row(7, column_sum(grad[:, :width]))
            add_row(8, column_sum(grad[:, width:]))
            kept["slope"][at, :] = grad.astype(bf16)
            if layer == top and half == 0:
                for number in range(HALVES):
                    rows = rows_of(number, HALVES)
                    total = gather(turn - 1, number * half_windows, half_windows)
                    x[rows, :] = x[rows, :] + total + wide(down_b, top)
            give(turn, half * half_windows, nt(kept["slope"][at, :], up_w[...]))
            point()
        free_weight(3)
        free_weight(2)
        ready("h2")
        finish_group(layer, 1, kept["h2"][...], kept["slope"])
        free("h2", "slope")
        ready("n2", "r2", "mix")
        if layer < top:
            load(1, layer).wait()
        for half in range(HALVES):
            at = rows_of(half, HALVES)
            grad = gather(turn, half * half_windows, half_windows)
            normed = kept["n2"][at, :].astype(f32)
            add_row(3, column_sum(grad * normed))
            add_row(4, column_sum(grad))
            total = dy[at, :] + norm_back(grad, normed, kept["r2"][at, :], wide(gain2, layer))
            dy[at, :] = total
            add_row(2, column_sum(total))
            low[at, :] = total.astype(bf16)
            grad_mix[at, :] = nt(low[at, :], proj_w[...]).astype(bf16)
            point()
        free("n2", "r2")
        free_weight(1)
        finish_group(layer, 2, low[...], kept["mix"])
        free("mix")

        ready("prob", "qkv")
        stacks, drops, lows = {}, {}, {}

        def operand(ref, window, tile):
            return ref[rows_of(window, WINDOWS), tile * LANES : (tile + 1) * LANES]

        def pull(window, tile):
            stacks[window, tile] = head_stack(operand(grad_mix, window, tile))
            drops[window, tile] = nt(operand(kept["qkv"].at[2], window, tile), stacks[window, tile])

        def harden(window, tile):
            prob = kept["prob"][window, tile].astype(f32)
            weighted = prob * drops.pop((window, tile))
            value = weighted - prob * column_sum(weighted)
            if window == 0:
                grad_score[tile] = value
            else:
                grad_score[tile] += value
            lows[window, tile] = value.astype(bf16)

        def split(window, tile):
            value = lows.pop((window, tile))
            grad_v = nn(kept["prob"][window, tile], stacks.pop((window, tile)))
            grad_k = nn(value, head_stack(operand(kept["qkv"].at[0], window, tile))) * SCALE
            grad_q = head_pick(tn(value, operand(kept["qkv"].at[1], window, tile))) * SCALE
            for slot, part_grad in enumerate((grad_q, grad_k, grad_v)):
                grad_qkv[slot, rows_of(window, WINDOWS), tile * LANES : (tile + 1) * LANES] = (
                    part_grad.astype(bf16)
                )
            add_row(6, column_sum(grad_q), tile * LANES)
            add_row(6, column_sum(grad_v), heads_width + tile * LANES)
            if tile == tiles - 1:
                point()

        staggered(pairs, (pull, harden, split))
        for head in range(heads):
            lane = head % PER_TILE * CELL
            grad_bias[layer * heads + head] = grad_score[head // PER_TILE, :, lane : lane + CELL]
        free("prob", "qkv")
        ready("h1")

        def finish_qkv():
            for place_index, slot in enumerate((2, 0, 1)):
                finish_chunk(layer, chunks - 3 + place_index, kept["h1"][...], grad_qkv[slot])

        if layer < top:
            finish_qkv()
            load(0, layer).wait()
        for half in range(HALVES):
            at = rows_of(half, HALVES)
            total = nt(grad_qkv[0, at, :], qkv_w[0])
            total = total + nt(grad_qkv[1, at, :], qkv_w[1])
            total = total + nt(grad_qkv[2, at, :], qkv_w[2])
            give(turn + 1, half * half_windows, total)
            point()
        free_weight(0)
        if layer == top:
            finish_qkv()
        free("h1")
        ready("n1", "r1")
        for half in range(HALVES):
            at = rows_of(half, HALVES)
            grad = gather(turn + 1, half * half_windows, half_windows)
            normed = kept["n1"][at, :].astype(f32)
            add_row(0, column_sum(grad * normed))
            add_row(1, column_sum(grad))
            out[at, :] = dy[at, :] + norm_back(grad, normed, kept["r1"][at, :], wide(gain1, layer))
            point()
        free("n1", "r1")
        if layer > 0:
            move_rows(out, dy, True, False)
        point()

    table[...] = jnp.zeros_like(table)
    groups = table.shape[0] // (LAYERS * heads)

    def scatter(step_index, carry):
        at = pl.ds(pl.multiple_of(step_index * UNROLL, 8), UNROLL)
        pair_sums = grad_bias[:, at, :].transpose(1, 0, 2)
        total = None
        for lane in range(UNROLL):
            hot, high = hot_rows(index_t, step_index * UNROLL + lane)
            score = pair_sums[lane]
            high = jnp.broadcast_to(high, score.shape)
            left = jnp.concatenate(
                [jnp.where(high == group, score, 0.0) for group in range(groups)], axis=0
            ).astype(bf16)
            value = nt(left, hot)
            total = value if total is None else total + value
        table[...] += total
        return carry

    steps = CELL // UNROLL
    for quarter in range(2):
        lax.fori_loop(quarter * steps // 2, (quarter + 1) * steps // 2, scatter, 0)
        if quarter == 0:
            move_rows(out, dy, False, None)
            write(dy, input_grad_hbm, 0).start()
        else:
            move_rows(x, out, True, None)
            write(out, output_hbm, 1).start()
        point()
    for layer in range(LAYERS):
        for group in range(groups):
            first = (group * LAYERS + layer) * heads
            vectors[0, layer, REL_ROW : REL_ROW + heads, group * 128 : (group + 1) * 128] = table[
                first : first + heads, :
            ]
    vector_copy(0).start()
    point()
    for layer in range(LAYERS):
        for chunk in range(chunks):
            chunk_result(layer, chunk).wait()
    write(dy, input_grad_hbm, 0).wait()
    write(out, output_hbm, 1).wait()


def run_step(shift, tokens, cot, valid, vectors, tables, weights):
    width = cot.shape[1]
    heads_width = weights[1].shape[1]
    hidden = weights[2].shape[2]
    heads = heads_width // HD
    tiles = heads_width // LANES
    entries = -(-tables[0].shape[2] // 128) * 128
    part = width >> BITS
    widths = chunk_widths(heads_width)
    shapes = saved_shapes(width, heads_width, hidden)
    vmem = pl.BlockSpec(memory_space=pltpu.VMEM)
    hbm = pl.BlockSpec(memory_space=pl.ANY)
    smem = pl.BlockSpec(memory_space=pltpu.SMEM)
    grads = [pltpu.VMEM((2,) * BITS + (part, w), bf16) for w in widths] * LAYERS
    landed = [
        pltpu.VMEM((2,) * (BITS - 1 - phase) + (part, w), bf16) for w in widths for phase in range(BITS)
    ]
    swaps = (2, WINDOWS, CELL, width)
    rounds = (4 * LAYERS, WINDOWS)
    sums = (LAYERS, VECTOR_ROWS, width)
    chunk_rounds = (LAYERS, len(widths), BITS)
    reduced = (LAYERS, part, sum(widths))
    outs = pl.pallas_call(
        functools.partial(step_kernel, shift),
        out_shape=[
            jax.ShapeDtypeStruct((ROWS, width), f32),
            jax.ShapeDtypeStruct((ROWS, width), f32),
            jax.ShapeDtypeStruct(reduced, f32),
            jax.ShapeDtypeStruct(sums, f32),
        ]
        + [jax.ShapeDtypeStruct(*shapes[name]) for name in SAVED],
        in_specs=[hbm, hbm, smem] + [vmem] * 11 + [hbm] * 4,
        out_specs=[hbm, hbm, hbm, vmem] + [hbm] * len(SAVED),
        scratch_shapes=[pltpu.VMEM(w.shape[1:], bf16) for w in weights]
        + [pltpu.VMEM(*shapes[name]) for name in SAVED]
        + grads
        + landed
        + [
            pltpu.VMEM((ROWS, width), f32),
            pltpu.VMEM((ROWS, width), f32),
            pltpu.VMEM((ROWS, width), f32),
            pltpu.VMEM((ROWS, width), bf16),
            pltpu.VMEM(swaps, bf16),
            pltpu.VMEM(swaps, bf16),
            pltpu.VMEM((ROWS, heads_width), bf16),
            pltpu.VMEM((3, ROWS, heads_width), bf16),
            pltpu.VMEM((LAYERS * heads, CELL, CELL), f32),
            pltpu.VMEM((LAYERS * tiles, CELL, PER_TILE * CELL), f32),
            pltpu.VMEM((WINDOWS, CELL, PER_TILE * CELL), bf16),
            pltpu.VMEM((CELL, CELL), jnp.int32),
            pltpu.VMEM((LAYERS * heads, entries), f32),
            pltpu.VMEM((tiles, CELL, PER_TILE * CELL), f32),
            pltpu.VMEM((entries // 128 * LAYERS * heads, 128), f32),
            pltpu.VMEM((BITS,) + sums, f32),
            pltpu.VMEM((BITS,) + sums, f32),
            pltpu.VMEM(reduced, f32),
            pltpu.SemaphoreType.DMA((4,)),
            pltpu.SemaphoreType.DMA((len(SAVED),)),
            pltpu.SemaphoreType.DMA((len(SAVED),)),
            pltpu.SemaphoreType.DMA(rounds),
            pltpu.SemaphoreType.DMA(rounds),
            pltpu.SemaphoreType.DMA(chunk_rounds),
            pltpu.SemaphoreType.DMA(chunk_rounds),
            pltpu.SemaphoreType.REGULAR(chunk_rounds[1:]),
            pltpu.SemaphoreType.DMA((BITS,)),
            pltpu.SemaphoreType.DMA((BITS,)),
            pltpu.SemaphoreType.DMA((2,)),
            pltpu.SemaphoreType.DMA(chunk_rounds[:2]),
        ],
        compiler_params=pltpu.CompilerParams(
            collective_id=0, has_side_effects=True, vmem_limit_bytes=VMEM_LIMIT
        ),
        name="step",
    )(tokens, cot, valid, *vectors, *tables, *weights)
    return outs[:4]


def result_kernel(x, dx, reduced, vectors, *outs):
    (output, input_grad, g1, o1, qkv_g, qv_g, rel_g, proj_g, pb_g, g2, o2, up_g, ub_g, down_g, db_g) = outs
    hidden = up_g.shape[2]
    heads_width = proj_g.shape[2]
    width = g1.shape[1]
    heads, _, entries = rel_g.shape
    output[...] = x[...]
    input_grad[...] = dx[...]
    for layer in range(LAYERS):
        first = 0
        for target, size in (
            (down_g.at[layer], hidden),
            (up_g.at[layer], hidden),
            (proj_g.at[layer], heads_width),
            (qkv_g.at[layer, 2], heads_width),
            (qkv_g.at[layer, 0], heads_width),
            (qkv_g.at[layer, 1], heads_width),
        ):
            target[...] = reduced[layer, :, first : first + size]
            first += size
        row = slice(layer, layer + 1)
        for number, ref in enumerate((g1, o1, pb_g, g2, o2, db_g)):
            ref[row, :] = vectors[layer, number : number + 1, :]
        qv_g[layer, 0:1, :] = vectors[layer, 6:7, :heads_width]
        qv_g[layer, 1:2, :] = vectors[layer, 6:7, heads_width:]
        ub_g[row, :width] = vectors[layer, 7:8, :]
        ub_g[row, width:] = vectors[layer, 8:9, :]
        rel_g[:, layer, :] = vectors[layer, REL_ROW : REL_ROW + heads, :entries]


def per_device(
    tokens,
    region_ids,
    rel_index,
    valid,
    ln1_gain,
    ln1_bias,
    qkv_weight,
    qv_bias,
    rel_table,
    proj_weight,
    proj_bias,
    ln2_gain,
    ln2_bias,
    fc1_weight,
    fc1_bias,
    fc2_weight,
    fc2_bias,
    cotangent,
):
    devices = lax.axis_size("dp")
    group = devices >> BITS
    shift = group.bit_length() - 1
    width = tokens.shape[1]
    heads_width = proj_weight.shape[1]
    hidden = fc1_weight.shape[2]
    tables = (rel_table.transpose(2, 0, 1), rel_index, region_ids)
    weights = (qkv_weight, proj_weight, fc1_weight, fc2_weight)
    vectors = (ln1_gain, ln1_bias, qv_bias, proj_bias, ln2_gain, ln2_bias, fc1_bias, fc2_bias)
    x, dx, reduced, sums = run_step(shift, tokens, cotangent, valid, vectors, tables, weights)
    if group > 1:
        sets = [list(range(first, first + group)) for first in range(0, devices, group)]
        reduced = lax.psum_scatter(
            reduced, "dp", scatter_dimension=1, axis_index_groups=sets, tiled=True
        )
        sums = lax.psum(sums, "dp", axis_index_groups=sets)
    part = width // devices
    shapes = (
        (ROWS, width),
        (ROWS, width),
        (LAYERS, width),
        (LAYERS, width),
        (LAYERS, 3, part, heads_width),
        (LAYERS, 2, heads_width),
        tables[0].shape,
        (LAYERS, part, heads_width),
        (LAYERS, width),
        (LAYERS, width),
        (LAYERS, width),
        (LAYERS, part, hidden),
        (LAYERS, hidden),
        (LAYERS, part, hidden),
        (LAYERS, width),
    )
    vmem = pl.BlockSpec(memory_space=pltpu.VMEM)
    outs = list(
        pl.pallas_call(
            result_kernel,
            out_shape=[jax.ShapeDtypeStruct(shape, f32) for shape in shapes],
            in_specs=[vmem] * 4,
            out_specs=[vmem] * len(shapes),
            compiler_params=pltpu.CompilerParams(vmem_limit_bytes=VMEM_LIMIT),
            name="results",
        )(x, dx, reduced, sums)
    )
    outs[6] = outs[6].transpose(1, 2, 0)
    outs[7] = outs[7].transpose(0, 2, 1)
    outs[13] = outs[13].transpose(0, 2, 1)
    return tuple(outs)


def solution(mesh):
    return jax.shard_map(
        per_device,
        mesh=mesh,
        in_specs=(
            P("dp", None),
            P(),
            P(),
            P("dp"),
            P(),
            P(),
            P(None, None, None, "tensor"),
            P(None, None, "tensor"),
            P(None, None, "tensor"),
            P(None, "tensor", None),
            P(),
            P(),
            P(),
            P(None, None, "tensor"),
            P(None, "tensor"),
            P(None, "tensor", None),
            P(),
            P("dp", None),
        ),
        out_specs=(
            P("dp", None),
            P("dp", None),
            P(),
            P(),
            P(None, None, "dp", "tensor"),
            P(None, None, "tensor"),
            P(None, None, "tensor"),
            P(None, "tensor", "dp"),
            P(),
            P(),
            P(),
            P(None, "dp", "tensor"),
            P(None, "tensor"),
            P(None, "tensor", "dp"),
            P(),
        ),
        check_vma=False,
    )
```
